32 devices in a mesh: fsdp: 4 (over z), ctx: 2 (over x), tp: 4 (over y, core).
Axes of the slice: x: 2, y: 2, z: 4, core: 2. Of those that a mesh axis runs over, the one named last changes fastest.
Arguments:
- tokens: bfloat16 [4, 2048, 1024], P(None, ('fsdp', 'ctx'), 'tp'), may hold values from -6 to 6
- time_embed: bfloat16 [4, 2048, 1024], P(None, ('fsdp', 'ctx'), 'tp'), may hold values from -3 to 3
- cotangent: bfloat16 [4, 2048, 1024], P(None, ('fsdp', 'ctx'), 'tp'), may hold values from -6 to 6
- segment_ids: int32 [4, 2048], P(None, 'fsdp'), may hold values from 0 to 31, as said below
- to_owner: int32 [4, 2048], P(None, ('fsdp', 'ctx')), may hold values from 0 to 2047, as said below
- from_owner: int32 [4, 2048], P(None, ('fsdp', 'ctx')), may hold values from 0 to 2047, as said below
- w_qkv: bfloat16 [2, 3, 1024, 1024], P(None, None, ('fsdp', 'ctx'), 'tp'), may hold values from -0.1875 to 0.1875
- w_out: bfloat16 [2, 1024, 1024], P(None, ('fsdp', 'ctx'), 'tp'), may hold values from -1.5 to 1.5
- w_up: bfloat16 [2, 1024, 4096], P(None, ('fsdp', 'ctx'), 'tp'), may hold values from -0.1875 to 0.1875
- w_down: bfloat16 [2, 1024, 4096], P(None, ('fsdp', 'ctx'), 'tp'), may hold values from -0.125 to 0.125
- biases: float32 [2, 4, 1024], P(None, None, 'tp'), may hold values from -3 to 3
- norm_gain: float32 [2, 2, 1024], P(None, None, 'tp'), may hold values from 0.5 to 1.5
- norm_bias: float32 [2, 2, 1024], P(None, None, 'tp'), may hold values from -3 to 3
- up_bias: float32 [2, 4096], P(None, 'tp'), may hold values from -3 to 3
Outputs:
- outputs: float32 [4, 2048, 1024], P(None, ('fsdp', 'ctx'), 'tp')
- input_grad: float32 [4, 2048, 1024], P(None, ('fsdp', 'ctx'), 'tp')
- w_qkv_grad: float32 [2, 3, 1024, 1024], P(None, None, ('fsdp', 'ctx'), 'tp')
- w_out_grad: float32 [2, 1024, 1024], P(None, ('fsdp', 'ctx'), 'tp')
- w_up_grad: float32 [2, 1024, 4096], P(None, ('fsdp', 'ctx'), 'tp')
- w_down_grad: float32 [2, 1024, 4096], P(None, ('fsdp', 'ctx'), 'tp')
- biases_grad: float32 [2, 4, 1024], P(None, None, 'tp')
- norm_gain_grad: float32 [2, 2, 1024], P(None, None, 'tp')
- norm_bias_grad: float32 [2, 2, 1024], P(None, None, 'tp')
- up_bias_grad: float32 [2, 4096], P(None, 'tp')
The draws below stay inside these ranges and needn't reach their ends.
Inputs may be any that keep to these rules, and one draw needn't show every extreme that they name: `to_owner`: for each micro-batch a permutation of the 2048 positions; every aligned block of 256 given positions sends exactly 32 tokens into every aligned block of 256 balanced positions. `from_owner`: for each micro-batch the inverse of to_owner. `segment_ids`: within the b-th aligned block of 512 tokens the numbers lie in 8 * b to 8 * b + 7, never fall, and the block's last token has 8 * b + 7; a sequence has 64 tokens or more; in every micro-batch some block other than the first is one sequence of 512 tokens, and every other block begins with number 8 * b.
All inputs are finite; a program needn't handle non-finite values.
Results may differ from the reference program's by a relative error of at most 0.025.
Values may be sent and summed in bfloat16 or wider, within the bound.
A program may use at most 256 MiB of HBM per device.

```python
import math
import jax
import jax.numpy as jnp
from jax import lax

D = 1024
H = 16
HD = 64
FF = 4096
LAYERS = 2
MICRO = 4
TOK_DEV = 256
GROUPS = 8
SENDS = 32
PACK = 512
TOKENS = 2048


def draw_segment_ids(key, part):
    packs = TOKENS // PACK
    chosen = jax.random.randint(key, (MICRO, packs, 6), 0, 2)
    chosen = chosen.at[:, :, 0].set(1)
    whole = jax.random.randint(jax.random.fold_in(key, 7), (MICRO,), 1, packs)
    single = jnp.arange(packs)[None, :] == whole[:, None]
    chosen = jnp.where(single[:, :, None], 0, chosen)
    cuts = (2 * jnp.arange(6) + 3) * (PACK // 16)
    position = jnp.arange(PACK)
    later = (cuts[None, None, None, :] > position[None, None, :, None]) & (chosen[:, :, None, :] == 1)
    local_ids = 7 - jnp.sum(later.astype(jnp.int32), axis=3)
    opening = (position[None, None, :] < cuts[0]) & jnp.logical_not(single[:, :, None])
    local_ids = jnp.where(opening, 0, local_ids)
    ids = local_ids + 8 * jnp.arange(packs)[None, :, None]
    return ids.reshape(MICRO, TOKENS).astype(jnp.int32)


def owner_maps(key):
    dest_keys = jax.random.split(jax.random.fold_in(key, 11), MICRO * GROUPS)
    source_keys = jax.random.split(jax.random.fold_in(key, 13), MICRO * GROUPS)
    dest_perm = jax.vmap(lambda one_key: jax.random.permutation(one_key, TOK_DEV))(dest_keys)
    source_perm = jax.vmap(lambda one_key: jax.random.permutation(one_key, TOK_DEV))(source_keys)
    dest_pos = dest_perm.reshape(MICRO, GROUPS, GROUPS, SENDS) + TOK_DEV * jnp.arange(GROUPS)[None, :, None, None]
    source_pos = source_perm.reshape(MICRO, GROUPS, GROUPS, SENDS) + TOK_DEV * jnp.arange(GROUPS)[None, :, None, None]
    dest_pos = jnp.transpose(dest_pos, (0, 2, 1, 3)).reshape(MICRO, TOKENS)
    source_pos = source_pos.reshape(MICRO, TOKENS)
    micro_rows = jnp.arange(MICRO)[:, None]
    to_rows = jnp.zeros((MICRO, TOKENS), jnp.int32).at[micro_rows, source_pos].set(dest_pos.astype(jnp.int32))
    from_rows = jnp.zeros((MICRO, TOKENS), jnp.int32).at[micro_rows, dest_pos].set(source_pos.astype(jnp.int32))
    return (to_rows, from_rows)


def draw_to_owner(key, part):
    return owner_maps(key)[0]


def draw_from_owner(key, part):
    return owner_maps(key)[1]


def levels(own_key, dims, cuts, least, top_value):
    def one(dim, parts):
        steps = jax.random.uniform(jax.random.fold_in(jax.random.fold_in(own_key, 6), dim), (parts,), jnp.float32, least / len(cuts), top_value / len(cuts))
        return jnp.repeat(jnp.exp(steps), dims[dim] // parts).reshape((-1,) + (1,) * (len(dims) - dim - 1))

    factor_of = one(*cuts[0])
    for cut in cuts[1:]:
        factor_of = factor_of * one(*cut)
    return factor_of


def gaussian(stream_key, dims, scale, most, cuts=(), held_as=jnp.bfloat16):
    level = levels(stream_key, dims, cuts, -0.22, 0.18) if cuts else 1.0
    array = jax.random.normal(stream_key, dims, jnp.float32) * scale * level
    return jnp.minimum(jnp.maximum(array, -most), most).astype(held_as)


def setup_inputs(seed: int = 0) -> dict:
    key_list = jax.random.split(jax.random.key(seed), 15)
    tokens = gaussian(key_list[0], (MICRO, TOKENS, D), 1.0, 6.0, ((1, 8), (2, 4)))
    time_embed = gaussian(key_list[1], (MICRO, TOKENS, D), 0.5, 3.0, ((1, 8), (2, 4)))
    cotangent = gaussian(key_list[2], (MICRO, TOKENS, D), 1.0, 6.0, ((1, 8), (2, 4)))
    segment_ids = draw_segment_ids(jax.random.fold_in(key_list[14], 71), 0)
    to_owner = draw_to_owner(jax.random.fold_in(key_list[14], 71), 0)
    from_owner = draw_from_owner(jax.random.fold_in(key_list[14], 71), 0)
    w_qkv = gaussian(key_list[6], (LAYERS, 3, D, D), D ** -0.5, 0.1875, ((2, 8), (3, 4)))
    w_out = gaussian(key_list[7], (LAYERS, D, D), (D // 64) ** -0.5, 1.5, ((1, 8), (2, 4)))
    w_up = gaussian(key_list[8], (LAYERS, D, FF), D ** -0.5, 0.1875, ((1, 8), (2, 4)))
    w_down = gaussian(key_list[9], (LAYERS, D, FF), (FF // 2) ** -0.5, 0.125, ((1, 8), (2, 4)))
    biases = gaussian(key_list[10], (LAYERS, 4, D), 0.5, 3.0, ((2, 4),), jnp.float32)
    norm_gain = jnp.clip(1.0 + 0.1 * jax.random.normal(key_list[11], (LAYERS, 2, D), jnp.float32), 0.5, 1.5)
    norm_bias = gaussian(key_list[12], (LAYERS, 2, D), 0.5, 3.0, ((2, 4),), jnp.float32)
    up_bias = gaussian(key_list[13], (LAYERS, FF), 0.5, 3.0, ((1, 4),), jnp.float32)
    return dict(tokens=tokens, time_embed=time_embed, cotangent=cotangent, segment_ids=segment_ids, to_owner=to_owner, from_owner=from_owner, w_qkv=w_qkv, w_out=w_out, w_up=w_up, w_down=w_down, biases=biases, norm_gain=norm_gain, norm_bias=norm_bias, up_bias=up_bias)


HIGH = lax.Precision.HIGHEST
NEG = -1e+30
EPS = 1e-05

@jax.custom_vjp
def low(v):
    return lax.optimization_barrier(v.astype(jnp.bfloat16)).astype(jnp.float32)

@jax.custom_vjp
def low_back(v):
    return v

def low_keep(v):
    return (low(v), None)

def low_pass(kept, grad):
    return (grad,)

def back_keep(v):
    return (v, None)

def back_low(kept, grad):
    return (low(grad),)
low.defvjp(low_keep, low_pass)
low_back.defvjp(back_keep, back_low)

def both_ways(value):
    return low(low_back(value))

def layer_norm(residual, gain_row, offset):
    row_mean = lax.optimization_barrier(jnp.mean(residual, axis=-1, keepdims=True))
    centred = residual - row_mean
    row_var = lax.optimization_barrier(jnp.mean(centred * centred, axis=-1, keepdims=True))
    return centred * lax.rsqrt(row_var + EPS) * gain_row + offset

def attend(pieces):
    queries, key_rows, value_rows, seq_ids = pieces
    row_count = queries.shape[0]
    query_heads = queries.reshape(row_count, H, HD)
    key_heads = key_rows.reshape(row_count, H, HD)
    value_heads = value_rows.reshape(row_count, H, HD)
    raw_scores = low_back(jnp.einsum('qhd,khd->hqk', query_heads, key_heads, precision=HIGH) * (1.0 / math.sqrt(HD)))
    same_seq = (seq_ids[:, None] == seq_ids[None, :])[None]
    masked = jnp.where(same_seq, raw_scores, NEG)
    row_top = lax.optimization_barrier(jnp.max(masked, axis=2, keepdims=True))
    weighted = jnp.exp(masked - row_top)
    soft_rows = weighted / lax.optimization_barrier(jnp.sum(weighted, axis=2, keepdims=True))
    mixed = jnp.einsum('hqk,khd->qhd', low(soft_rows), value_heads, precision=HIGH)
    return mixed.reshape(row_count, H * HD)

def encoder_layer(residual, seq_ids, params):
    w_qkv, w_out, w_up, w_down, bias_rows, gain_rows, offsets, up_offset = params
    acting = low(residual)
    projected = jnp.einsum('td,cdh->cth', acting, w_qkv, precision=HIGH)
    queries = both_ways(projected[0] + bias_rows[0])
    key_rows = both_ways(projected[1])
    value_rows = both_ways(projected[2] + bias_rows[1])
    packs = residual.shape[0] // PACK

    def in_blocks(values):
        return values.reshape(packs, PACK, D)
    attended = lax.map(jax.checkpoint(attend), (in_blocks(queries), in_blocks(key_rows), in_blocks(value_rows), seq_ids.reshape(packs, PACK)))
    attended = both_ways(attended.reshape(residual.shape[0], D))
    mixed = low_back(jnp.einsum('th,dh->td', attended, w_out, precision=HIGH))
    hidden = layer_norm(residual + mixed + bias_rows[2], gain_rows[0], offsets[0])
    upper = low_back(jnp.dot(low(hidden), w_up, precision=HIGH) + up_offset)
    activated = both_ways(jax.nn.gelu(upper, approximate=False))
    lowered = low_back(jnp.einsum('tf,df->td', activated, w_down, precision=HIGH))
    return layer_norm(hidden + lowered + bias_rows[3], gain_rows[1], offsets[1])

def forward(token_rows, params, time_rows, seq_ids, to_rows, from_rows):
    embedded = low(token_rows + time_rows)
    residual = embedded[from_rows]
    for layer_index in range(LAYERS):
        residual = encoder_layer(residual, seq_ids, tuple((member[layer_index] for member in params)))
    return residual[to_rows]

def reference(tokens, time_embed, cotangent, segment_ids, to_owner, from_owner, w_qkv, w_out, w_up, w_down, biases, norm_gain, norm_bias, up_bias):
    params = tuple((member.astype(jnp.float32) for member in (w_qkv, w_out, w_up, w_down, biases, norm_gain, norm_bias, up_bias)))
    totals = tuple((jnp.zeros_like(member) for member in params))
    result_rows = []
    grad_rows = []
    for micro_index in range(MICRO):
        time_rows = time_embed[micro_index].astype(jnp.float32)
        seq_ids = segment_ids[micro_index]
        to_rows = to_owner[micro_index]
        from_rows = from_owner[micro_index]

        def run(token_rows, weights):
            return forward(token_rows, weights, time_rows, seq_ids, to_rows, from_rows)
        result, pull = jax.vjp(run, tokens[micro_index].astype(jnp.float32), params)
        grad_tokens, grad_params = pull(cotangent[micro_index].astype(jnp.float32))
        totals = tuple((total + part for total, part in zip(totals, grad_params)))
        result_rows.append(result)
        grad_rows.append(grad_tokens)
    return (jnp.stack(result_rows), jnp.stack(grad_rows), totals[0], totals[1], totals[2], totals[3], totals[4], totals[5], totals[6], totals[7])
```

```python
import functools
import math

import jax
import jax.numpy as jnp
from jax import lax
from jax.experimental import pallas as pl
from jax.experimental.pallas import tpu as pltpu
from jax.sharding import PartitionSpec as P

HD = 64
NEG = -1e30
EPS = 1e-05
BF = jnp.bfloat16
F32 = jnp.float32
GRP = ("fsdp", "ctx")


def dot(left, right, dims):
    return lax.dot_general(left, right, (dims, ((), ())), preferred_element_type=F32)


NN = ((1,), (0,))
NT = ((1,), (1,))
TN = ((0,), (0,))


def head_probs(query, key_rows, same_seq):
    scores = jnp.where(same_seq, dot(query, key_rows, NT) * (1.0 / math.sqrt(HD)), NEG)
    top = jnp.max(scores, axis=1, keepdims=True)
    weighted = jnp.exp(scores - top)
    return weighted * (1.0 / jnp.sum(weighted, axis=1, keepdims=True))


def attend_kernel(qkv_ref, seg_col, seg_row, out_ref):
    same_seq = seg_col[0] == seg_row[0]
    for head in range(qkv_ref.shape[3] // HD):
        cols = slice(head * HD, (head + 1) * HD)
        probs = head_probs(qkv_ref[0, 0, :, cols], qkv_ref[1, 0, :, cols], same_seq)
        out_ref[0, :, cols] = dot(probs.astype(BF), qkv_ref[2, 0, :, cols], NN).astype(BF)


def attend_back_kernel(qkv_ref, grad_ref, seg_col, seg_row, out_ref):
    same_seq = seg_col[0] == seg_row[0]
    scale = 1.0 / math.sqrt(HD)
    for head in range(qkv_ref.shape[3] // HD):
        cols = slice(head * HD, (head + 1) * HD)
        query, key_rows, value_rows = (qkv_ref[c, 0, :, cols] for c in range(3))
        grad = grad_ref[0, :, cols]
        probs = head_probs(query, key_rows, same_seq)
        grad_probs = dot(grad, value_rows, NT)
        delta = jnp.sum(probs * grad_probs, axis=1, keepdims=True)
        grad_scores = (probs * (grad_probs - delta)).astype(BF)
        out_ref[0, 0, :, cols] = (dot(grad_scores, key_rows, NN) * scale).astype(BF)
        out_ref[1, 0, :, cols] = (dot(grad_scores, query, TN) * scale).astype(BF)
        out_ref[2, 0, :, cols] = dot(probs.astype(BF), grad, TN).astype(BF)


def attend(qkv, seg_col, seg_row):
    _, packs, rows, width = qkv.shape
    return pl.pallas_call(
        attend_kernel,
        grid=(packs,),
        in_specs=[
            pl.BlockSpec((3, 1, rows, width), lambda k: (0, k, 0, 0)),
            pl.BlockSpec((1, rows, 1), lambda k: (k, 0, 0)),
            pl.BlockSpec((1, 1, rows), lambda k: (k, 0, 0)),
        ],
        out_specs=pl.BlockSpec((1, rows, width), lambda k: (k, 0, 0)),
        out_shape=jax.ShapeDtypeStruct((packs, rows, width), BF),
        compiler_params=pltpu.CompilerParams(vmem_limit_bytes=32 << 20),
    )(qkv, seg_col, seg_row)


def attend_back(qkv, grad, seg_col, seg_row):
    _, packs, rows, width = qkv.shape
    return pl.pallas_call(
        attend_back_kernel,
        grid=(packs,),
        in_specs=[
            pl.BlockSpec((3, 1, rows, width), lambda k: (0, k, 0, 0)),
            pl.BlockSpec((1, rows, width), lambda k: (k, 0, 0)),
            pl.BlockSpec((1, rows, 1), lambda k: (k, 0, 0)),
            pl.BlockSpec((1, 1, rows), lambda k: (k, 0, 0)),
        ],
        out_specs=pl.BlockSpec((3, 1, rows, width), lambda k: (0, k, 0, 0)),
        out_shape=jax.ShapeDtypeStruct((3, packs, rows, width), BF),
        compiler_params=pltpu.CompilerParams(vmem_limit_bytes=32 << 20),
    )(qkv, grad, seg_col, seg_row)


def gather_rows(values):
    return lax.all_gather(values.astype(BF), "tp", axis=1, tiled=True)


def scatter_rows(values):
    return lax.psum_scatter(
        values.astype(BF), "tp", scatter_dimension=1, tiled=True
    ).astype(F32)


def norm_forward(residual, gain, offset):
    mean = jnp.mean(residual, axis=-1, keepdims=True)
    centred = residual - mean
    scale = lax.rsqrt(jnp.mean(centred * centred, axis=-1, keepdims=True) + EPS)
    normed = centred * scale
    return normed * gain + offset, normed, scale


def norm_backward(upstream, normed, scale, gain):
    scaled = upstream * gain
    first = jnp.mean(scaled, axis=-1, keepdims=True)
    second = jnp.mean(scaled * normed, axis=-1, keepdims=True)
    grad = scale * (scaled - first - normed * second)
    return grad, jnp.sum(upstream * normed, axis=(0, 1)), jnp.sum(upstream, axis=(0, 1))


def gelu(values):
    return jax.nn.gelu(values, approximate=False)


def mm(spec, left, right):
    return jnp.einsum(spec, left, right, preferred_element_type=F32)


def layer_forward(resid, act, weights, vectors, seg_col, seg_row):
    w_qkv, w_out, w_up, w_down = weights
    head_bias, full_bias, gain, offset, up_bias = vectors
    proj = mm("ktd,cdh->ckth", act, w_qkv)
    zero = jnp.zeros_like(head_bias[0])
    qkv = (proj + jnp.stack([head_bias[0], zero, head_bias[1]])[:, None, None, :]).astype(BF)
    attended = attend(qkv, seg_col, seg_row)
    mixed = scatter_rows(mm("kth,dh->ktd", attended, w_out))
    hidden, normed1, scale1 = norm_forward(resid + mixed + full_bias[0], gain[0], offset[0])
    hidden_full = gather_rows(hidden)
    upper = mm("ktd,df->ktf", hidden_full, w_up) + up_bias
    gelu_low = gelu(upper).astype(BF)
    lowered = scatter_rows(mm("ktf,df->ktd", gelu_low, w_down))
    out, normed2, scale2 = norm_forward(hidden + lowered + full_bias[1], gain[1], offset[1])
    return out, (act, qkv, attended, normed1, scale1, hidden_full, upper, gelu_low, normed2, scale2)


def layer_backward(upstream, saved, weights, vectors, seg_col, seg_row):
    w_qkv, w_out, w_up, w_down = weights
    head_bias, full_bias, gain, offset, up_bias = vectors
    act, qkv, attended, normed1, scale1, hidden_full, upper, gelu_low, normed2, scale2 = saved
    grad2, gain2, offset2 = norm_backward(upstream, normed2, scale2, gain[1])
    grad_lowered = gather_rows(grad2)
    g_down = mm("ktd,ktf->df", grad_lowered, gelu_low).astype(BF)
    grad_gelu = mm("ktd,df->ktf", grad_lowered, w_down).astype(BF)
    _, pull = jax.vjp(gelu, upper)
    grad_upper = pull(grad_gelu.astype(F32))[0].astype(BF)
    up_grad = jnp.sum(grad_upper, axis=(0, 1), dtype=F32)
    g_up = mm("ktd,ktf->df", hidden_full, grad_upper).astype(BF)
    grad_hidden = scatter_rows(mm("ktf,df->ktd", grad_upper, w_up)) + grad2
    grad1, gain1, offset1 = norm_backward(grad_hidden, normed1, scale1, gain[0])
    grad_mixed = gather_rows(grad1)
    g_out = mm("ktd,kth->dh", grad_mixed, attended).astype(BF)
    grad_attended = mm("ktd,dh->kth", grad_mixed, w_out).astype(BF)
    grad_qkv = attend_back(qkv, grad_attended, seg_col, seg_row)
    g_qkv = mm("ktd,ckth->cdh", act, grad_qkv).astype(BF)
    grad_act = scatter_rows(mm("ckth,cdh->ktd", grad_qkv, w_qkv))
    full_part = jnp.stack(
        [jnp.sum(grad1, axis=(0, 1)), jnp.sum(grad2, axis=(0, 1)), gain1, gain2, offset1, offset2]
    )
    head_part = jnp.sum(grad_qkv, axis=(1, 2), dtype=F32)[0::2]
    return grad_act + grad1, (g_qkv, g_out, g_up, g_down), (full_part, head_part, up_grad)


def local(
    tokens, time_embed, cotangent, segment_ids, to_owner, from_owner,
    w_qkv, w_out, w_up, w_down, biases, norm_gain, norm_bias, up_bias,
):
    micro, rows, width = tokens.shape
    layers = w_qkv.shape[0]
    fs, cx, tp = (lax.axis_size(a) for a in ("fsdp", "ctx", "tp"))
    groups = fs * cx
    mine = micro // cx
    pack = segment_ids.shape[1]
    sends = rows // fs
    my_first = lax.axis_index("ctx") * mine
    tp_index = lax.axis_index("tp")

    weights = []
    for layer in range(layers):
        weights.append(
            (
                lax.all_gather(w_qkv[layer], GRP, axis=1, tiled=True),
                lax.all_gather(w_out[layer], GRP, axis=0, tiled=True),
                lax.all_gather(w_up[layer], GRP, axis=0, tiled=True),
                lax.all_gather(w_down[layer], GRP, axis=0, tiled=True),
            )
        )
    vec = jnp.concatenate([biases[:, 2:], norm_gain, norm_bias], axis=1)
    vec = lax.all_gather(vec, "tp", axis=2, tiled=True)
    vectors = [
        (biases[layer, :2], vec[layer, 0:2], vec[layer, 2:4], vec[layer, 4:6], up_bias[layer])
        for layer in range(layers)
    ]

    to_pack = to_owner // pack
    earlier = jnp.arange(rows)[None, :] < jnp.arange(rows)[:, None]
    rank = jnp.sum((to_pack[:, :, None] == to_pack[:, None, :]) & earlier[None], axis=2)
    out_slot = to_pack * sends + rank
    pick_out = (jnp.arange(rows)[None, :, None] == out_slot[:, None, :]).astype(BF)
    given = lax.all_gather(from_owner, "ctx", axis=1, tiled=True)
    given = lax.dynamic_slice_in_dim(given, my_first, mine)
    source = given // rows
    before = (given[:, None, :] < given[:, :, None]) & (
        given[:, None, :] >= (source * rows)[:, :, None]
    )
    in_slot = source * sends + jnp.sum(before, axis=2)
    pick_in = (jnp.arange(pack)[None, None, :] == in_slot[:, :, None]).astype(BF)

    def to_packs(values):
        slots = mm("msg,mgw->msw", pick_out, values).astype(BF)
        slots = slots.reshape(cx, mine, fs, sends, width).transpose(2, 0, 1, 3, 4)
        slots = slots.reshape(groups, mine, sends, width)
        slots = lax.all_to_all(slots, GRP, split_axis=0, concat_axis=0, tiled=True)
        slots = slots.transpose(1, 0, 2, 3).reshape(mine, pack, width)
        return mm("kps,ksw->kpw", pick_in, slots).astype(BF)

    def from_packs(values):
        values = lax.all_to_all(values.astype(BF), "tp", split_axis=2, concat_axis=1, tiled=True)
        slots = mm("kps,kpw->ksw", pick_in, values).astype(BF)
        slots = slots.reshape(mine, groups, sends, width).transpose(1, 0, 2, 3)
        slots = lax.all_to_all(slots, GRP, split_axis=0, concat_axis=0, tiled=True)
        slots = slots.reshape(fs, cx, mine, sends, width).transpose(1, 2, 0, 3, 4)
        return mm("msg,msw->mgw", pick_out, slots.reshape(micro, rows, width))

    embedded = (tokens.astype(F32) + time_embed.astype(F32)).astype(BF)
    act = lax.all_gather(to_packs(embedded), "tp", axis=2, tiled=True)
    resid = lax.dynamic_slice_in_dim(act, tp_index * (pack // tp), pack // tp, 1).astype(F32)
    upstream = lax.all_to_all(
        to_packs(cotangent), "tp", split_axis=1, concat_axis=2, tiled=True
    ).astype(F32)
    seg = lax.dynamic_slice_in_dim(segment_ids, my_first, mine)
    seg_col, seg_row = seg[:, :, None], seg[:, None, :]

    saved = []
    for layer in range(layers):
        if layer:
            act = gather_rows(resid)
        resid, kept = layer_forward(resid, act, weights[layer], vectors[layer], seg_col, seg_row)
        saved.append(kept)
    outputs = from_packs(resid)
    shards = [None] * layers
    parts = [None] * layers
    for layer in reversed(range(layers)):
        upstream, grads, parts[layer] = layer_backward(
            upstream, saved[layer], weights[layer], vectors[layer], seg_col, seg_row
        )
        shards[layer] = (
            lax.psum_scatter(grads[0], GRP, scatter_dimension=1, tiled=True),
            lax.psum_scatter(grads[1], GRP, scatter_dimension=0, tiled=True),
            lax.psum_scatter(grads[2], GRP, scatter_dimension=0, tiled=True),
            lax.psum_scatter(grads[3], GRP, scatter_dimension=0, tiled=True),
        )
    input_grad = from_packs(upstream)
    full_part, head_part, up_part = (jnp.stack([p[i] for p in parts]) for i in range(3))
    full_part = lax.psum_scatter(full_part, "tp", scatter_dimension=2, tiled=True)
    full_part, head_part, up_part = lax.psum((full_part, head_part, up_part), GRP)
    return (
        outputs,
        input_grad,
        *(jnp.stack([s[i] for s in shards]).astype(F32) for i in range(4)),
        jnp.concatenate([head_part, full_part[:, 0:2]], axis=1),
        full_part[:, 2:4],
        full_part[:, 4:6],
        up_part,
    )


def solution(mesh):
    wide = P(None, GRP, "tp")
    vec = P(None, None, "tp")
    qkv = P(None, None, GRP, "tp")
    owner = P(None, GRP)
    return jax.shard_map(
        local,
        mesh=mesh,
        in_specs=(
            wide, wide, wide, P(None, "fsdp"), owner, owner, qkv, wide, wide, wide,
            vec, vec, vec, P(None, "tp"),
        ),
        out_specs=(wide, wide, qkv, wide, wide, wide, vec, vec, vec, P(None, "tp")),
        check_vma=False,
    )
```

```python
import functools
import math

import jax
import jax.numpy as jnp
from jax import lax
from jax.experimental import pallas as pl
from jax.experimental.pallas import tpu as pltpu
from jax.sharding import PartitionSpec as P

HD = 64
NEG = -1e30
EPS = 1e-05
BF = jnp.bfloat16
F32 = jnp.float32
GRP = ("fsdp", "ctx")


def dot(left, right, dims):
    return lax.dot_general(left, right, (dims, ((), ())), preferred_element_type=F32)


NN = ((1,), (0,))
NT = ((1,), (1,))
TN = ((0,), (0,))


def head_probs(query, key_rows, same_seq):
    scores = jnp.where(same_seq, dot(query, key_rows, NT) * (1.0 / math.sqrt(HD)), NEG)
    top = jnp.max(scores, axis=1, keepdims=True)
    weighted = jnp.exp(scores - top)
    return weighted * (1.0 / jnp.sum(weighted, axis=1, keepdims=True))


def attend_kernel(qkv_ref, seg_col, seg_row, out_ref):
    same_seq = seg_col[0] == seg_row[0]
    for head in range(qkv_ref.shape[3] // HD):
        cols = slice(head * HD, (head + 1) * HD)
        probs = head_probs(qkv_ref[0, 0, :, cols], qkv_ref[1, 0, :, cols], same_seq)
        out_ref[0, :, cols] = dot(probs.astype(BF), qkv_ref[2, 0, :, cols], NN).astype(BF)


def attend_back_kernel(qkv_ref, grad_ref, seg_col, seg_row, out_ref):
    same_seq = seg_col[0] == seg_row[0]
    scale = 1.0 / math.sqrt(HD)
    for head in range(qkv_ref.shape[3] // HD):
        cols = slice(head * HD, (head + 1) * HD)
        query, key_rows, value_rows = (qkv_ref[c, 0, :, cols] for c in range(3))
        grad = grad_ref[0, :, cols]
        probs = head_probs(query, key_rows, same_seq)
        grad_probs = dot(grad, value_rows, NT)
        delta = jnp.sum(probs * grad_probs, axis=1, keepdims=True)
        grad_scores = (probs * (grad_probs - delta)).astype(BF)
        out_ref[0, 0, :, cols] = (dot(grad_scores, key_rows, NN) * scale).astype(BF)
        out_ref[1, 0, :, cols] = (dot(grad_scores, query, TN) * scale).astype(BF)
        out_ref[2, 0, :, cols] = dot(probs.astype(BF), grad, TN).astype(BF)


def attend(qkv, seg_col, seg_row):
    _, packs, rows, width = qkv.shape
    return pl.pallas_call(
        attend_kernel,
        grid=(packs,),
        in_specs=[
            pl.BlockSpec((3, 1, rows, width), lambda k: (0, k, 0, 0)),
            pl.BlockSpec((1, rows, 1), lambda k: (k, 0, 0)),
            pl.BlockSpec((1, 1, rows), lambda k: (k, 0, 0)),
        ],
        out_specs=pl.BlockSpec((1, rows, width), lambda k: (k, 0, 0)),
        out_shape=jax.ShapeDtypeStruct((packs, rows, width), BF),
        compiler_params=pltpu.CompilerParams(vmem_limit_bytes=32 << 20),
    )(qkv, seg_col, seg_row)


def attend_back(qkv, grad, seg_col, seg_row):
    _, packs, rows, width = qkv.shape
    return pl.pallas_call(
        attend_back_kernel,
        grid=(packs,),
        in_specs=[
            pl.BlockSpec((3, 1, rows, width), lambda k: (0, k, 0, 0)),
            pl.BlockSpec((1, rows, width), lambda k: (k, 0, 0)),
            pl.BlockSpec((1, rows, 1), lambda k: (k, 0, 0)),
            pl.BlockSpec((1, 1, rows), lambda k: (k, 0, 0)),
        ],
        out_specs=pl.BlockSpec((3, 1, rows, width), lambda k: (0, k, 0, 0)),
        out_shape=jax.ShapeDtypeStruct((3, packs, rows, width), BF),
        compiler_params=pltpu.CompilerParams(vmem_limit_bytes=32 << 20),
    )(qkv, grad, seg_col, seg_row)


MESH = pl.DeviceIdType.MESH
LOG2E = 1.4426950408889634


def gelu_pair(values):
    bell = jnp.exp2(values * values * (-0.5 * LOG2E))
    t = 1.0 / (1.0 + (0.3275911 * math.sqrt(0.5)) * jnp.abs(values))
    poly = t * (
        0.127414796 + t * (-0.142248368 + t * (0.7107068705 + t * (-0.7265760135 + t * 0.5307027145)))
    )
    tail = poly * bell
    phi = jnp.where(values < 0, tail, 1.0 - tail)
    return values * phi, phi + values * bell * (1.0 / math.sqrt(2.0 * math.pi))


class Links:
    def __init__(self):
        self.fs, self.cx = lax.axis_size("fsdp"), lax.axis_size("ctx")
        self.f, self.c, self.t = (lax.axis_index(a) for a in ("fsdp", "ctx", "tp"))
        self.core, self.chip = lax.rem(self.t, 2), self.t // 2
        self.sib_t = self.t + 1 - 2 * self.core
        self.peer_t = lax.rem(self.t + 2, 4)
        self.sib = (self.f, self.c, self.sib_t)
        self.peer = (self.f, self.c, self.peer_t)
        self.across = (self.f, 1 - self.c, self.t)

    def away(self, step):
        return (lax.rem(self.f + step, self.fs), self.c, self.t)

    def barrier(self):
        sem = pltpu.get_barrier_semaphore()
        for target in (self.sib, self.peer, self.across):
            pl.semaphore_signal(sem, inc=1, device_id=target, device_id_type=MESH)

        def greet(step, carry):
            pl.semaphore_signal(sem, inc=1, device_id=self.away(step), device_id_type=MESH)
            return carry

        lax.fori_loop(1, self.fs, greet, 0)
        pl.semaphore_wait(sem, 2 + self.fs)


def remote(src, dst, send, recv, target):
    return pltpu.make_async_remote_copy(
        src_ref=src, dst_ref=dst, send_sem=send, recv_sem=recv,
        device_id=target, device_id_type=MESH,
    )


class RowSum:
    def __init__(self, lk, part, from_sib, to_peer, from_peer, send, recv):
        self.lk, self.part, self.from_sib = lk, part, from_sib
        self.to_peer, self.from_peer, self.send, self.recv = to_peer, from_peer, send, recv

    def sib_copy(self, k):
        return remote(
            self.part.at[k, 1 - self.lk.core], self.from_sib.at[k],
            self.send.at[k, 0], self.recv.at[k, 0], self.lk.sib,
        )

    def peer_copy(self, k):
        return remote(
            self.to_peer.at[k], self.from_peer.at[k],
            self.send.at[k, 1], self.recv.at[k, 1], self.lk.peer,
        )

    def first(self, k):
        self.sib_copy(k).start()

    def second(self, k):
        self.sib_copy(k).wait_recv()
        other = 1 - self.lk.chip
        total = self.part[k, self.lk.core, other].astype(F32) + self.from_sib[k, other].astype(F32)
        self.to_peer[k] = total.astype(BF)
        self.peer_copy(k).start()

    def last(self, k):
        own = self.part[k, self.lk.core, self.lk.chip].astype(F32)
        own = own + self.from_sib[k, self.lk.chip].astype(F32)
        self.peer_copy(k).wait_recv()
        self.sib_copy(k).wait_send()
        self.peer_copy(k).wait_send()
        return own + self.from_peer[k].astype(F32)


class RowGather:
    def __init__(self, lk, rows, send, recv):
        self.lk, self.rows, self.send, self.recv = lk, rows, send, recv

    def block(self, ref, index):
        return ref.at[pl.ds(pl.multiple_of(index * self.rows, self.rows), self.rows)]

    def copy(self, ref, k, which):
        index = self.lk.t if which < 2 else self.lk.peer_t
        part = self.block(ref, index)
        target = self.lk.peer if which == 0 else self.lk.sib
        return remote(part, part, self.send.at[k, which], self.recv.at[k, which], target)

    def first(self, ref, k):
        self.copy(ref, k, 0).start()
        self.copy(ref, k, 1).start()

    def second(self, ref, k):
        self.copy(ref, k, 0).wait_recv()
        self.copy(ref, k, 2).start()

    def last(self, ref, k):
        self.copy(ref, k, 1).wait_recv()
        self.copy(ref, k, 2).wait_recv()
        for which in range(3):
            self.copy(ref, k, which).wait_send()


class WeightGather:
    def __init__(self, lk, shard, full, z_send, z_recv, x_send, x_recv, own):
        self.lk, self.shard, self.full = lk, shard, full
        self.z_send, self.z_recv, self.x_send, self.x_recv = z_send, z_recv, x_send, x_recv
        self.own = own
        self.rows = shard.shape[1]

    def block(self, chunk, f, c):
        first = pl.multiple_of((f * self.lk.cx + c) * self.rows, self.rows)
        return self.full.at[chunk, pl.ds(first, self.rows)]

    def z_copy(self, chunk, step):
        return remote(
            self.shard.at[chunk], self.block(chunk, self.lk.f, self.lk.c),
            self.z_send.at[chunk, step], self.z_recv.at[chunk, self.lk.fs - step],
            self.lk.away(step),
        )

    def x_copy(self, chunk, step):
        f = lax.rem(self.lk.f + step, self.lk.fs)
        part = self.block(chunk, f, self.lk.c)
        return remote(
            part, part, self.x_send.at[chunk, step], self.x_recv.at[chunk, step], self.lk.across
        )

    def x_own(self, chunk):
        return remote(
            self.shard.at[chunk], self.block(chunk, self.lk.f, self.lk.c),
            self.x_send.at[chunk, 0], self.x_recv.at[chunk, 0], self.lk.across,
        )

    def own_copy(self, chunk):
        return pltpu.make_async_copy(
            self.shard.at[chunk], self.block(chunk, self.lk.f, self.lk.c), self.own.at[chunk]
        )

    def each(self, first, work):
        def body(step, carry):
            work(step)
            return carry

        lax.fori_loop(first, self.lk.fs, body, 0)

    def start(self, chunk):
        self.own_copy(chunk).start()
        self.x_own(chunk).start()
        self.each(1, lambda step: self.z_copy(chunk, step).start())

    def forward(self, chunk):
        def work(step):
            self.z_copy(chunk, self.lk.fs - step).wait_recv()
            self.x_copy(chunk, step).start()

        self.each(1, work)

    def finish(self, chunk):
        self.own_copy(chunk).wait()
        self.each(0, lambda step: self.x_copy(chunk, step).wait_recv())

    def drain(self, chunk):
        self.each(1, lambda step: self.z_copy(chunk, step).wait_send())
        self.each(0, lambda step: self.x_copy(chunk, step).wait_send())


def store_part(part, k, cols, values, rows):
    for block in range(4):
        part[k, block % 2, block // 2, :, cols] = values[block * rows : (block + 1) * rows].astype(
            BF
        )


def masked_scores(query, key_rows, same_seq):
    return jnp.where(
        same_seq, dot(query, key_rows, NT) * (LOG2E / math.sqrt(HD)), NEG
    )


def forward_kernel(
    act_in, shard, vec, head_bias, up_bias, seg_col, seg_row,
    out_w, out_act, out_qkv, out_att, out_nrm, out_std, out_hid, out_glu, out_dglu, out_lse,
    out_u,
    w, act, qkv, att, nrm, std, hid, glu, dglu, lse, u, h, part, from_sib, to_peer, from_peer,
    in_sem, out_sem, rs_send, rs_recv, ag_send, ag_recv, z_send, z_recv, x_send, x_recv, own,
):
    layers, packs, rows, width = act.shape
    mine = rows // 4
    heads_width = att.shape[3]
    chunks = shard.shape[0]
    lk = Links()
    lk.barrier()
    rs = RowSum(lk, part, from_sib, to_peer, from_peer, rs_send, rs_recv)
    ag = RowGather(lk, mine, ag_send, ag_recv)
    wg = WeightGather(lk, shard, w, z_send, z_recv, x_send, x_recv, own)
    pending = []

    def save(src, dst):
        copy = pltpu.make_async_copy(src, dst, out_sem.at[len(pending)])
        copy.start()
        pending.append(copy)

    load = pltpu.make_async_copy(act_in, act.at[0], in_sem)
    load.start()
    wg.start(0)
    load.wait()
    my_rows = pl.ds(pl.multiple_of(lk.t * mine, mine), mine)
    for k in range(packs):
        u[k] = act[0, k, my_rows].astype(F32)
    lse[...] = jnp.zeros_like(lse)
    wg.forward(0)
    wg.start(1)
    wg.finish(0)
    save(w.at[0], out_w.at[0])

    def project(layer, k):
        for j in range(3):
            cols = slice(j * heads_width, (j + 1) * heads_width)
            acc = dot(act[layer, k], w[3 * layer, :, cols], NN)
            if j != 1:
                acc = acc + head_bias[layer, j // 2 : j // 2 + 1]
            qkv[layer, k, :, cols] = acc.astype(BF)
        save(qkv.at[layer, k], out_qkv.at[layer, k])

    def attention(layer, k):
        same_seq = seg_col[k] == seg_row[k]
        for head in range(heads_width // HD):
            cols = [slice(j * heads_width + head * HD, j * heads_width + (head + 1) * HD) for j in range(3)]
            scores = masked_scores(qkv[layer, k, :, cols[0]], qkv[layer, k, :, cols[1]], same_seq)
            top = jnp.max(scores, axis=1, keepdims=True)
            weighted = jnp.exp2(scores - top)
            total = jnp.sum(weighted, axis=1, keepdims=True)
            lse[layer, k, :, head : head + 1] = top + jnp.log2(total)
            probs = (weighted * (1.0 / total)).astype(BF)
            att[layer, k, :, cols[0]] = dot(probs, qkv[layer, k, :, cols[2]], NN).astype(BF)
        save(lse.at[layer, k], out_lse.at[layer, k])
        save(att.at[layer, k], out_att.at[layer, k])
        for j in range(width // 256):
            cols = slice(j * 256, (j + 1) * 256)
            acc = dot(att[layer, k], w[3 * layer, cols, 3 * heads_width :], NT)
            store_part(part, k, cols, acc, mine)
        rs.first(k)

    def normalize(layer, which, k, resid):
        mean = jnp.mean(resid, axis=1, keepdims=True)
        centred = resid - mean
        scale = lax.rsqrt(jnp.mean(centred * centred, axis=1, keepdims=True) + EPS)
        normed = centred * scale
        nrm[layer, which, k] = normed
        std[layer, which, k] = jnp.broadcast_to(scale, std.shape[3:])
        save(nrm.at[layer, which, k], out_nrm.at[layer, which, k])
        save(std.at[layer, which, k], out_std.at[layer, which, k])
        return normed * vec[layer, 2 + which : 3 + which] + vec[layer, 4 + which : 5 + which]

    def norm_one(layer, k):
        hidden = normalize(layer, 0, k, u[k] + rs.last(k) + vec[layer, 0:1])
        h[k] = hidden
        hid[layer, k, my_rows] = hidden.astype(BF)
        ag.first(hid.at[layer, k], k)

    def expand(layer, k):
        def tile(j, carry):
            cols = pl.ds(pl.multiple_of(j * 256, 256), 256)
            acc = dot(hid[layer, k], w[3 * layer + 1, :, cols], NN) + up_bias[layer, :, cols]
            value, slope = gelu_pair(acc)
            glu[layer, k, :, cols] = value.astype(BF)
            dglu[layer, k, :, cols] = slope.astype(BF)
            return carry

        lax.fori_loop(0, width // 256, tile, 0)
        save(glu.at[layer, k], out_glu.at[layer, k])
        save(dglu.at[layer, k], out_dglu.at[layer, k])

    def contract(layer, k):
        def tile(j, carry):
            cols = pl.ds(pl.multiple_of(j * 256, 256), 256)
            acc = dot(glu[layer, k], w[3 * layer + 2, cols, :], NT)
            store_part(part, k, cols, acc, mine)
            return carry

        lax.fori_loop(0, width // 256, tile, 0)
        rs.first(k)

    def norm_two(layer, k):
        out = normalize(layer, 1, k, h[k] + rs.last(k) + vec[layer, 1:2])
        u[k] = out
        if layer + 1 < layers:
            act[layer + 1, k, my_rows] = out.astype(BF)
            ag.first(act.at[layer + 1, k], k)
        else:
            save(u.at[k], out_u.at[k])

    def weights_next(chunk):
        if chunk < chunks:
            if chunk + 1 < chunks:
                wg.start(chunk + 1)
            wg.forward(chunk)

    def weights_ready(chunk):
        wg.finish(chunk)
        save(w.at[chunk], out_w.at[chunk])

    for layer in range(layers):
        base = 3 * layer
        more = layer + 1 < layers
        if layer:
            weights_ready(base)
            ag.last(act.at[layer, 0], 0)
            save(act.at[layer, 0], out_act.at[layer - 1, 0])
        project(layer, 0)
        if layer:
            ag.second(act.at[layer, 1], 1)
        attention(layer, 0)
        weights_next(base + 1)
        if layer:
            ag.last(act.at[layer, 1], 1)
            save(act.at[layer, 1], out_act.at[layer - 1, 1])
        project(layer, 1)
        rs.second(0)
        attention(layer, 1)
        norm_one(layer, 0)
        rs.second(1)
        ag.second(hid.at[layer, 0], 0)
        norm_one(layer, 1)
        weights_ready(base + 1)
        weights_next(base + 2)
        ag.last(hid.at[layer, 0], 0)
        save(hid.at[layer, 0], out_hid.at[layer, 0])
        expand(layer, 0)
        ag.second(hid.at[layer, 1], 1)
        weights_ready(base + 2)
        contract(layer, 0)
        weights_next(base + 3)
        ag.last(hid.at[layer, 1], 1)
        save(hid.at[layer, 1], out_hid.at[layer, 1])
        expand(layer, 1)
        rs.second(0)
        contract(layer, 1)
        norm_two(layer, 0)
        rs.second(1)
        if more:
            ag.second(act.at[layer + 1, 0], 0)
        norm_two(layer, 1)
    for chunk in range(chunks):
        wg.drain(chunk)
    for copy in pending:
        copy.wait()


def forward(act, shard, vec, head_bias, up_bias, seg_col, seg_row):
    packs, rows, width = act.shape
    chunks = shard.shape[0]
    layers = chunks // 3
    mine = rows // 4
    heads = head_bias.shape[2]
    fs = lax.axis_size("fsdp")
    shapes = dict(
        w=((chunks, width, width), BF),
        act=((layers, packs, rows, width), BF),
        qkv=((layers, packs, rows, 3 * heads), BF),
        att=((layers, packs, rows, heads), BF),
        nrm=((layers, 2, packs, mine, width), F32),
        std=((layers, 2, packs, mine, 128), F32),
        hid=((layers, packs, rows, width), BF),
        glu=((layers, packs, rows, width), BF),
        dglu=((layers, packs, rows, width), BF),
        lse=((layers, packs, rows, 128), F32),
        u=((packs, mine, width), F32),
    )
    outs = {name: jax.ShapeDtypeStruct(*shape) for name, shape in shapes.items()}
    outs["act"] = jax.ShapeDtypeStruct((layers - 1, packs, rows, width), BF)
    copies = chunks + (layers - 1) * packs + layers * packs * 10 + packs
    dma = pltpu.SemaphoreType.DMA
    whole = pl.BlockSpec(memory_space=pl.ANY)
    vmem = pl.BlockSpec(memory_space=pltpu.VMEM)
    return pl.pallas_call(
        forward_kernel,
        in_specs=[whole, whole, vmem, vmem, vmem, vmem, vmem],
        out_specs=[whole] * len(outs),
        out_shape=list(outs.values()),
        scratch_shapes=[pltpu.VMEM(*shape) for shape in shapes.values()]
        + [
            pltpu.VMEM((packs, mine, width), F32),
            pltpu.VMEM((packs, 2, 2, mine, width), BF),
            pltpu.VMEM((packs, 2, mine, width), BF),
            pltpu.VMEM((packs, mine, width), BF),
            pltpu.VMEM((packs, mine, width), BF),
            dma(()), dma((copies,)),
            dma((packs, 2)), dma((packs, 2)), dma((packs, 3)), dma((packs, 3)),
            dma((chunks, fs)), dma((chunks, fs)), dma((chunks, fs)), dma((chunks, fs)),
            dma((chunks,)),
        ],
        compiler_params=pltpu.CompilerParams(
            collective_id=0, has_side_effects=True, vmem_limit_bytes=60 << 20
        ),
        name="forward",
    )(act, shard, vec, head_bias, up_bias, seg_col, seg_row)


def gather_rows(values):
    return lax.all_gather(values.astype(BF), "tp", axis=1, tiled=True)


def scatter_rows(values):
    return lax.psum_scatter(
        values.astype(BF), "tp", scatter_dimension=1, tiled=True
    ).astype(F32)


def norm_forward(residual, gain, offset):
    mean = jnp.mean(residual, axis=-1, keepdims=True)
    centred = residual - mean
    scale = lax.rsqrt(jnp.mean(centred * centred, axis=-1, keepdims=True) + EPS)
    normed = centred * scale
    return normed * gain + offset, normed, scale


def norm_backward(upstream, normed, scale, gain):
    scaled = upstream * gain
    first = jnp.mean(scaled, axis=-1, keepdims=True)
    second = jnp.mean(scaled * normed, axis=-1, keepdims=True)
    grad = scale * (scaled - first - normed * second)
    return grad, jnp.sum(upstream * normed, axis=(0, 1)), jnp.sum(upstream, axis=(0, 1))


def gelu(values):
    return jax.nn.gelu(values, approximate=False)


def mm(spec, left, right):
    return jnp.einsum(spec, left, right, preferred_element_type=F32)


def layer_backward(upstream, saved, weights, vectors, seg_col, seg_row):
    w_qkv, w_out, w_up, w_down = weights
    head_bias, full_bias, gain, offset, up_bias = vectors
    act, qkv, attended, normed1, scale1, hidden_full, upper, gelu_low, normed2, scale2 = saved
    grad2, gain2, offset2 = norm_backward(upstream, normed2, scale2, gain[1])
    grad_lowered = gather_rows(grad2)
    g_down = mm("ktd,ktf->df", grad_lowered, gelu_low).astype(BF)
    grad_gelu = mm("ktd,df->ktf", grad_lowered, w_down).astype(BF)
    grad_upper = (grad_gelu.astype(F32) * upper.astype(F32)).astype(BF)
    up_grad = jnp.sum(grad_upper, axis=(0, 1), dtype=F32)
    g_up = mm("ktd,ktf->df", hidden_full, grad_upper).astype(BF)
    grad_hidden = scatter_rows(mm("ktf,df->ktd", grad_upper, w_up)) + grad2
    grad1, gain1, offset1 = norm_backward(grad_hidden, normed1, scale1, gain[0])
    grad_mixed = gather_rows(grad1)
    g_out = mm("ktd,kth->dh", grad_mixed, attended).astype(BF)
    grad_attended = mm("ktd,dh->kth", grad_mixed, w_out).astype(BF)
    grad_qkv = attend_back(qkv, grad_attended, seg_col, seg_row)
    g_qkv = mm("ktd,ckth->cdh", act, grad_qkv).astype(BF)
    grad_act = scatter_rows(mm("ckth,cdh->ktd", grad_qkv, w_qkv))
    full_part = jnp.stack(
        [jnp.sum(grad1, axis=(0, 1)), jnp.sum(grad2, axis=(0, 1)), gain1, gain2, offset1, offset2]
    )
    head_part = jnp.sum(grad_qkv, axis=(1, 2), dtype=F32)[0::2]
    return grad_act + grad1, (g_qkv, g_out, g_up, g_down), (full_part, head_part, up_grad)


def local(
    tokens, time_embed, cotangent, segment_ids, to_owner, from_owner,
    w_qkv, w_out, w_up, w_down, biases, norm_gain, norm_bias, up_bias,
):
    micro, rows, width = tokens.shape
    layers = w_qkv.shape[0]
    fs, cx, tp = (lax.axis_size(a) for a in ("fsdp", "ctx", "tp"))
    groups = fs * cx
    mine = micro // cx
    pack = segment_ids.shape[1]
    sends = rows // fs
    my_first = lax.axis_index("ctx") * mine
    tp_index = lax.axis_index("tp")

    shard = jnp.concatenate(
        [w_qkv[:, 0], w_qkv[:, 1], w_qkv[:, 2], w_out, w_up, w_down], axis=2
    )
    shard = shard.reshape(layers, shard.shape[1], 3, -1).transpose(0, 2, 1, 3)
    shard = shard.reshape(layers * 3, shard.shape[2], -1)
    vec = jnp.concatenate([biases[:, 2:], norm_gain, norm_bias], axis=1)
    vec = lax.all_gather(vec, "tp", axis=2, tiled=True)
    vectors = [
        (biases[layer, :2], vec[layer, 0:2], vec[layer, 2:4], vec[layer, 4:6], up_bias[layer])
        for layer in range(layers)
    ]

    to_pack = to_owner // pack
    earlier = jnp.arange(rows)[None, :] < jnp.arange(rows)[:, None]
    rank = jnp.sum((to_pack[:, :, None] == to_pack[:, None, :]) & earlier[None], axis=2)
    out_slot = to_pack * sends + rank
    pick_out = (jnp.arange(rows)[None, :, None] == out_slot[:, None, :]).astype(BF)
    given = lax.all_gather(from_owner, "ctx", axis=1, tiled=True)
    given = lax.dynamic_slice_in_dim(given, my_first, mine)
    source = given // rows
    before = (given[:, None, :] < given[:, :, None]) & (
        given[:, None, :] >= (source * rows)[:, :, None]
    )
    in_slot = source * sends + jnp.sum(before, axis=2)
    pick_in = (jnp.arange(pack)[None, None, :] == in_slot[:, :, None]).astype(BF)

    def to_packs(values):
        slots = mm("msg,mgw->msw", pick_out, values).astype(BF)
        slots = slots.reshape(cx, mine, fs, sends, width).transpose(2, 0, 1, 3, 4)
        slots = slots.reshape(groups, mine, sends, width)
        slots = lax.all_to_all(slots, GRP, split_axis=0, concat_axis=0, tiled=True)
        slots = slots.transpose(1, 0, 2, 3).reshape(mine, pack, width)
        return mm("kps,ksw->kpw", pick_in, slots).astype(BF)

    def from_packs(values):
        values = lax.all_to_all(values.astype(BF), "tp", split_axis=2, concat_axis=1, tiled=True)
        slots = mm("kps,kpw->ksw", pick_in, values).astype(BF)
        slots = slots.reshape(mine, groups, sends, width).transpose(1, 0, 2, 3)
        slots = lax.all_to_all(slots, GRP, split_axis=0, concat_axis=0, tiled=True)
        slots = slots.reshape(fs, cx, mine, sends, width).transpose(1, 2, 0, 3, 4)
        return mm("msg,msw->mgw", pick_out, slots.reshape(micro, rows, width))

    embedded = (tokens.astype(F32) + time_embed.astype(F32)).astype(BF)
    act = lax.all_gather(to_packs(embedded), "tp", axis=2, tiled=True)
    upstream = lax.all_to_all(
        to_packs(cotangent), "tp", split_axis=1, concat_axis=2, tiled=True
    ).astype(F32)
    seg = lax.dynamic_slice_in_dim(segment_ids, my_first, mine)
    seg_col, seg_row = seg[:, :, None], seg[:, None, :]

    full_w, o_act, o_qkv, o_att, o_nrm, o_std, o_hid, o_glu, o_dglu, o_lse, resid = forward(
        act, shard, vec, biases[:, :2], up_bias[:, None], seg_col, seg_row
    )
    weights = []
    saved = []
    hw = o_att.shape[3]
    for layer in range(layers):
        first = full_w[3 * layer]
        weights.append(
            (
                jnp.stack([first[:, c * hw : (c + 1) * hw] for c in range(3)]),
                first[:, 3 * hw :], full_w[3 * layer + 1], full_w[3 * layer + 2],
            )
        )
        saved.append(
            (
                act if layer == 0 else o_act[layer - 1],
                jnp.stack([o_qkv[layer, :, :, c * hw : (c + 1) * hw] for c in range(3)]),
                o_att[layer], o_nrm[layer, 0], o_std[layer, 0, :, :, :1], o_hid[layer],
                o_dglu[layer], o_glu[layer], o_nrm[layer, 1], o_std[layer, 1, :, :, :1],
            )
        )
    outputs = from_packs(resid)
    shards = [None] * layers
    parts = [None] * layers
    for layer in reversed(range(layers)):
        upstream, grads, parts[layer] = layer_backward(
            upstream, saved[layer], weights[layer], vectors[layer], seg_col, seg_row
        )
        shards[layer] = (
            lax.psum_scatter(grads[0], GRP, scatter_dimension=1, tiled=True),
            lax.psum_scatter(grads[1], GRP, scatter_dimension=0, tiled=True),
            lax.psum_scatter(grads[2], GRP, scatter_dimension=0, tiled=True),
            lax.psum_scatter(grads[3], GRP, scatter_dimension=0, tiled=True),
        )
    input_grad = from_packs(upstream)
    full_part, head_part, up_part = (jnp.stack([p[i] for p in parts]) for i in range(3))
    full_part = lax.psum_scatter(full_part, "tp", scatter_dimension=2, tiled=True)
    full_part, head_part, up_part = lax.psum((full_part, head_part, up_part), GRP)
    return (
        outputs,
        input_grad,
        *(jnp.stack([s[i] for s in shards]).astype(F32) for i in range(4)),
        jnp.concatenate([head_part, full_part[:, 0:2]], axis=1),
        full_part[:, 2:4],
        full_part[:, 4:6],
        up_part,
    )


def solution(mesh):
    wide = P(None, GRP, "tp")
    vec = P(None, None, "tp")
    qkv = P(None, None, GRP, "tp")
    owner = P(None, GRP)
    return jax.shard_map(
        local,
        mesh=mesh,
        in_specs=(
            wide, wide, wide, P(None, "fsdp"), owner, owner, qkv, wide, wide, wide,
            vec, vec, vec, P(None, "tp"),
        ),
        out_specs=(wide, wide, qkv, wide, wide, wide, vec, vec, vec, P(None, "tp")),
        check_vma=False,
    )
```

```python
import functools
import math

import jax
import jax.numpy as jnp
from jax import lax
from jax.experimental import pallas as pl
from jax.experimental.pallas import tpu as pltpu
from jax.sharding import PartitionSpec as P

HD = 64
NEG = -1e30
EPS = 1e-05
BF = jnp.bfloat16
F32 = jnp.float32
GRP = ("fsdp", "ctx")


def dot(left, right, dims):
    return lax.dot_general(left, right, (dims, ((), ())), preferred_element_type=F32)


NN = ((1,), (0,))
NT = ((1,), (1,))
TN = ((0,), (0,))

MESH = pl.DeviceIdType.MESH
LOG2E = 1.4426950408889634


def gelu_pair(values):
    bell = jnp.exp2(values * values * (-0.5 * LOG2E))
    t = 1.0 / (1.0 + (0.3275911 * math.sqrt(0.5)) * jnp.abs(values))
    poly = t * (
        0.127414796 + t * (-0.142248368 + t * (0.7107068705 + t * (-0.7265760135 + t * 0.5307027145)))
    )
    tail = poly * bell
    phi = jnp.where(values < 0, tail, 1.0 - tail)
    return values * phi, phi + values * bell * (1.0 / math.sqrt(2.0 * math.pi))


class Links:
    def __init__(self):
        self.fs, self.cx = lax.axis_size("fsdp"), lax.axis_size("ctx")
        self.f, self.c, self.t = (lax.axis_index(a) for a in ("fsdp", "ctx", "tp"))
        self.core, self.chip = lax.rem(self.t, 2), self.t // 2
        self.sib_t = self.t + 1 - 2 * self.core
        self.peer_t = lax.rem(self.t + 2, 4)
        self.sib = (self.f, self.c, self.sib_t)
        self.peer = (self.f, self.c, self.peer_t)
        self.across = (self.f, 1 - self.c, self.t)

    def away(self, step):
        return (lax.rem(self.f + step, self.fs), self.c, self.t)

    def barrier(self):
        sem = pltpu.get_barrier_semaphore()
        for target in (self.sib, self.peer, self.across):
            pl.semaphore_signal(sem, inc=1, device_id=target, device_id_type=MESH)

        def greet(step, carry):
            pl.semaphore_signal(sem, inc=1, device_id=self.away(step), device_id_type=MESH)
            return carry

        lax.fori_loop(1, self.fs, greet, 0)
        pl.semaphore_wait(sem, 2 + self.fs)


def remote(src, dst, send, recv, target):
    return pltpu.make_async_remote_copy(
        src_ref=src, dst_ref=dst, send_sem=send, recv_sem=recv,
        device_id=target, device_id_type=MESH,
    )


class RowSum:
    def __init__(self, lk, part, from_sib, to_peer, from_peer, send, recv):
        self.lk, self.part, self.from_sib = lk, part, from_sib
        self.to_peer, self.from_peer, self.send, self.recv = to_peer, from_peer, send, recv

    def sib_copy(self, k):
        return remote(
            self.part.at[k, 1 - self.lk.core], self.from_sib.at[k],
            self.send.at[k, 0], self.recv.at[k, 0], self.lk.sib,
        )

    def peer_copy(self, k):
        return remote(
            self.to_peer.at[k], self.from_peer.at[k],
            self.send.at[k, 1], self.recv.at[k, 1], self.lk.peer,
        )

    def first(self, k):
        self.sib_copy(k).start()

    def second(self, k):
        self.sib_copy(k).wait_recv()
        other = 1 - self.lk.chip
        total = self.part[k, self.lk.core, other].astype(F32) + self.from_sib[k, other].astype(F32)
        self.to_peer[k] = total.astype(BF)
        self.peer_copy(k).start()

    def last(self, k):
        own = self.part[k, self.lk.core, self.lk.chip].astype(F32)
        own = own + self.from_sib[k, self.lk.chip].astype(F32)
        self.peer_copy(k).wait_recv()
        self.sib_copy(k).wait_send()
        self.peer_copy(k).wait_send()
        return own + self.from_peer[k].astype(F32)


class RowGather:
    def __init__(self, lk, rows, send, recv):
        self.lk, self.rows, self.send, self.recv = lk, rows, send, recv

    def block(self, ref, index):
        return ref.at[pl.ds(pl.multiple_of(index * self.rows, self.rows), self.rows)]

    def copy(self, ref, k, which):
        index = self.lk.t if which < 2 else self.lk.peer_t
        part = self.block(ref, index)
        target = self.lk.peer if which == 0 else self.lk.sib
        return remote(part, part, self.send.at[k, which], self.recv.at[k, which], target)

    def first(self, ref, k):
        self.copy(ref, k, 0).start()
        self.copy(ref, k, 1).start()

    def second(self, ref, k):
        self.copy(ref, k, 0).wait_recv()
        self.copy(ref, k, 2).start()

    def last(self, ref, k):
        self.copy(ref, k, 1).wait_recv()
        self.copy(ref, k, 2).wait_recv()
        for which in range(3):
            self.copy(ref, k, which).wait_send()


class WeightGather:
    def __init__(self, lk, shard, full, z_send, z_recv, x_send, x_recv, own):
        self.lk, self.shard, self.full = lk, shard, full
        self.z_send, self.z_recv, self.x_send, self.x_recv = z_send, z_recv, x_send, x_recv
        self.own = own
        self.rows = shard.shape[1]

    def block(self, chunk, f, c):
        first = pl.multiple_of((f * self.lk.cx + c) * self.rows, self.rows)
        return self.full.at[chunk, pl.ds(first, self.rows)]

    def z_copy(self, chunk, step):
        return remote(
            self.shard.at[chunk], self.block(chunk, self.lk.f, self.lk.c),
            self.z_send.at[chunk, step], self.z_recv.at[chunk, self.lk.fs - step],
            self.lk.away(step),
        )

    def x_copy(self, chunk, step):
        f = lax.rem(self.lk.f + step, self.lk.fs)
        part = self.block(chunk, f, self.lk.c)
        return remote(
            part, part, self.x_send.at[chunk, step], self.x_recv.at[chunk, step], self.lk.across
        )

    def x_own(self, chunk):
        return remote(
            self.shard.at[chunk], self.block(chunk, self.lk.f, self.lk.c),
            self.x_send.at[chunk, 0], self.x_recv.at[chunk, 0], self.lk.across,
        )

    def own_copy(self, chunk):
        return pltpu.make_async_copy(
            self.shard.at[chunk], self.block(chunk, self.lk.f, self.lk.c), self.own.at[chunk]
        )

    def each(self, first, work):
        def body(step, carry):
            work(step)
            return carry

        lax.fori_loop(first, self.lk.fs, body, 0)

    def start(self, chunk):
        self.own_copy(chunk).start()
        self.x_own(chunk).start()
        self.each(1, lambda step: self.z_copy(chunk, step).start())

    def forward(self, chunk):
        def work(step):
            self.z_copy(chunk, self.lk.fs - step).wait_recv()
            self.x_copy(chunk, step).start()

        self.each(1, work)

    def finish(self, chunk):
        self.own_copy(chunk).wait()
        self.each(0, lambda step: self.x_copy(chunk, step).wait_recv())

    def drain(self, chunk):
        self.each(1, lambda step: self.z_copy(chunk, step).wait_send())
        self.each(0, lambda step: self.x_copy(chunk, step).wait_send())


def store_part(part, k, cols, values, rows):
    for block in range(4):
        part[k, block % 2, block // 2, :, cols] = values[block * rows : (block + 1) * rows].astype(
            BF
        )


def masked_scores(query, key_rows, same_seq):
    return jnp.where(
        same_seq, dot(query, key_rows, NT) * (LOG2E / math.sqrt(HD)), NEG
    )


def forward_kernel(
    act_in, shard, vec, head_bias, up_bias, seg_col, seg_row,
    out_w, out_act, out_qkv, out_att, out_nrm, out_std, out_hid, out_glu, out_dglu, out_lse,
    out_u,
    w, act, qkv, att, nrm, std, hid, glu, dglu, lse, u, h, part, from_sib, to_peer, from_peer,
    in_sem, out_sem, rs_send, rs_recv, ag_send, ag_recv, z_send, z_recv, x_send, x_recv, own,
):
    layers, packs, rows, width = act.shape
    mine = rows // 4
    heads_width = att.shape[3]
    chunks = shard.shape[0]
    lk = Links()
    lk.barrier()
    rs = RowSum(lk, part, from_sib, to_peer, from_peer, rs_send, rs_recv)
    ag = RowGather(lk, mine, ag_send, ag_recv)
    wg = WeightGather(lk, shard, w, z_send, z_recv, x_send, x_recv, own)
    pending = []

    def save(src, dst):
        copy = pltpu.make_async_copy(src, dst, out_sem.at[len(pending)])
        copy.start()
        pending.append(copy)

    load = pltpu.make_async_copy(act_in, act.at[0], in_sem)
    load.start()
    wg.start(0)
    load.wait()
    my_rows = pl.ds(pl.multiple_of(lk.t * mine, mine), mine)
    for k in range(packs):
        u[k] = act[0, k, my_rows].astype(F32)
    lse[...] = jnp.zeros_like(lse)
    wg.forward(0)
    wg.start(1)
    wg.finish(0)
    save(w.at[0], out_w.at[0])

    def project(layer, k):
        for j in range(3):
            cols = slice(j * heads_width, (j + 1) * heads_width)
            acc = dot(act[layer, k], w[3 * layer, :, cols], NN)
            if j != 1:
                acc = acc + head_bias[layer, j // 2 : j // 2 + 1]
            qkv[layer, k, :, cols] = acc.astype(BF)
        save(qkv.at[layer, k], out_qkv.at[layer, k])

    def attention(layer, k):
        same_seq = seg_col[k] == seg_row[k]
        for head in range(heads_width // HD):
            cols = [slice(j * heads_width + head * HD, j * heads_width + (head + 1) * HD) for j in range(3)]
            scores = masked_scores(qkv[layer, k, :, cols[0]], qkv[layer, k, :, cols[1]], same_seq)
            top = jnp.max(scores, axis=1, keepdims=True)
            weighted = jnp.exp2(scores - top)
            total = jnp.sum(weighted, axis=1, keepdims=True)
            lse[layer, k, :, head : head + 1] = top + jnp.log2(total)
            probs = (weighted * (1.0 / total)).astype(BF)
            att[layer, k, :, cols[0]] = dot(probs, qkv[layer, k, :, cols[2]], NN).astype(BF)
        save(lse.at[layer, k], out_lse.at[layer, k])
        save(att.at[layer, k], out_att.at[layer, k])
        for j in range(width // 256):
            cols = slice(j * 256, (j + 1) * 256)
            acc = dot(att[layer, k], w[3 * layer, cols, 3 * heads_width :], NT)
            store_part(part, k, cols, acc, mine)
        rs.first(k)

    def normalize(layer, which, k, resid):
        mean = jnp.mean(resid, axis=1, keepdims=True)
        centred = resid - mean
        scale = lax.rsqrt(jnp.mean(centred * centred, axis=1, keepdims=True) + EPS)
        normed = centred * scale
        nrm[layer, which, k] = normed
        std[layer, which, k] = jnp.broadcast_to(scale, std.shape[3:])
        save(nrm.at[layer, which, k], out_nrm.at[layer, which, k])
        save(std.at[layer, which, k], out_std.at[layer, which, k])
        return normed * vec[layer, 2 + which : 3 + which] + vec[layer, 4 + which : 5 + which]

    def norm_one(layer, k):
        hidden = normalize(layer, 0, k, u[k] + rs.last(k) + vec[layer, 0:1])
        h[k] = hidden
        hid[layer, k, my_rows] = hidden.astype(BF)
        ag.first(hid.at[layer, k], k)

    def expand(layer, k):
        def tile(j, carry):
            cols = pl.ds(pl.multiple_of(j * 256, 256), 256)
            acc = dot(hid[layer, k], w[3 * layer + 1, :, cols], NN) + up_bias[layer, :, cols]
            value, slope = gelu_pair(acc)
            glu[layer, k, :, cols] = value.astype(BF)
            dglu[layer, k, :, cols] = slope.astype(BF)
            return carry

        lax.fori_loop(0, width // 256, tile, 0)
        save(glu.at[layer, k], out_glu.at[layer, k])
        save(dglu.at[layer, k], out_dglu.at[layer, k])

    def contract(layer, k):
        def tile(j, carry):
            cols = pl.ds(pl.multiple_of(j * 256, 256), 256)
            acc = dot(glu[layer, k], w[3 * layer + 2, cols, :], NT)
            store_part(part, k, cols, acc, mine)
            return carry

        lax.fori_loop(0, width // 256, tile, 0)
        rs.first(k)

    def norm_two(layer, k):
        out = normalize(layer, 1, k, h[k] + rs.last(k) + vec[layer, 1:2])
        u[k] = out
        if layer + 1 < layers:
            act[layer + 1, k, my_rows] = out.astype(BF)
            ag.first(act.at[layer + 1, k], k)
        else:
            save(u.at[k], out_u.at[k])

    def weights_next(chunk):
        if chunk < chunks:
            if chunk + 1 < chunks:
                wg.start(chunk + 1)
            wg.forward(chunk)

    def weights_ready(chunk):
        wg.finish(chunk)
        save(w.at[chunk], out_w.at[chunk])

    for layer in range(layers):
        base = 3 * layer
        more = layer + 1 < layers
        if layer:
            weights_ready(base)
            ag.last(act.at[layer, 0], 0)
            save(act.at[layer, 0], out_act.at[layer - 1, 0])
        project(layer, 0)
        if layer:
            ag.second(act.at[layer, 1], 1)
        attention(layer, 0)
        weights_next(base + 1)
        if layer:
            ag.last(act.at[layer, 1], 1)
            save(act.at[layer, 1], out_act.at[layer - 1, 1])
        project(layer, 1)
        rs.second(0)
        attention(layer, 1)
        norm_one(layer, 0)
        rs.second(1)
        ag.second(hid.at[layer, 0], 0)
        norm_one(layer, 1)
        weights_ready(base + 1)
        weights_next(base + 2)
        ag.last(hid.at[layer, 0], 0)
        save(hid.at[layer, 0], out_hid.at[layer, 0])
        expand(layer, 0)
        ag.second(hid.at[layer, 1], 1)
        weights_ready(base + 2)
        contract(layer, 0)
        weights_next(base + 3)
        ag.last(hid.at[layer, 1], 1)
        save(hid.at[layer, 1], out_hid.at[layer, 1])
        expand(layer, 1)
        rs.second(0)
        contract(layer, 1)
        norm_two(layer, 0)
        rs.second(1)
        if more:
            ag.second(act.at[layer + 1, 0], 0)
        norm_two(layer, 1)
    for chunk in range(chunks):
        wg.drain(chunk)
    for copy in pending:
        copy.wait()


def forward(act, shard, vec, head_bias, up_bias, seg_col, seg_row):
    packs, rows, width = act.shape
    chunks = shard.shape[0]
    layers = chunks // 3
    mine = rows // 4
    heads = head_bias.shape[2]
    fs = lax.axis_size("fsdp")
    shapes = dict(
        w=((chunks, width, width), BF),
        act=((layers, packs, rows, width), BF),
        qkv=((layers, packs, rows, 3 * heads), BF),
        att=((layers, packs, rows, heads), BF),
        nrm=((layers, 2, packs, mine, width), F32),
        std=((layers, 2, packs, mine, 128), F32),
        hid=((layers, packs, rows, width), BF),
        glu=((layers, packs, rows, width), BF),
        dglu=((layers, packs, rows, width), BF),
        lse=((layers, packs, rows, 128), F32),
        u=((packs, mine, width), F32),
    )
    outs = {name: jax.ShapeDtypeStruct(*shape) for name, shape in shapes.items()}
    outs["act"] = jax.ShapeDtypeStruct((layers - 1, packs, rows, width), BF)
    copies = chunks + (layers - 1) * packs + layers * packs * 10 + packs
    dma = pltpu.SemaphoreType.DMA
    whole = pl.BlockSpec(memory_space=pl.ANY)
    vmem = pl.BlockSpec(memory_space=pltpu.VMEM)
    return pl.pallas_call(
        forward_kernel,
        in_specs=[whole, whole, vmem, vmem, vmem, vmem, vmem],
        out_specs=[whole] * len(outs),
        out_shape=list(outs.values()),
        scratch_shapes=[pltpu.VMEM(*shape) for shape in shapes.values()]
        + [
            pltpu.VMEM((packs, mine, width), F32),
            pltpu.VMEM((packs, 2, 2, mine, width), BF),
            pltpu.VMEM((packs, 2, mine, width), BF),
            pltpu.VMEM((packs, mine, width), BF),
            pltpu.VMEM((packs, mine, width), BF),
            dma(()), dma((copies,)),
            dma((packs, 2)), dma((packs, 2)), dma((packs, 3)), dma((packs, 3)),
            dma((chunks, fs)), dma((chunks, fs)), dma((chunks, fs)), dma((chunks, fs)),
            dma((chunks,)),
        ],
        compiler_params=pltpu.CompilerParams(
            collective_id=0, has_side_effects=True, vmem_limit_bytes=60 << 20
        ),
        name="forward",
    )(act, shard, vec, head_bias, up_bias, seg_col, seg_row)


class GradScatter:
    def __init__(self, lk, grad, from_x, from_z, x_send, x_recv, z_send, z_recv):
        self.lk, self.grad, self.from_x, self.from_z = lk, grad, from_x, from_z
        self.x_send, self.x_recv, self.z_send, self.z_recv = x_send, x_recv, z_send, z_recv
        self.rows = from_x.shape[2]

    def block(self, chunk, step, c):
        f = lax.rem(self.lk.f + step, self.lk.fs)
        first = pl.multiple_of((f * self.lk.cx + c) * self.rows, self.rows)
        return self.grad.at[chunk, pl.ds(first, self.rows)]

    def x_copy(self, chunk, step):
        return remote(
            self.block(chunk, step, 1 - self.lk.c), self.from_x.at[chunk, step],
            self.x_send.at[chunk, step], self.x_recv.at[chunk, step], self.lk.across,
        )

    def z_copy(self, chunk, step):
        slot = self.lk.fs - step
        return remote(
            self.block(chunk, step, self.lk.c), self.from_z.at[chunk, slot - 1],
            self.z_send.at[chunk, step], self.z_recv.at[chunk, slot], self.lk.away(step),
        )

    def each(self, first, work):
        def body(step, carry):
            work(step)
            return carry

        lax.fori_loop(first, self.lk.fs, body, 0)

    def first(self, chunk):
        self.each(1, lambda step: self.x_copy(chunk, step).start())
        self.x_copy(chunk, 0).start()

    def second(self, chunk):
        def work(step):
            self.x_copy(chunk, step).wait_recv()
            own = self.block(chunk, step, self.lk.c)
            own[...] = (own[...].astype(F32) + self.from_x[chunk, step].astype(F32)).astype(BF)
            self.z_copy(chunk, step).start()

        self.each(1, work)

    def last(self, chunk, out):
        self.x_copy(chunk, 0).wait_recv()
        out[...] = self.block(chunk, 0, self.lk.c)[...].astype(F32) + self.from_x[chunk, 0].astype(F32)

        def work(step):
            self.z_copy(chunk, self.lk.fs - step).wait_recv()
            out[...] = out[...] + self.from_z[chunk, step - 1].astype(F32)

        self.each(1, work)

    def drain(self, chunk):
        self.each(0, lambda step: self.x_copy(chunk, step).wait_send())
        self.each(1, lambda step: self.z_copy(chunk, step).wait_send())


def backward_kernel(
    up_in, act_first, act_more, w_in, qkv_in, att_in, nrm_in, std_in, hid_in, glu_in, dglu_in,
    lse_in, vec, seg_col, seg_row,
    out_qkv, out_out, out_up, out_down, out_u, out_vec, out_head, out_bias,
    w, qkv, att, nrm, std, hid, glu, dglu, lse, up, gtwo, gl, gm, gup, gqkv, gatt,
    part, from_sib, to_peer, from_peer, grad, from_x, from_z, gsum, low,
    in_sem, out_sem, rs_send, rs_recv, ag_send, ag_recv, x_send, x_recv, z_send, z_recv,
):
    packs, rows, width = hid.shape
    layers = vec.shape[0]
    mine = rows // 4
    heads_width = att.shape[2]
    lk = Links()
    sources = dict(
        nrm1=lambda layer: (nrm_in.at[layer, 1], nrm.at[1]),
        std1=lambda layer: (std_in.at[layer, 1], std.at[1]),
        nrm0=lambda layer: (nrm_in.at[layer, 0], nrm.at[0]),
        std0=lambda layer: (std_in.at[layer, 0], std.at[0]),
        w2=lambda layer: (w_in.at[3 * layer + 2], w.at[2]),
        dglu=lambda layer: (dglu_in.at[layer], dglu),
        w1=lambda layer: (w_in.at[3 * layer + 1], w.at[1]),
        glu=lambda layer: (glu_in.at[layer], glu),
        hid=lambda layer: (hid_in.at[layer], hid),
        w0=lambda layer: (w_in.at[3 * layer], w.at[0]),
        qkv=lambda layer: (qkv_in.at[layer], qkv),
        lse=lambda layer: (lse_in.at[layer], lse),
        att=lambda layer: (att_in.at[layer], att),
        act=lambda layer: (act_more.at[layer - 1] if layer else act_first, hid),
    )
    order = {name: index for index, name in enumerate(sources)}

    def fetch(name, layer):
        if layer >= 0:
            src, dst = sources[name](layer)
            pltpu.make_async_copy(src, dst, in_sem.at[order[name]]).start()

    def ready(name, layer):
        src, dst = sources[name](layer)
        pltpu.make_async_copy(src, dst, in_sem.at[order[name]]).wait()

    load = pltpu.make_async_copy(up_in, up, in_sem.at[len(order)])
    load.start()
    for name in sources:
        if name != "act":
            fetch(name, layers - 1)
    lk.barrier()
    rs = RowSum(lk, part, from_sib, to_peer, from_peer, rs_send, rs_recv)
    ag = RowGather(lk, mine, ag_send, ag_recv)
    gs = GradScatter(lk, grad, from_x, from_z, x_send, x_recv, z_send, z_recv)
    my_rows = pl.ds(pl.multiple_of(lk.t * mine, mine), mine)
    pending = []
    held = {}
    used = []

    def save(src, dst):
        copy = pltpu.make_async_copy(src, dst, out_sem.at[len(used)])
        copy.start()
        used.append(1)
        pending.append(copy)

    out_vec[...] = jnp.zeros_like(out_vec)
    out_head[...] = jnp.zeros_like(out_head)
    out_bias[...] = jnp.zeros_like(out_bias)

    def norm_back(layer, which, k, upstream):
        normed = nrm[which, k]
        scale = std[which, k][:, 0:1]
        out_vec[layer, 2 + which : 3 + which] += jnp.sum(upstream * normed, axis=0, keepdims=True)
        out_vec[layer, 4 + which : 5 + which] += jnp.sum(upstream, axis=0, keepdims=True)
        scaled = upstream * vec[layer, 2 + which : 3 + which]
        first = jnp.mean(scaled, axis=1, keepdims=True)
        second = jnp.mean(scaled * normed, axis=1, keepdims=True)
        result = scale * (scaled - first - normed * second)
        out_vec[layer, which : which + 1] += jnp.sum(result, axis=0, keepdims=True)
        return result

    def norm_two(layer, k):
        result = norm_back(layer, 1, k, up[k])
        gtwo[k] = result
        gl[k, my_rows] = result.astype(BF)
        ag.first(gl.at[k], k)

    def norm_one(layer, k):
        result = norm_back(layer, 0, k, gtwo[k] + rs.last(k))
        up[k] = result
        gm[k, my_rows] = result.astype(BF)
        ag.first(gm.at[k], k)

    def tiles(work):
        def body(j, carry):
            work(pl.ds(pl.multiple_of(j * 256, 256), 256))
            return carry

        lax.fori_loop(0, width // 256, body, 0)

    def through_down(layer, k):
        def tile(cols):
            grad_gelu = dot(gl[k], w[2, :, cols], NN).astype(BF).astype(F32)
            result = (grad_gelu * dglu[k, :, cols].astype(F32)).astype(BF)
            gup[k, :, cols] = result
            out_bias[layer, :, cols] += jnp.sum(result.astype(F32), axis=0, keepdims=True)

        tiles(tile)

    def through_up(layer, k):
        tiles(lambda cols: store_part(part, k, cols, dot(gup[k], w[1, cols, :], NT), mine))
        rs.first(k)

    def through_out(k):
        gatt[k] = dot(gm[k], w[0, :, 3 * heads_width :], NN).astype(BF)

    def attention(layer, k):
        same_seq = seg_col[k] == seg_row[k]
        scale = 1.0 / math.sqrt(HD)
        for head in range(heads_width // HD):
            cols = [slice(j * heads_width + head * HD, j * heads_width + (head + 1) * HD) for j in range(3)]
            query, keys, values = (qkv[k, :, c] for c in cols)
            grads = gatt[k, :, cols[0]]
            probs = jnp.exp2(masked_scores(query, keys, same_seq) - lse[k, :, head : head + 1])
            grad_probs = dot(grads, values, NT)
            delta = jnp.sum(probs * grad_probs, axis=1, keepdims=True)
            grad_scores = (probs * (grad_probs - delta)).astype(BF)
            gqkv[k, :, cols[0]] = (dot(grad_scores, keys, NN) * scale).astype(BF)
            gqkv[k, :, cols[1]] = (dot(grad_scores, query, TN) * scale).astype(BF)
            gqkv[k, :, cols[2]] = dot(probs.astype(BF), grads, TN).astype(BF)
        for j in range(2):
            cols = slice(2 * j * heads_width, (2 * j + 1) * heads_width)
            out_head[layer, j : j + 1] += jnp.sum(
                gqkv[k, :, cols].astype(F32), axis=0, keepdims=True
            )

    def through_qkv(k):
        tiles(
            lambda cols: store_part(
                part, k, cols, dot(gqkv[k], w[0, cols, : 3 * heads_width], NT), mine
            )
        )
        rs.first(k)

    def product(left, right, cols, right_cols=slice(None)):
        total = dot(left[0, :, cols], right[0, :, right_cols], TN)
        for k in range(1, packs):
            total = total + dot(left[k, :, cols], right[k, :, right_cols], TN)
        return total.astype(BF)

    def down_grad(layer):
        def tile(cols):
            grad[3 * layer + 2, cols, :] = product(gl, glu, cols)

        tiles(tile)
        gs.first(3 * layer + 2)

    def up_grad(layer):
        def tile(cols):
            grad[3 * layer + 1, cols, :] = product(hid, gup, cols)

        tiles(tile)
        gs.first(3 * layer + 1)

    def first_grad(layer):
        def tile(cols):
            grad[3 * layer, cols, : 3 * heads_width] = product(hid, gqkv, cols)
            grad[3 * layer, cols, 3 * heads_width :] = product(gm, att, cols)

        tiles(tile)
        gs.first(3 * layer)

    def emit(layer, which):
        chunk = 3 * layer + which
        out = gsum.at[which]
        while held.get(which):
            held[which].pop().wait()
        gs.last(chunk, out)
        held[which] = []
        saved = len(pending)
        if which == 2:
            save(out, out_down.at[layer])
        elif which == 1:
            save(out, out_up.at[layer])
        else:
            for c in range(3):
                save(out.at[:, c * heads_width : (c + 1) * heads_width], out_qkv.at[layer, c])
            save(out.at[:, 3 * heads_width :], out_out.at[layer])
        held[which] = [pending.pop() for _ in range(len(pending) - saved)]

    load.wait()
    top = layers - 1
    ready("nrm1", top)
    ready("std1", top)
    for k in range(packs):
        norm_two(top, k)
    fetch("nrm1", top - 1)
    fetch("std1", top - 1)
    for layer in reversed(range(layers)):
        ag.second(gl.at[0], 0)
        if layer < top:
            ready("act", layer + 1)
            first_grad(layer + 1)
            fetch("att", layer)
            fetch("hid", layer)
        ready("w2", layer)
        ready("dglu", layer)
        ag.last(gl.at[0], 0)
        through_down(layer, 0)
        ag.second(gl.at[1], 1)
        ready("w1", layer)
        through_up(layer, 0)
        ag.last(gl.at[1], 1)
        through_down(layer, 1)
        fetch("w2", layer - 1)
        fetch("dglu", layer - 1)
        rs.second(0)
        through_up(layer, 1)
        fetch("w1", layer - 1)
        ready("glu", layer)
        down_grad(layer)
        fetch("glu", layer - 1)
        rs.second(1)
        ready("nrm0", layer)
        ready("std0", layer)
        norm_one(layer, 0)
        if layer < top:
            gs.second(3 * (layer + 1) + 1)
        ready("hid", layer)
        up_grad(layer)
        fetch("act", layer)
        ag.second(gm.at[0], 0)
        norm_one(layer, 1)
        fetch("nrm0", layer - 1)
        fetch("std0", layer - 1)
        ready("w0", layer)
        ready("qkv", layer)
        ready("lse", layer)
        ag.last(gm.at[0], 0)
        through_out(0)
        attention(layer, 0)
        ag.second(gm.at[1], 1)
        through_qkv(0)
        if layer < top:
            gs.second(3 * (layer + 1))
        else:
            gs.second(3 * layer + 2)
        ag.last(gm.at[1], 1)
        through_out(1)
        rs.second(0)
        attention(layer, 1)
        fetch("qkv", layer - 1)
        fetch("lse", layer - 1)
        through_qkv(1)
        fetch("w0", layer - 1)
        ready("att", layer)
        if layer == 0:
            ready("act", layer)
            first_grad(0)
        for k in range(packs):
            if k:
                rs.second(k)
            up[k] = rs.last(k) + up[k]
            if layer:
                if k == 0:
                    ready("nrm1", layer - 1)
                    ready("std1", layer - 1)
                norm_two(layer - 1, k)
            else:
                low[k] = up[k].astype(BF)
                save(low.at[k], out_u.at[k])
        if layer:
            fetch("nrm1", layer - 2)
            fetch("std1", layer - 2)
        if layer < top:
            for which in (2, 1, 0):
                emit(layer + 1, which)
    gs.second(2)
    emit(0, 2)
    gs.second(1)
    emit(0, 1)
    gs.second(0)
    emit(0, 0)
    for chunk in range(3 * layers):
        gs.drain(chunk)
    for copy in pending + sum(held.values(), []):
        copy.wait()


def backward(upstream, act, saved, vec, seg_col, seg_row):
    full_w, o_act, o_qkv, o_att, o_nrm, o_std, o_hid, o_glu, o_dglu, o_lse = saved
    packs, rows, width = act.shape
    layers, mine = vec.shape[0], rows // 4
    chunks = 3 * layers
    heads = o_att.shape[3]
    fs, cx = lax.axis_size("fsdp"), lax.axis_size("ctx")
    shard = width // (fs * cx)
    outs = [
        jax.ShapeDtypeStruct((layers, 3, shard, heads), F32),
        jax.ShapeDtypeStruct((layers, shard, heads), F32),
        jax.ShapeDtypeStruct((layers, shard, width), F32),
        jax.ShapeDtypeStruct((layers, shard, width), F32),
        jax.ShapeDtypeStruct((packs, mine, width), BF),
        jax.ShapeDtypeStruct((layers, 6, width), F32),
        jax.ShapeDtypeStruct((layers, 2, heads), F32),
        jax.ShapeDtypeStruct((layers, 1, width), F32),
    ]
    dma = pltpu.SemaphoreType.DMA
    whole = pl.BlockSpec(memory_space=pl.ANY)
    vmem = pl.BlockSpec(memory_space=pltpu.VMEM)
    full = pltpu.VMEM((packs, rows, width), BF)
    rowed = pltpu.VMEM((packs, mine, width), F32)
    return pl.pallas_call(
        backward_kernel,
        in_specs=[whole] * 12 + [vmem] * 3,
        out_specs=[whole] * 5 + [vmem] * 3,
        out_shape=outs,
        scratch_shapes=[
            pltpu.VMEM((3, width, width), BF),
            pltpu.VMEM((packs, rows, 3 * heads), BF),
            pltpu.VMEM((packs, rows, heads), BF),
            pltpu.VMEM((2, packs, mine, width), F32),
            pltpu.VMEM((2, packs, mine, 128), F32),
            full, full, full,
            pltpu.VMEM((packs, rows, 128), F32),
            rowed, rowed,
            full, full, full,
            pltpu.VMEM((packs, rows, 3 * heads), BF),
            pltpu.VMEM((packs, rows, heads), BF),
            pltpu.VMEM((packs, 2, 2, mine, width), BF),
            pltpu.VMEM((packs, 2, mine, width), BF),
            pltpu.VMEM((packs, mine, width), BF),
            pltpu.VMEM((packs, mine, width), BF),
            pltpu.VMEM((chunks, width, width), BF),
            pltpu.VMEM((chunks, fs, shard, width), BF),
            pltpu.VMEM((chunks, fs - 1, shard, width), BF),
            pltpu.VMEM((3, shard, width), F32),
            pltpu.VMEM((packs, mine, width), BF),
            dma((15,)), dma((packs + 6 * layers,)),
            dma((packs, 2)), dma((packs, 2)), dma((packs, 3)), dma((packs, 3)),
            dma((chunks, fs)), dma((chunks, fs)), dma((chunks, fs)), dma((chunks, fs)),
        ],
        compiler_params=pltpu.CompilerParams(
            collective_id=1, has_side_effects=True, vmem_limit_bytes=60 << 20
        ),
        name="backward",
    )(
        upstream, act, o_act, full_w, o_qkv, o_att, o_nrm, o_std, o_hid, o_glu, o_dglu, o_lse,
        vec, seg_col, seg_row,
    )


def mm(spec, left, right):
    return jnp.einsum(spec, left, right, preferred_element_type=F32)


def local(
    tokens, time_embed, cotangent, segment_ids, to_owner, from_owner,
    w_qkv, w_out, w_up, w_down, biases, norm_gain, norm_bias, up_bias,
):
    micro, rows, width = tokens.shape
    layers = w_qkv.shape[0]
    fs, cx, tp = (lax.axis_size(a) for a in ("fsdp", "ctx", "tp"))
    groups = fs * cx
    mine = micro // cx
    pack = segment_ids.shape[1]
    sends = rows // fs
    my_first = lax.axis_index("ctx") * mine
    tp_index = lax.axis_index("tp")

    shard = jnp.concatenate(
        [w_qkv[:, 0], w_qkv[:, 1], w_qkv[:, 2], w_out, w_up, w_down], axis=2
    )
    shard = shard.reshape(layers, shard.shape[1], 3, -1).transpose(0, 2, 1, 3)
    shard = shard.reshape(layers * 3, shard.shape[2], -1)
    vec = jnp.concatenate([biases[:, 2:], norm_gain, norm_bias], axis=1)
    vec = lax.all_gather(vec, "tp", axis=2, tiled=True)
    vectors = [
        (biases[layer, :2], vec[layer, 0:2], vec[layer, 2:4], vec[layer, 4:6], up_bias[layer])
        for layer in range(layers)
    ]

    to_pack = to_owner // pack
    earlier = jnp.arange(rows)[None, :] < jnp.arange(rows)[:, None]
    rank = jnp.sum((to_pack[:, :, None] == to_pack[:, None, :]) & earlier[None], axis=2)
    out_slot = to_pack * sends + rank
    pick_out = (jnp.arange(rows)[None, :, None] == out_slot[:, None, :]).astype(BF)
    given = lax.all_gather(from_owner, "ctx", axis=1, tiled=True)
    given = lax.dynamic_slice_in_dim(given, my_first, mine)
    source = given // rows
    before = (given[:, None, :] < given[:, :, None]) & (
        given[:, None, :] >= (source * rows)[:, :, None]
    )
    in_slot = source * sends + jnp.sum(before, axis=2)
    pick_in = (jnp.arange(pack)[None, None, :] == in_slot[:, :, None]).astype(BF)

    def to_packs(values):
        slots = mm("msg,mgw->msw", pick_out, values).astype(BF)
        slots = slots.reshape(cx, mine, fs, sends, width).transpose(2, 0, 1, 3, 4)
        slots = slots.reshape(groups, mine, sends, width)
        slots = lax.all_to_all(slots, GRP, split_axis=0, concat_axis=0, tiled=True)
        slots = slots.transpose(1, 0, 2, 3).reshape(mine, pack, width)
        return mm("kps,ksw->kpw", pick_in, slots).astype(BF)

    def from_packs(values):
        values = lax.all_to_all(values.astype(BF), "tp", split_axis=2, concat_axis=1, tiled=True)
        slots = mm("kps,kpw->ksw", pick_in, values).astype(BF)
        slots = slots.reshape(mine, groups, sends, width).transpose(1, 0, 2, 3)
        slots = lax.all_to_all(slots, GRP, split_axis=0, concat_axis=0, tiled=True)
        slots = slots.reshape(fs, cx, mine, sends, width).transpose(1, 2, 0, 3, 4)
        return mm("msg,msw->mgw", pick_out, slots.reshape(micro, rows, width))

    embedded = (tokens.astype(F32) + time_embed.astype(F32)).astype(BF)
    act = lax.all_gather(to_packs(embedded), "tp", axis=2, tiled=True)
    upstream = lax.all_to_all(
        to_packs(cotangent), "tp", split_axis=1, concat_axis=2, tiled=True
    ).astype(F32)
    seg = lax.dynamic_slice_in_dim(segment_ids, my_first, mine)
    seg_col, seg_row = seg[:, :, None], seg[:, None, :]

    *saved, resid = forward(
        act, shard, vec, biases[:, :2], up_bias[:, None], seg_col, seg_row
    )
    outputs = from_packs(resid)
    g_qkv, g_out, g_up, g_down, upstream, full_part, head_part, up_part = backward(
        upstream, act, saved, vec, seg_col, seg_row
    )
    input_grad = from_packs(upstream)
    up_part = up_part[:, 0]
    full_part = lax.psum_scatter(full_part, "tp", scatter_dimension=2, tiled=True)
    full_part, head_part, up_part = lax.psum((full_part, head_part, up_part), GRP)
    return (
        outputs,
        input_grad,
        g_qkv, g_out, g_up, g_down,
        jnp.concatenate([head_part, full_part[:, 0:2]], axis=1),
        full_part[:, 2:4],
        full_part[:, 4:6],
        up_part,
    )


def solution(mesh):
    wide = P(None, GRP, "tp")
    vec = P(None, None, "tp")
    qkv = P(None, None, GRP, "tp")
    owner = P(None, GRP)
    return jax.shard_map(
        local,
        mesh=mesh,
        in_specs=(
            wide, wide, wide, P(None, "fsdp"), owner, owner, qkv, wide, wide, wide,
            vec, vec, vec, P(None, "tp"),
        ),
        out_specs=(wide, wide, qkv, wide, wide, wide, vec, vec, vec, P(None, "tp")),
        check_vma=False,
    )
```

```python
import math

import jax
import jax.numpy as jnp
from jax import lax
from jax.experimental import pallas as pl
from jax.experimental.pallas import tpu as pltpu
from jax.sharding import PartitionSpec as P

HD = 64
NEG = -1e30
EPS = 1e-05
BF = jnp.bfloat16
F32 = jnp.float32
GRP = ("fsdp", "ctx")


def dot(left, right, dims):
    return lax.dot_general(left, right, (dims, ((), ())), preferred_element_type=F32)


NN = ((1,), (0,))
NT = ((1,), (1,))
TN = ((0,), (0,))

MESH = pl.DeviceIdType.MESH
LOG2E = 1.4426950408889634


def gelu_pair(values):
    bell = jnp.exp2(values * values * (-0.5 * LOG2E))
    t = 1.0 / (1.0 + (0.3275911 * math.sqrt(0.5)) * jnp.abs(values))
    poly = t * (
        0.127414796 + t * (-0.142248368 + t * (0.7107068705 + t * (-0.7265760135 + t * 0.5307027145)))
    )
    tail = poly * bell
    phi = jnp.where(values < 0, tail, 1.0 - tail)
    return values * phi, phi + values * bell * (1.0 / math.sqrt(2.0 * math.pi))


class Links:
    def __init__(self):
        self.fs, self.cx = lax.axis_size("fsdp"), lax.axis_size("ctx")
        self.f, self.c, self.t = (lax.axis_index(a) for a in ("fsdp", "ctx", "tp"))
        self.core, self.chip = lax.rem(self.t, 2), self.t // 2
        self.sib_t = self.t + 1 - 2 * self.core
        self.peer_t = lax.rem(self.t + 2, 4)
        self.sib = (self.f, self.c, self.sib_t)
        self.peer = (self.f, self.c, self.peer_t)
        self.diag_t = 3 - self.t
        self.diag = (self.f, self.c, self.diag_t)
        self.across = (self.f, 1 - self.c, self.t)
        self.g = self.f * self.cx + self.c

    def away(self, step, c=None):
        return (lax.rem(self.f + step, self.fs), self.c if c is None else c, self.t)

    def barrier(self):
        sem = pltpu.get_barrier_semaphore()
        for target in (self.sib, self.peer, self.diag, self.across):
            pl.semaphore_signal(sem, inc=1, device_id=target, device_id_type=MESH)

        def greet(step, carry):
            for c in (self.c, 1 - self.c):
                pl.semaphore_signal(
                    sem, inc=1, device_id=self.away(step, c), device_id_type=MESH
                )
            return carry

        lax.fori_loop(1, self.fs, greet, 0)
        pl.semaphore_wait(sem, 2 + 2 * self.fs)


def remote(src, dst, send, recv, target):
    return pltpu.make_async_remote_copy(
        src_ref=src, dst_ref=dst, send_sem=send, recv_sem=recv,
        device_id=target, device_id_type=MESH,
    )


class RowSum:
    def __init__(self, lk, part, from_sib, to_peer, from_peer, send, recv):
        self.lk, self.part, self.from_sib = lk, part, from_sib
        self.to_peer, self.from_peer, self.send, self.recv = to_peer, from_peer, send, recv

    def sib_copy(self, k):
        return remote(
            self.part.at[k, 1 - self.lk.core], self.from_sib.at[k],
            self.send.at[k, 0], self.recv.at[k, 0], self.lk.sib,
        )

    def peer_copy(self, k):
        return remote(
            self.to_peer.at[k], self.from_peer.at[k],
            self.send.at[k, 1], self.recv.at[k, 1], self.lk.peer,
        )

    def first(self, k):
        self.sib_copy(k).start()

    def second(self, k):
        self.sib_copy(k).wait_recv()
        other = 1 - self.lk.chip
        total = self.part[k, self.lk.core, other].astype(F32) + self.from_sib[k, other].astype(F32)
        self.to_peer[k] = total.astype(BF)
        self.peer_copy(k).start()

    def last(self, k):
        own = self.part[k, self.lk.core, self.lk.chip].astype(F32)
        own = own + self.from_sib[k, self.lk.chip].astype(F32)
        self.peer_copy(k).wait_recv()
        self.sib_copy(k).wait_send()
        self.peer_copy(k).wait_send()
        return own + self.from_peer[k].astype(F32)


class RowGather:
    def __init__(self, lk, rows, send, recv, by_columns=False):
        self.lk, self.rows, self.send, self.recv = lk, rows, send, recv
        self.by_columns = by_columns

    def block(self, ref, index):
        part = part_of(self.rows, index)
        return ref.at[:, part] if self.by_columns else ref.at[part]

    def copy(self, ref, k, which):
        index = self.lk.t if which < 2 else self.lk.peer_t
        part = self.block(ref, index)
        target = self.lk.peer if which == 0 else self.lk.sib
        return remote(part, part, self.send.at[k, which], self.recv.at[k, which], target)

    def first(self, ref, k):
        self.copy(ref, k, 0).start()
        self.copy(ref, k, 1).start()

    def second(self, ref, k):
        self.copy(ref, k, 0).wait_recv()
        self.copy(ref, k, 2).start()

    def last(self, ref, k):
        self.copy(ref, k, 1).wait_recv()
        self.copy(ref, k, 2).wait_recv()
        for which in range(3):
            self.copy(ref, k, which).wait_send()


class Exchange:
    def __init__(self, lk, src, dst, send, recv, in_place=False):
        self.lk, self.src, self.dst, self.send, self.recv = lk, src, dst, send, recv
        self.in_place = in_place

    def copy(self, other, step):
        lk = self.lk
        c = 1 - lk.c if other else lk.c
        target = lax.rem(lk.f + step, lk.fs) * lk.cx + c
        return remote(
            self.src(target), self.dst(lk.g), self.send.at[other, step],
            self.recv.at[other, lax.rem(lk.fs - step, lk.fs)], lk.away(step, c),
        )

    def each(self, work):
        def body(step, carry):
            work(1, step)
            work(0, step)
            return carry

        work(1, 0)
        lax.fori_loop(1, self.lk.fs, body, 0)

    def first(self):
        self.each(lambda other, step: self.copy(other, step).start())
        if not self.in_place:
            self.dst(self.lk.g)[...] = self.src(self.lk.g)[...]

    def last(self):
        def work(other, step):
            self.copy(other, lax.rem(self.lk.fs - step, self.lk.fs)).wait_recv()

        self.each(work)

    def drain(self):
        self.each(lambda other, step: self.copy(other, step).wait_send())


class Trade:
    def __init__(self, lk, src, dst, send, recv):
        self.lk, self.src, self.dst, self.send, self.recv = lk, src, dst, send, recv

    def copies(self):
        lk = self.lk
        pairs = ((lk.peer_t, lk.peer), (lk.diag_t, lk.diag), (lk.sib_t, lk.sib))
        return [
            remote(self.src(index), self.dst(lk.t), self.send.at[i], self.recv.at[i], target)
            for i, (index, target) in enumerate(pairs)
        ]

    def first(self):
        for copy in self.copies():
            copy.start()
        self.dst(self.lk.t)[...] = self.src(self.lk.t)[...]

    def last(self):
        for copy in self.copies():
            copy.wait_recv()
            copy.wait_send()


def part_of(size, index):
    return pl.ds(pl.multiple_of(index * size, size), size)


def stored_slots(dst, values, first, count, sends, block):
    for i in range(count):
        dst(i)[block * sends : (block + 1) * sends] = values[
            (first + i) * sends : (first + i + 1) * sends
        ].astype(BF)


class WeightGather:
    def __init__(self, lk, shard, full, z_send, z_recv, x_send, x_recv, own):
        self.lk, self.shard, self.full = lk, shard, full
        self.z_send, self.z_recv, self.x_send, self.x_recv = z_send, z_recv, x_send, x_recv
        self.own = own
        self.rows = shard.shape[1]

    def block(self, chunk, f, c):
        first = pl.multiple_of((f * self.lk.cx + c) * self.rows, self.rows)
        return self.full.at[chunk, pl.ds(first, self.rows)]

    def z_copy(self, chunk, step):
        return remote(
            self.shard.at[chunk], self.block(chunk, self.lk.f, self.lk.c),
            self.z_send.at[chunk, step], self.z_recv.at[chunk, self.lk.fs - step],
            self.lk.away(step),
        )

    def x_copy(self, chunk, step):
        f = lax.rem(self.lk.f + step, self.lk.fs)
        part = self.block(chunk, f, self.lk.c)
        return remote(
            part, part, self.x_send.at[chunk, step], self.x_recv.at[chunk, step], self.lk.across
        )

    def x_own(self, chunk):
        return remote(
            self.shard.at[chunk], self.block(chunk, self.lk.f, self.lk.c),
            self.x_send.at[chunk, 0], self.x_recv.at[chunk, 0], self.lk.across,
        )

    def own_copy(self, chunk):
        return pltpu.make_async_copy(
            self.shard.at[chunk], self.block(chunk, self.lk.f, self.lk.c), self.own.at[chunk]
        )

    def each(self, first, work):
        def body(step, carry):
            work(step)
            return carry

        lax.fori_loop(first, self.lk.fs, body, 0)

    def start(self, chunk):
        self.own_copy(chunk).start()
        self.x_own(chunk).start()
        self.each(1, lambda step: self.z_copy(chunk, step).start())

    def forward(self, chunk):
        def work(step):
            self.z_copy(chunk, self.lk.fs - step).wait_recv()
            self.x_copy(chunk, step).start()

        self.each(1, work)

    def finish(self, chunk):
        self.own_copy(chunk).wait()
        self.each(0, lambda step: self.x_copy(chunk, step).wait_recv())

    def drain(self, chunk):
        self.each(1, lambda step: self.z_copy(chunk, step).wait_send())
        self.each(0, lambda step: self.x_copy(chunk, step).wait_send())


def store_part(part, k, cols, values, rows):
    for block in range(4):
        part[k, block % 2, block // 2, :, cols] = values[block * rows : (block + 1) * rows].astype(
            BF
        )


def masked_scores(query, key_rows, same_seq):
    return jnp.where(
        same_seq, dot(query, key_rows, NT) * (LOG2E / math.sqrt(HD)), NEG
    )


def forward_kernel(
    tokens, time_embed, cot, pick_out, pick_in, shard, vec, head_bias, up_bias, seg_col, seg_row,
    out_w, out_act, out_qkv, out_att, out_nrm, out_std, out_hid, out_glu, out_dglu, out_lse,
    out_u, out_cot,
    w, act, qkv, att, nrm, std, hid, glu, dglu, lse, u, h, part, from_sib, to_peer, from_peer,
    slots, arrived, cot_part, cot_rows, u_low,
    out_sem, rs_send, rs_recv, ag_send, ag_recv, z_send, z_recv, x_send, x_recv, own,
    ex_send, ex_recv, tr_send, tr_recv,
):
    layers, packs, rows, width = act.shape
    sends = slots.shape[2] // packs
    local_width = slots.shape[3]
    mine = rows // 4
    heads_width = att.shape[3]
    chunks = shard.shape[0]
    lk = Links()
    lk.barrier()
    rs = RowSum(lk, part, from_sib, to_peer, from_peer, rs_send, rs_recv)
    ag = RowGather(lk, mine, ag_send, ag_recv)
    wg = WeightGather(lk, shard, w, z_send, z_recv, x_send, x_recv, own)
    pending = []

    def save(src, dst):
        copy = pltpu.make_async_copy(src, dst, out_sem.at[len(pending)])
        copy.start()
        pending.append(copy)

    my_rows = part_of(mine, lk.t)
    my_cols = part_of(local_width, lk.t)
    swaps = [
        Exchange(
            lk, lambda g, i=i: slots.at[i, g], lambda g, i=i: arrived.at[i, g],
            ex_send.at[i], ex_recv.at[i],
        )
        for i in range(2)
    ]

    def send_slots(which, values):
        for c in range(2):
            for k in range(packs):
                m = c * packs + k
                picked = dot(pick_out[m], values(m), NN)
                for f in range(picked.shape[0] // sends):
                    slots[which, 2 * f + c, k * sends : (k + 1) * sends] = picked[
                        f * sends : (f + 1) * sends
                    ].astype(BF)
        swaps[which].first()

    def placed_rows(which, k):
        blocks = [
            arrived[which, g, k * sends : (k + 1) * sends] for g in range(arrived.shape[1])
        ]
        return dot(pick_in[k], jnp.concatenate(blocks, axis=0), NN).astype(BF)

    wg.start(0)
    send_slots(0, lambda m: (tokens[m].astype(F32) + time_embed[m].astype(F32)).astype(BF))
    lse[...] = jnp.zeros_like(lse)
    first_ag = RowGather(lk, local_width, ag_send, ag_recv, by_columns=True)
    swaps[0].last()
    for k in range(packs):
        act[0, k, :, my_cols] = placed_rows(0, k)
        first_ag.first(act.at[0, k], k)
    wg.forward(0)
    wg.start(1)
    for k in range(packs):
        first_ag.second(act.at[0, k], k)
    for k in range(packs):
        first_ag.last(act.at[0, k], k)
        u[k] = act[0, k, my_rows].astype(F32)
        save(act.at[0, k], out_act.at[0, k])
    wg.finish(0)
    save(w.at[0], out_w.at[0])

    def project(layer, k):
        for j in range(3):
            cols = slice(j * heads_width, (j + 1) * heads_width)
            acc = dot(act[layer, k], w[3 * layer, :, cols], NN)
            if j != 1:
                acc = acc + head_bias[layer, j // 2 : j // 2 + 1]
            qkv[layer, k, :, cols] = acc.astype(BF)
        save(qkv.at[layer, k], out_qkv.at[layer, k])

    def attention(layer, k):
        same_seq = seg_col[k] == seg_row[k]
        for head in range(heads_width // HD):
            cols = [slice(j * heads_width + head * HD, j * heads_width + (head + 1) * HD) for j in range(3)]
            scores = masked_scores(qkv[layer, k, :, cols[0]], qkv[layer, k, :, cols[1]], same_seq)
            top = jnp.max(scores, axis=1, keepdims=True)
            weighted = jnp.exp2(scores - top)
            total = jnp.sum(weighted, axis=1, keepdims=True)
            lse[layer, k, :, head : head + 1] = top + jnp.log2(total)
            probs = (weighted * (1.0 / total)).astype(BF)
            att[layer, k, :, cols[0]] = dot(probs, qkv[layer, k, :, cols[2]], NN).astype(BF)
        save(lse.at[layer, k], out_lse.at[layer, k])
        save(att.at[layer, k], out_att.at[layer, k])
        for j in range(width // 256):
            cols = slice(j * 256, (j + 1) * 256)
            acc = dot(att[layer, k], w[3 * layer, cols, 3 * heads_width :], NT)
            store_part(part, k, cols, acc, mine)
        rs.first(k)

    def normalize(layer, which, k, resid):
        mean = jnp.mean(resid, axis=1, keepdims=True)
        centred = resid - mean
        scale = lax.rsqrt(jnp.mean(centred * centred, axis=1, keepdims=True) + EPS)
        normed = centred * scale
        nrm[layer, which, k] = normed
        std[layer, which, k] = jnp.broadcast_to(scale, std.shape[3:])
        save(nrm.at[layer, which, k], out_nrm.at[layer, which, k])
        save(std.at[layer, which, k], out_std.at[layer, which, k])
        return normed * vec[layer, 2 + which : 3 + which] + vec[layer, 4 + which : 5 + which]

    def norm_one(layer, k):
        hidden = normalize(layer, 0, k, u[k] + rs.last(k) + vec[layer, 0:1])
        h[k] = hidden
        hid[layer, k, my_rows] = hidden.astype(BF)
        ag.first(hid.at[layer, k], k)

    def expand(layer, k):
        def tile(j, carry):
            cols = pl.ds(pl.multiple_of(j * 256, 256), 256)
            acc = dot(hid[layer, k], w[3 * layer + 1, :, cols], NN) + up_bias[layer, :, cols]
            value, slope = gelu_pair(acc)
            glu[layer, k, :, cols] = value.astype(BF)
            dglu[layer, k, :, cols] = slope.astype(BF)
            return carry

        lax.fori_loop(0, width // 256, tile, 0)
        save(glu.at[layer, k], out_glu.at[layer, k])
        save(dglu.at[layer, k], out_dglu.at[layer, k])

    def contract(layer, k):
        def tile(j, carry):
            cols = pl.ds(pl.multiple_of(j * 256, 256), 256)
            acc = dot(glu[layer, k], w[3 * layer + 2, cols, :], NT)
            store_part(part, k, cols, acc, mine)
            return carry

        lax.fori_loop(0, width // 256, tile, 0)
        rs.first(k)

    def norm_two(layer, k):
        out = normalize(layer, 1, k, h[k] + rs.last(k) + vec[layer, 1:2])
        u[k] = out
        if layer + 1 < layers:
            act[layer + 1, k, my_rows] = out.astype(BF)
            ag.first(act.at[layer + 1, k], k)
        else:
            u_low[k] = out.astype(BF)
            save(u_low.at[k], out_u.at[k])

    def weights_next(chunk):
        if chunk < chunks:
            if chunk + 1 < chunks:
                wg.start(chunk + 1)
            wg.forward(chunk)

    def weights_ready(chunk):
        wg.finish(chunk)
        save(w.at[chunk], out_w.at[chunk])

    trade = Trade(
        lk, lambda t: cot_part.at[:, part_of(mine, t)],
        lambda t: cot_rows.at[:, :, part_of(local_width, t)], tr_send, tr_recv,
    )
    for layer in range(layers):
        base = 3 * layer
        more = layer + 1 < layers
        if layer:
            weights_ready(base)
            ag.last(act.at[layer, 0], 0)
            save(act.at[layer, 0], out_act.at[layer, 0])
        project(layer, 0)
        if layer:
            ag.second(act.at[layer, 1], 1)
        attention(layer, 0)
        weights_next(base + 1)
        if layer:
            ag.last(act.at[layer, 1], 1)
            save(act.at[layer, 1], out_act.at[layer, 1])
        project(layer, 1)
        rs.second(0)
        attention(layer, 1)
        norm_one(layer, 0)
        rs.second(1)
        ag.second(hid.at[layer, 0], 0)
        norm_one(layer, 1)
        weights_ready(base + 1)
        weights_next(base + 2)
        ag.last(hid.at[layer, 0], 0)
        save(hid.at[layer, 0], out_hid.at[layer, 0])
        expand(layer, 0)
        ag.second(hid.at[layer, 1], 1)
        weights_ready(base + 2)
        contract(layer, 0)
        weights_next(base + 3)
        if not more:
            send_slots(1, lambda m: cot[m])
        ag.last(hid.at[layer, 1], 1)
        save(hid.at[layer, 1], out_hid.at[layer, 1])
        expand(layer, 1)
        rs.second(0)
        contract(layer, 1)
        if not more:
            swaps[1].last()
            for k in range(packs):
                cot_part[k] = placed_rows(1, k)
            trade.first()
        norm_two(layer, 0)
        rs.second(1)
        if more:
            ag.second(act.at[layer + 1, 0], 0)
        norm_two(layer, 1)
    trade.last()
    save(cot_rows, out_cot)
    for chunk in range(chunks):
        wg.drain(chunk)
    for swap in swaps:
        swap.drain()
    for copy in pending:
        copy.wait()


def forward(
    tokens, time_embed, cot, pick_out, pick_in, shard, vec, head_bias, up_bias, seg_col, seg_row
):
    packs, rows = pick_in.shape[:2]
    width = shard.shape[2]
    local_width = tokens.shape[2]
    chunks = shard.shape[0]
    layers = chunks // 3
    mine = rows // 4
    heads = head_bias.shape[2]
    fs, cx = lax.axis_size("fsdp"), lax.axis_size("ctx")
    groups = fs * cx
    sends = tokens.shape[1] // fs
    shapes = dict(
        w=((chunks, width, width), BF),
        act=((layers, packs, rows, width), BF),
        qkv=((layers, packs, rows, 3 * heads), BF),
        att=((layers, packs, rows, heads), BF),
        nrm=((layers, 2, packs, mine, width), F32),
        std=((layers, 2, packs, mine, 128), F32),
        hid=((layers, packs, rows, width), BF),
        glu=((layers, packs, rows, width), BF),
        dglu=((layers, packs, rows, width), BF),
        lse=((layers, packs, rows, 128), F32),
        u=((packs, mine, width), F32),
    )
    outs = {name: jax.ShapeDtypeStruct(*shape) for name, shape in shapes.items()}
    outs["u"] = jax.ShapeDtypeStruct((packs, mine, width), BF)
    outs["cot"] = jax.ShapeDtypeStruct((packs, mine, width), BF)
    copies = chunks + layers * packs * 11 + packs + 1
    dma = pltpu.SemaphoreType.DMA
    whole = pl.BlockSpec(memory_space=pl.ANY)
    vmem = pl.BlockSpec(memory_space=pltpu.VMEM)
    return pl.pallas_call(
        forward_kernel,
        in_specs=[vmem] * 5 + [whole] + [vmem] * 5,
        out_specs=[whole] * len(outs),
        out_shape=list(outs.values()),
        scratch_shapes=[pltpu.VMEM(*shape) for shape in shapes.values()]
        + [
            pltpu.VMEM((packs, mine, width), F32),
            pltpu.VMEM((packs, 2, 2, mine, width), BF),
            pltpu.VMEM((packs, 2, mine, width), BF),
            pltpu.VMEM((packs, mine, width), BF),
            pltpu.VMEM((packs, mine, width), BF),
            pltpu.VMEM((2, groups, packs * sends, local_width), BF),
            pltpu.VMEM((2, groups, packs * sends, local_width), BF),
            pltpu.VMEM((packs, rows, local_width), BF),
            pltpu.VMEM((packs, mine, width), BF),
            pltpu.VMEM((packs, mine, width), BF),
            dma((copies,)),
            dma((packs, 2)), dma((packs, 2)), dma((packs, 3)), dma((packs, 3)),
            dma((chunks, fs)), dma((chunks, fs)), dma((chunks, fs)), dma((chunks, fs)),
            dma((chunks,)),
            dma((2, 2, fs)), dma((2, 2, fs)), dma((3,)), dma((3,)),
        ],
        compiler_params=pltpu.CompilerParams(
            collective_id=0, has_side_effects=True, vmem_limit_bytes=60 << 20
        ),
        name="forward",
    )(
        tokens, time_embed, cot, pick_out, pick_in, shard, vec, head_bias, up_bias, seg_col,
        seg_row,
    )


class GradScatter:
    def __init__(self, lk, grad, from_x, from_z, x_send, x_recv, z_send, z_recv):
        self.lk, self.grad, self.from_x, self.from_z = lk, grad, from_x, from_z
        self.x_send, self.x_recv, self.z_send, self.z_recv = x_send, x_recv, z_send, z_recv
        self.rows = from_x.shape[2]

    def block(self, chunk, step, c):
        f = lax.rem(self.lk.f + step, self.lk.fs)
        first = pl.multiple_of((f * self.lk.cx + c) * self.rows, self.rows)
        return self.grad.at[chunk, pl.ds(first, self.rows)]

    def x_copy(self, chunk, step):
        return remote(
            self.block(chunk, step, 1 - self.lk.c), self.from_x.at[chunk, step],
            self.x_send.at[chunk, step], self.x_recv.at[chunk, step], self.lk.across,
        )

    def z_copy(self, chunk, step):
        slot = self.lk.fs - step
        return remote(
            self.block(chunk, step, self.lk.c), self.from_z.at[chunk, slot - 1],
            self.z_send.at[chunk, step], self.z_recv.at[chunk, slot], self.lk.away(step),
        )

    def each(self, first, work):
        def body(step, carry):
            work(step)
            return carry

        lax.fori_loop(first, self.lk.fs, body, 0)

    def first(self, chunk):
        self.each(1, lambda step: self.x_copy(chunk, step).start())
        self.x_copy(chunk, 0).start()

    def second(self, chunk):
        def work(step):
            self.x_copy(chunk, step).wait_recv()
            own = self.block(chunk, step, self.lk.c)
            own[...] = (own[...].astype(F32) + self.from_x[chunk, step].astype(F32)).astype(BF)
            self.z_copy(chunk, step).start()

        self.each(1, work)

    def last(self, chunk, out):
        self.x_copy(chunk, 0).wait_recv()
        out[...] = self.block(chunk, 0, self.lk.c)[...].astype(F32) + self.from_x[chunk, 0].astype(F32)

        def work(step):
            self.z_copy(chunk, self.lk.fs - step).wait_recv()
            out[...] = out[...] + self.from_z[chunk, step - 1].astype(F32)

        self.each(1, work)

    def drain(self, chunk):
        self.each(0, lambda step: self.x_copy(chunk, step).wait_send())
        self.each(1, lambda step: self.z_copy(chunk, step).wait_send())


def backward_kernel(
    up_in, u_in, pick_out, pick_in, act_in, w_in, qkv_in, att_in, nrm_in, std_in, hid_in, glu_in, dglu_in,
    lse_in, vec, seg_col, seg_row,
    out_qkv, out_out, out_up, out_down, out_ret, out_sums,
    w, qkv, att, nrm, std, hid, glu, dglu, lse, up, gtwo, gl, gm, gup, gqkv, gatt,
    part, from_sib, to_peer, from_peer, grad, from_x, from_z, gsum, low, ret_in,
    out_vec, out_head, out_bias, vec_parts, sums,
    in_sem, out_sem, rs_send, rs_recv, ag_send, ag_recv, x_send, x_recv, z_send, z_recv,
    ex_send, ex_recv, tr_send, tr_recv, pick_sem,
):
    packs, rows, width = hid.shape
    layers = vec.shape[0]
    mine = rows // 4
    heads_width = att.shape[2]
    lk = Links()
    sources = dict(
        nrm1=lambda layer: (nrm_in.at[layer, 1], nrm.at[1]),
        std1=lambda layer: (std_in.at[layer, 1], std.at[1]),
        nrm0=lambda layer: (nrm_in.at[layer, 0], nrm.at[0]),
        std0=lambda layer: (std_in.at[layer, 0], std.at[0]),
        w2=lambda layer: (w_in.at[3 * layer + 2], w.at[2]),
        dglu=lambda layer: (dglu_in.at[layer], dglu),
        w1=lambda layer: (w_in.at[3 * layer + 1], w.at[1]),
        glu=lambda layer: (glu_in.at[layer], glu),
        hid=lambda layer: (hid_in.at[layer], hid),
        w0=lambda layer: (w_in.at[3 * layer], w.at[0]),
        qkv=lambda layer: (qkv_in.at[layer], qkv),
        lse=lambda layer: (lse_in.at[layer], lse),
        att=lambda layer: (att_in.at[layer], att),
        act=lambda layer: (act_in.at[layer], hid),
    )
    order = {name: index for index, name in enumerate(sources)}

    def fetch(name, layer):
        if layer >= 0:
            src, dst = sources[name](layer)
            pltpu.make_async_copy(src, dst, in_sem.at[order[name]]).start()

    def ready(name, layer):
        src, dst = sources[name](layer)
        pltpu.make_async_copy(src, dst, in_sem.at[order[name]]).wait()

    loads = [
        pltpu.make_async_copy(up_in, to_peer, in_sem.at[len(order)]),
        pltpu.make_async_copy(u_in, low, in_sem.at[len(order) + 1]),
    ]
    for load in loads:
        load.start()
    for name in sources:
        if name != "act":
            fetch(name, layers - 1)
    lk.barrier()
    rs = RowSum(lk, part, from_sib, to_peer, from_peer, rs_send, rs_recv)
    ag = RowGather(lk, mine, ag_send, ag_recv)
    gs = GradScatter(lk, grad, from_x, from_z, x_send, x_recv, z_send, z_recv)
    my_rows = pl.ds(pl.multiple_of(lk.t * mine, mine), mine)
    pending = []
    held = {}
    local_width = ret_in.shape[1]
    swap_rows = width // (lk.fs * lk.cx)
    sends = swap_rows // packs
    low_cols, next_cols, third_cols, last_cols = (
        slice(i * local_width, (i + 1) * local_width) for i in range(4)
    )

    class Return:
        def __init__(self, index, first, second, landed):
            self.index, self.first_buf, self.second_buf, self.landed = index, first, second, landed
            self.trade = Trade(
                lk, lambda t: low.at[:, :, part_of(local_width, t)],
                lambda t: gup.at[:, part_of(mine, t), low_cols],
                tr_send.at[index], tr_recv.at[index],
            )
            self.swap = Exchange(
                lk, lambda g: first.at[part_of(swap_rows, g), low_cols],
                lambda g: landed.at[part_of(swap_rows, g)], ex_send.at[index], ex_recv.at[index],
            )
            self.picks = [
                pltpu.make_async_copy(
                    pick_in, second.at[:, : 2 * local_width], pick_sem.at[index, 0]
                ),
                pltpu.make_async_copy(pick_out, second.at[:, third_cols], pick_sem.at[index, 1]),
            ]

        def load(self):
            for copy in self.picks:
                copy.start()

        def middle(self):
            self.trade.last()
            self.picks[0].wait()
            for k in range(packs):
                pick = self.second_buf[k * rows : (k + 1) * rows, : 2 * local_width]
                values = dot(pick, gup[k, :, low_cols], TN).astype(BF)
                for g in range(rows // sends):
                    first = g * swap_rows + k * sends
                    self.first_buf[first : first + sends, low_cols] = values[
                        g * sends : (g + 1) * sends
                    ]
            self.swap.first()

        def last(self):
            self.swap.last()
            self.picks[1].wait()
            given = pick_out.shape[1]
            for c in range(2):
                for k in range(packs):
                    m = c * packs + k
                    blocks = [
                        self.landed[
                            (2 * f + c) * swap_rows + k * sends :
                            (2 * f + c) * swap_rows + (k + 1) * sends
                        ]
                        for f in range(given // sends)
                    ]
                    pick = self.second_buf[m * given : (m + 1) * given, third_cols]
                    values = dot(pick, jnp.concatenate(blocks, axis=0), TN)
                    self.second_buf[m * given : (m + 1) * given, last_cols] = values.astype(BF)
            save(self.second_buf.at[:, last_cols], out_ret.at[self.index])
            self.saved = pending.pop()

        def finish(self):
            self.swap.drain()
            self.saved.wait()

    give_back = [
        Return(0, grad.at[0], grad.at[1], grad.at[0, :, next_cols]),
        Return(1, grad.at[3 * layers - 1], grad.at[3 * layers - 2], ret_in),
    ]
    vec_trade = Trade(
        lk, lambda t: out_vec.at[:, :, part_of(local_width, t)], lambda t: vec_parts.at[t],
        tr_send.at[2], tr_recv.at[2],
    )
    vec_swap = Exchange(
        lk, lambda g: sums.at[lk.g], lambda g: sums.at[g], ex_send.at[2], ex_recv.at[2],
        in_place=True,
    )

    def vec_middle():
        vec_trade.last()
        total = vec_parts[0]
        for t in range(1, 4):
            total = total + vec_parts[t]
        sums[lk.g, :, 0:6] = total
        sums[lk.g, :, 6:8] = out_head[...]
        for j in range(4):
            sums[lk.g, :, 8 + j : 9 + j] = out_bias[:, :, j * local_width : (j + 1) * local_width]
        vec_swap.first()

    def vec_last():
        vec_swap.last()

        def add(g, total):
            return total + sums[g]

        out_sums[...] = lax.fori_loop(1, sums.shape[0], add, sums[0])

    used = []

    def save(src, dst):
        copy = pltpu.make_async_copy(src, dst, out_sem.at[len(used)])
        copy.start()
        used.append(1)
        pending.append(copy)

    out_vec[...] = jnp.zeros_like(out_vec)
    out_head[...] = jnp.zeros_like(out_head)
    out_bias[...] = jnp.zeros_like(out_bias)

    def norm_back(layer, which, k, upstream):
        normed = nrm[which, k]
        scale = std[which, k][:, 0:1]
        out_vec[layer, 2 + which : 3 + which] += jnp.sum(upstream * normed, axis=0, keepdims=True)
        out_vec[layer, 4 + which : 5 + which] += jnp.sum(upstream, axis=0, keepdims=True)
        scaled = upstream * vec[layer, 2 + which : 3 + which]
        first = jnp.mean(scaled, axis=1, keepdims=True)
        second = jnp.mean(scaled * normed, axis=1, keepdims=True)
        result = scale * (scaled - first - normed * second)
        out_vec[layer, which : which + 1] += jnp.sum(result, axis=0, keepdims=True)
        return result

    def norm_two(layer, k):
        result = norm_back(layer, 1, k, up[k])
        gtwo[k] = result
        gl[k, my_rows] = result.astype(BF)
        ag.first(gl.at[k], k)

    def norm_one(layer, k):
        result = norm_back(layer, 0, k, gtwo[k] + rs.last(k))
        up[k] = result
        gm[k, my_rows] = result.astype(BF)
        ag.first(gm.at[k], k)

    def tiles(work):
        def body(j, carry):
            work(pl.ds(pl.multiple_of(j * 256, 256), 256))
            return carry

        lax.fori_loop(0, width // 256, body, 0)

    def through_down(layer, k):
        def tile(cols):
            grad_gelu = dot(gl[k], w[2, :, cols], NN).astype(BF).astype(F32)
            result = (grad_gelu * dglu[k, :, cols].astype(F32)).astype(BF)
            gup[k, :, cols] = result
            out_bias[layer, :, cols] += jnp.sum(result.astype(F32), axis=0, keepdims=True)

        tiles(tile)

    def through_up(layer, k):
        tiles(lambda cols: store_part(part, k, cols, dot(gup[k], w[1, cols, :], NT), mine))
        rs.first(k)

    def through_out(k):
        gatt[k] = dot(gm[k], w[0, :, 3 * heads_width :], NN).astype(BF)

    def attention(layer, k):
        same_seq = seg_col[k] == seg_row[k]
        scale = 1.0 / math.sqrt(HD)
        for head in range(heads_width // HD):
            cols = [slice(j * heads_width + head * HD, j * heads_width + (head + 1) * HD) for j in range(3)]
            query, keys, values = (qkv[k, :, c] for c in cols)
            grads = gatt[k, :, cols[0]]
            probs = jnp.exp2(masked_scores(query, keys, same_seq) - lse[k, :, head : head + 1])
            grad_probs = dot(grads, values, NT)
            delta = jnp.sum(probs * grad_probs, axis=1, keepdims=True)
            grad_scores = (probs * (grad_probs - delta)).astype(BF)
            gqkv[k, :, cols[0]] = (dot(grad_scores, keys, NN) * scale).astype(BF)
            gqkv[k, :, cols[1]] = (dot(grad_scores, query, TN) * scale).astype(BF)
            gqkv[k, :, cols[2]] = dot(probs.astype(BF), grads, TN).astype(BF)
        for j in range(2):
            cols = slice(2 * j * heads_width, (2 * j + 1) * heads_width)
            out_head[layer, j : j + 1] += jnp.sum(
                gqkv[k, :, cols].astype(F32), axis=0, keepdims=True
            )

    def through_qkv(k):
        tiles(
            lambda cols: store_part(
                part, k, cols, dot(gqkv[k], w[0, cols, : 3 * heads_width], NT), mine
            )
        )
        rs.first(k)

    def product(left, right, cols, right_cols=slice(None)):
        total = dot(left[0, :, cols], right[0, :, right_cols], TN)
        for k in range(1, packs):
            total = total + dot(left[k, :, cols], right[k, :, right_cols], TN)
        return total.astype(BF)

    def down_grad(layer):
        def tile(cols):
            grad[3 * layer + 2, cols, :] = product(gl, glu, cols)

        tiles(tile)
        gs.first(3 * layer + 2)

    def up_grad(layer):
        def tile(cols):
            grad[3 * layer + 1, cols, :] = product(hid, gup, cols)

        tiles(tile)
        gs.first(3 * layer + 1)

    def first_grad(layer):
        def tile(cols):
            grad[3 * layer, cols, : 3 * heads_width] = product(hid, gqkv, cols)
            grad[3 * layer, cols, 3 * heads_width :] = product(gm, att, cols)

        tiles(tile)
        gs.first(3 * layer)

    def emit(layer, which):
        chunk = 3 * layer + which
        out = gsum.at[which]
        while held.get(which):
            held[which].pop().wait()
        gs.last(chunk, out)
        held[which] = []
        saved = len(pending)
        if which == 2:
            save(out, out_down.at[layer])
        elif which == 1:
            save(out, out_up.at[layer])
        else:
            for c in range(3):
                save(out.at[:, c * heads_width : (c + 1) * heads_width], out_qkv.at[layer, c])
            save(out.at[:, 3 * heads_width :], out_out.at[layer])
        held[which] = [pending.pop() for _ in range(len(pending) - saved)]

    give_back[0].load()
    for load in loads:
        load.wait()
    top = layers - 1
    ready("nrm1", top)
    ready("std1", top)
    for k in range(packs):
        up[k] = to_peer[k].astype(F32)
        norm_two(top, k)
    give_back[0].trade.first()
    fetch("nrm1", top - 1)
    fetch("std1", top - 1)
    for layer in reversed(range(layers)):
        ag.second(gl.at[0], 0)
        if layer < top:
            ready("act", layer + 1)
            first_grad(layer + 1)
            fetch("att", layer)
            fetch("hid", layer)
        else:
            give_back[0].middle()
        ready("w2", layer)
        ready("dglu", layer)
        ag.last(gl.at[0], 0)
        through_down(layer, 0)
        ag.second(gl.at[1], 1)
        ready("w1", layer)
        through_up(layer, 0)
        ag.last(gl.at[1], 1)
        through_down(layer, 1)
        fetch("w2", layer - 1)
        fetch("dglu", layer - 1)
        rs.second(0)
        through_up(layer, 1)
        fetch("w1", layer - 1)
        ready("glu", layer)
        down_grad(layer)
        fetch("glu", layer - 1)
        rs.second(1)
        ready("nrm0", layer)
        ready("std0", layer)
        norm_one(layer, 0)
        if layer < top:
            gs.second(3 * (layer + 1) + 1)
        ready("hid", layer)
        up_grad(layer)
        fetch("act", layer)
        ag.second(gm.at[0], 0)
        norm_one(layer, 1)
        fetch("nrm0", layer - 1)
        fetch("std0", layer - 1)
        ready("w0", layer)
        ready("qkv", layer)
        ready("lse", layer)
        ag.last(gm.at[0], 0)
        through_out(0)
        attention(layer, 0)
        ag.second(gm.at[1], 1)
        through_qkv(0)
        if layer < top:
            gs.second(3 * (layer + 1))
        else:
            gs.second(3 * layer + 2)
        ag.last(gm.at[1], 1)
        through_out(1)
        rs.second(0)
        attention(layer, 1)
        fetch("qkv", layer - 1)
        fetch("lse", layer - 1)
        through_qkv(1)
        fetch("w0", layer - 1)
        ready("att", layer)
        if layer == 0:
            ready("act", layer)
            first_grad(0)
        for k in range(packs):
            if k:
                rs.second(k)
            up[k] = rs.last(k) + up[k]
            if layer:
                if k == 0:
                    ready("nrm1", layer - 1)
                    ready("std1", layer - 1)
                norm_two(layer - 1, k)
            else:
                low[k] = up[k].astype(BF)
        if layer == top:
            give_back[0].last()
            give_back[0].finish()
        if layer:
            fetch("nrm1", layer - 2)
            fetch("std1", layer - 2)
        if layer < top:
            for which in (2, 1, 0):
                emit(layer + 1, which)
    for chunk in (3 * layers - 1, 3 * layers - 2):
        gs.drain(chunk)
    give_back[1].load()
    give_back[1].trade.first()
    vec_trade.first()
    gs.second(2)
    give_back[1].middle()
    vec_middle()
    gs.second(1)
    emit(0, 2)
    gs.second(0)
    give_back[1].last()
    vec_last()
    emit(0, 1)
    emit(0, 0)
    for chunk in range(3 * layers - 2):
        gs.drain(chunk)
    give_back[1].finish()
    vec_swap.drain()
    for copy in pending + sum(held.values(), []):
        copy.wait()


def backward(upstream, u, pick_out, pick_in, saved, vec, seg_col, seg_row):
    full_w, o_act, o_qkv, o_att, o_nrm, o_std, o_hid, o_glu, o_dglu, o_lse = saved
    layers, packs, rows, width = o_act.shape
    mine = rows // 4
    chunks = 3 * layers
    heads = o_att.shape[3]
    local_width = width // 4
    fs, cx = lax.axis_size("fsdp"), lax.axis_size("ctx")
    groups = fs * cx
    shard = width // groups
    given = pick_out.shape[0]
    outs = [
        jax.ShapeDtypeStruct((layers, 3, shard, heads), F32),
        jax.ShapeDtypeStruct((layers, shard, heads), F32),
        jax.ShapeDtypeStruct((layers, shard, width), F32),
        jax.ShapeDtypeStruct((layers, shard, width), F32),
        jax.ShapeDtypeStruct((2, given, local_width), BF),
        jax.ShapeDtypeStruct((layers, 12, local_width), F32),
    ]
    dma = pltpu.SemaphoreType.DMA
    whole = pl.BlockSpec(memory_space=pl.ANY)
    vmem = pl.BlockSpec(memory_space=pltpu.VMEM)
    full = pltpu.VMEM((packs, rows, width), BF)
    rowed = pltpu.VMEM((packs, mine, width), F32)
    return pl.pallas_call(
        backward_kernel,
        in_specs=[whole] * 14 + [vmem] * 3,
        out_specs=[whole] * 5 + [vmem],
        out_shape=outs,
        scratch_shapes=[
            pltpu.VMEM((3, width, width), BF),
            pltpu.VMEM((packs, rows, 3 * heads), BF),
            pltpu.VMEM((packs, rows, heads), BF),
            pltpu.VMEM((2, packs, mine, width), F32),
            pltpu.VMEM((2, packs, mine, 128), F32),
            full, full, full,
            pltpu.VMEM((packs, rows, 128), F32),
            rowed, rowed,
            full, full, full,
            pltpu.VMEM((packs, rows, 3 * heads), BF),
            pltpu.VMEM((packs, rows, heads), BF),
            pltpu.VMEM((packs, 2, 2, mine, width), BF),
            pltpu.VMEM((packs, 2, mine, width), BF),
            pltpu.VMEM((packs, mine, width), BF),
            pltpu.VMEM((packs, mine, width), BF),
            pltpu.VMEM((chunks, width, width), BF),
            pltpu.VMEM((chunks, fs, shard, width), BF),
            pltpu.VMEM((chunks, fs - 1, shard, width), BF),
            pltpu.VMEM((3, shard, width), F32),
            pltpu.VMEM((packs, mine, width), BF),
            pltpu.VMEM((given, local_width), BF),
            pltpu.VMEM((layers, 6, width), F32),
            pltpu.VMEM((layers, 2, heads), F32),
            pltpu.VMEM((layers, 1, width), F32),
            pltpu.VMEM((4, layers, 6, local_width), F32),
            pltpu.VMEM((groups, layers, 12, local_width), F32),
            dma((16,)), dma((packs + 6 * layers + 2,)),
            dma((packs, 2)), dma((packs, 2)), dma((packs, 3)), dma((packs, 3)),
            dma((chunks, fs)), dma((chunks, fs)), dma((chunks, fs)), dma((chunks, fs)),
            dma((3, 2, fs)), dma((3, 2, fs)), dma((3, 3)), dma((3, 3)), dma((2, 2)),
        ],
        compiler_params=pltpu.CompilerParams(
            collective_id=1, has_side_effects=True, vmem_limit_bytes=62 << 20
        ),
        name="backward",
    )(
        upstream, u, pick_out, pick_in, o_act, full_w, o_qkv, o_att, o_nrm, o_std, o_hid,
        o_glu, o_dglu, o_lse, vec, seg_col, seg_row,
    )


def local(
    tokens, time_embed, cotangent, segment_ids, to_owner, from_owner,
    w_qkv, w_out, w_up, w_down, biases, norm_gain, norm_bias, up_bias,
):
    micro, rows, width = tokens.shape
    layers = w_qkv.shape[0]
    fs, cx = lax.axis_size("fsdp"), lax.axis_size("ctx")
    mine = micro // cx
    pack = segment_ids.shape[1]
    sends = rows // fs
    my_first = lax.axis_index("ctx") * mine

    shard = jnp.concatenate(
        [w_qkv[:, 0], w_qkv[:, 1], w_qkv[:, 2], w_out, w_up, w_down], axis=2
    )
    shard = shard.reshape(layers, shard.shape[1], 3, -1).transpose(0, 2, 1, 3)
    shard = shard.reshape(layers * 3, shard.shape[2], -1)
    vec = jnp.concatenate([biases[:, 2:], norm_gain, norm_bias], axis=1)
    vec = lax.all_gather(vec, "tp", axis=2, tiled=True)

    to_pack = to_owner // pack
    earlier = jnp.arange(rows)[None, :] < jnp.arange(rows)[:, None]
    rank = jnp.sum((to_pack[:, :, None] == to_pack[:, None, :]) & earlier[None], axis=2)
    out_slot = to_pack * sends + rank
    pick_out = (jnp.arange(rows)[None, :, None] == out_slot[:, None, :]).astype(BF)
    given = lax.all_gather(from_owner, "ctx", axis=1, tiled=True)
    given = lax.dynamic_slice_in_dim(given, my_first, mine)
    source = given // rows
    before = (given[:, None, :] < given[:, :, None]) & (
        given[:, None, :] >= (source * rows)[:, :, None]
    )
    in_slot = source * sends + jnp.sum(before, axis=2)
    pick_in = (jnp.arange(pack)[None, None, :] == in_slot[:, :, None]).astype(BF)

    seg = lax.dynamic_slice_in_dim(segment_ids, my_first, mine)
    seg_col, seg_row = seg[:, :, None], seg[:, None, :]

    *saved, u, upstream = forward(
        tokens, time_embed, cotangent, pick_out, pick_in, shard, vec, biases[:, :2],
        up_bias[:, None], seg_col, seg_row,
    )
    g_qkv, g_out, g_up, g_down, returned, sums = backward(
        upstream, u, pick_out.reshape(micro * rows, rows), pick_in.reshape(mine * pack, pack),
        saved, vec, seg_col, seg_row,
    )
    returned = returned.reshape(2, micro, rows, width).astype(F32)
    return (
        returned[0],
        returned[1],
        g_qkv, g_out, g_up, g_down,
        jnp.concatenate([sums[:, 6:8], sums[:, 0:2]], axis=1),
        sums[:, 2:4],
        sums[:, 4:6],
        sums[:, 8:12].reshape(layers, -1),
    )


def solution(mesh):
    wide = P(None, GRP, "tp")
    vec = P(None, None, "tp")
    qkv = P(None, None, GRP, "tp")
    owner = P(None, GRP)
    return jax.shard_map(
        local,
        mesh=mesh,
        in_specs=(
            wide, wide, wide, P(None, "fsdp"), owner, owner, qkv, wide, wide, wide,
            vec, vec, vec, P(None, "tp"),
        ),
        out_specs=(wide, wide, qkv, wide, wide, wide, vec, vec, vec, P(None, "tp")),
        check_vma=False,
    )
```

```python
import math

import jax
import jax.numpy as jnp
from jax import lax
from jax.experimental import pallas as pl
from jax.experimental.pallas import tpu as pltpu
from jax.sharding import PartitionSpec as P

HD = 64
NEG = -1e30
EPS = 1e-05
BF = jnp.bfloat16
F32 = jnp.float32
GRP = ("fsdp", "ctx")


def dot(left, right, dims):
    return lax.dot_general(left, right, (dims, ((), ())), preferred_element_type=F32)


NN = ((1,), (0,))
NT = ((1,), (1,))
TN = ((0,), (0,))

MESH = pl.DeviceIdType.MESH
LOG2E = 1.4426950408889634
HALVES = 1


def gelu_pair(values):
    bell = jnp.exp2(values * values * (-0.5 * LOG2E))
    t = 1.0 / (1.0 + (0.3275911 * math.sqrt(0.5)) * jnp.abs(values))
    poly = t * (
        0.127414796 + t * (-0.142248368 + t * (0.7107068705 + t * (-0.7265760135 + t * 0.5307027145)))
    )
    tail = poly * bell
    phi = jnp.where(values < 0, tail, 1.0 - tail)
    return values * phi, phi + values * bell * (1.0 / math.sqrt(2.0 * math.pi))


class Links:
    def __init__(self):
        self.fs, self.cx = lax.axis_size("fsdp"), lax.axis_size("ctx")
        self.f, self.c, self.t = (lax.axis_index(a) for a in ("fsdp", "ctx", "tp"))
        self.core, self.chip = lax.rem(self.t, 2), self.t // 2
        self.sib_t = self.t + 1 - 2 * self.core
        self.peer_t = lax.rem(self.t + 2, 4)
        self.sib = (self.f, self.c, self.sib_t)
        self.peer = (self.f, self.c, self.peer_t)
        self.diag_t = 3 - self.t
        self.diag = (self.f, self.c, self.diag_t)
        self.across = (self.f, 1 - self.c, self.t)
        self.g = self.f * self.cx + self.c

    def away(self, step, c=None):
        return (lax.rem(self.f + step, self.fs), self.c if c is None else c, self.t)

    def barrier(self):
        sem = pltpu.get_barrier_semaphore()
        for target in (self.sib, self.peer, self.diag, self.across):
            pl.semaphore_signal(sem, inc=1, device_id=target, device_id_type=MESH)

        def greet(step, carry):
            for c in (self.c, 1 - self.c):
                pl.semaphore_signal(
                    sem, inc=1, device_id=self.away(step, c), device_id_type=MESH
                )
            return carry

        lax.fori_loop(1, self.fs, greet, 0)
        pl.semaphore_wait(sem, 2 + 2 * self.fs)


def remote(src, dst, send, recv, target):
    return pltpu.make_async_remote_copy(
        src_ref=src, dst_ref=dst, send_sem=send, recv_sem=recv,
        device_id=target, device_id_type=MESH,
    )


class RowSum:
    def __init__(self, lk, part, from_sib, to_peer, from_peer, send, recv):
        self.lk, self.part, self.from_sib = lk, part, from_sib
        self.to_peer, self.from_peer, self.send, self.recv = to_peer, from_peer, send, recv

    def sib_copy(self, k):
        return remote(
            self.part.at[k, 1 - self.lk.core], self.from_sib.at[k],
            self.send.at[k, 0], self.recv.at[k, 0], self.lk.sib,
        )

    def peer_copy(self, k):
        return remote(
            self.to_peer.at[k], self.from_peer.at[k],
            self.send.at[k, 1], self.recv.at[k, 1], self.lk.peer,
        )

    def first(self, k):
        self.sib_copy(k).start()

    def second(self, k):
        self.sib_copy(k).wait_recv()
        other = 1 - self.lk.chip
        total = self.part[k, self.lk.core, other].astype(F32) + self.from_sib[k, other].astype(F32)
        self.to_peer[k] = total.astype(BF)
        self.peer_copy(k).start()

    def last(self, k):
        own = self.part[k, self.lk.core, self.lk.chip].astype(F32)
        own = own + self.from_sib[k, self.lk.chip].astype(F32)
        self.peer_copy(k).wait_recv()
        self.sib_copy(k).wait_send()
        self.peer_copy(k).wait_send()
        return own + self.from_peer[k].astype(F32)


class RowGather:
    def __init__(self, lk, rows, send, recv, by_columns=False):
        self.lk, self.rows, self.send, self.recv = lk, rows, send, recv
        self.by_columns = by_columns

    def block(self, ref, index):
        part = part_of(self.rows, index)
        return ref.at[:, part] if self.by_columns else ref.at[part]

    def copy(self, ref, k, which):
        index = self.lk.t if which < 2 else self.lk.peer_t
        part = self.block(ref, index)
        target = self.lk.peer if which == 0 else self.lk.sib
        return remote(part, part, self.send.at[k, which], self.recv.at[k, which], target)

    def first(self, ref, k):
        self.copy(ref, k, 0).start()
        self.copy(ref, k, 1).start()

    def second(self, ref, k):
        self.copy(ref, k, 0).wait_recv()
        self.copy(ref, k, 2).start()

    def last(self, ref, k):
        self.copy(ref, k, 1).wait_recv()
        self.copy(ref, k, 2).wait_recv()
        for which in range(3):
            self.copy(ref, k, which).wait_send()


class Exchange:
    def __init__(self, lk, src, dst, send, recv, in_place=False):
        self.lk, self.src, self.dst, self.send, self.recv = lk, src, dst, send, recv
        self.in_place = in_place

    def copy(self, other, step):
        lk = self.lk
        c = 1 - lk.c if other else lk.c
        target = lax.rem(lk.f + step, lk.fs) * lk.cx + c
        return remote(
            self.src(target), self.dst(lk.g), self.send.at[other, step],
            self.recv.at[other, lax.rem(lk.fs - step, lk.fs)], lk.away(step, c),
        )

    def each(self, work):
        def body(step, carry):
            work(1, step)
            work(0, step)
            return carry

        work(1, 0)
        lax.fori_loop(1, self.lk.fs, body, 0)

    def first(self):
        self.each(lambda other, step: self.copy(other, step).start())
        if not self.in_place:
            self.dst(self.lk.g)[...] = self.src(self.lk.g)[...]

    def last(self):
        def work(other, step):
            self.copy(other, lax.rem(self.lk.fs - step, self.lk.fs)).wait_recv()

        self.each(work)

    def drain(self):
        self.each(lambda other, step: self.copy(other, step).wait_send())


class Trade:
    def __init__(self, lk, src, dst, send, recv):
        self.lk, self.src, self.dst, self.send, self.recv = lk, src, dst, send, recv

    def copies(self):
        lk = self.lk
        pairs = ((lk.peer_t, lk.peer), (lk.diag_t, lk.diag), (lk.sib_t, lk.sib))
        return [
            remote(self.src(index), self.dst(lk.t), self.send.at[i], self.recv.at[i], target)
            for i, (index, target) in enumerate(pairs)
        ]

    def first(self):
        for copy in self.copies():
            copy.start()
        self.dst(self.lk.t)[...] = self.src(self.lk.t)[...]

    def last(self):
        for copy in self.copies():
            copy.wait_recv()
            copy.wait_send()


def third(count, part):
    return 1 + (count - 1) * part // 3, 1 + (count - 1) * (part + 1) // 3


def part_of(size, index):
    return pl.ds(pl.multiple_of(index * size, size), size)


def stored_slots(dst, values, first, count, sends, block):
    for i in range(count):
        dst(i)[block * sends : (block + 1) * sends] = values[
            (first + i) * sends : (first + i + 1) * sends
        ].astype(BF)


def one_hot(rows, values):
    return (lax.broadcasted_iota(jnp.int32, (rows, values.shape[1]), 0) == values).astype(BF)


def counts_before(present):
    size = present.shape[1]
    earlier = lax.broadcasted_iota(jnp.int32, (size, size), 0) < lax.broadcasted_iota(
        jnp.int32, (size, size), 1
    )
    return dot(present, earlier.astype(BF), NN)


def leaving_slots(to_row, packs_total, pack, sends):
    groups = one_hot(packs_total, to_row // pack)
    base = lax.broadcasted_iota(jnp.int32, groups.shape, 0) * sends
    slot = (counts_before(groups) + base.astype(F32)) * groups.astype(F32)
    return one_hot(to_row.shape[1], jnp.sum(slot, axis=0, keepdims=True).astype(jnp.int32))


def coming_slots(given, groups, rows, sends):
    source = one_hot(groups, given // rows)
    within = one_hot(rows, lax.rem(given, rows))
    ranks = counts_before(dot(source, within, NT).astype(BF)).astype(BF)
    base = lax.broadcasted_iota(jnp.int32, source.shape, 0) * sends
    slot = (dot(ranks, within, NN) + base.astype(F32)) * source.astype(F32)
    return one_hot(groups * sends, jnp.sum(slot, axis=0, keepdims=True).astype(jnp.int32))


def same_sequence(seg_ref, row):
    member = one_hot(8, lax.rem(seg_ref[pl.ds(row, 1)], 8))
    return dot(member, member, TN) > 0.5


class WeightGather:
    def __init__(self, lk, shard, full, z_send, z_recv, x_send, x_recv, own):
        self.lk, self.shard, self.full = lk, shard, full
        self.z_send, self.z_recv, self.x_send, self.x_recv = z_send, z_recv, x_send, x_recv
        self.own = own
        self.rows = shard.shape[1]
        self.cols = shard.shape[2] // HALVES

    def part(self, chunk):
        return slice(chunk % HALVES * self.cols, (chunk % HALVES + 1) * self.cols)

    def mine(self, chunk):
        return self.shard.at[chunk // HALVES, :, self.part(chunk)]

    def block(self, chunk, f, c):
        rows = part_of(self.rows, f * self.lk.cx + c)
        return self.full.at[chunk // HALVES, rows, self.part(chunk)]

    def z_copy(self, chunk, step):
        return remote(
            self.mine(chunk), self.block(chunk, self.lk.f, self.lk.c),
            self.z_send.at[chunk, step], self.z_recv.at[chunk, self.lk.fs - step],
            self.lk.away(step),
        )

    def x_copy(self, chunk, step):
        f = lax.rem(self.lk.f + step, self.lk.fs)
        part = self.block(chunk, f, self.lk.c)
        return remote(
            part, part, self.x_send.at[chunk, step], self.x_recv.at[chunk, step], self.lk.across
        )

    def x_own(self, chunk):
        return remote(
            self.mine(chunk), self.block(chunk, self.lk.f, self.lk.c),
            self.x_send.at[chunk, 0], self.x_recv.at[chunk, 0], self.lk.across,
        )

    def own_copy(self, chunk):
        return pltpu.make_async_copy(
            self.mine(chunk), self.block(chunk, self.lk.f, self.lk.c), self.own.at[chunk]
        )

    def each(self, first, work):
        def body(step, carry):
            work(step)
            return carry

        lax.fori_loop(first, self.lk.fs, body, 0)

    def start(self, chunk):
        self.own_copy(chunk).start()
        self.x_own(chunk).start()
        self.each(1, lambda step: self.z_copy(chunk, step).start())

    def forward(self, chunk):
        def work(step):
            self.z_copy(chunk, self.lk.fs - step).wait_recv()
            self.x_copy(chunk, step).start()

        self.each(1, work)

    def finish(self, chunk):
        self.own_copy(chunk).wait()
        self.each(0, lambda step: self.x_copy(chunk, step).wait_recv())

    def drain(self, chunk):
        self.each(1, lambda step: self.z_copy(chunk, step).wait_send())
        self.each(0, lambda step: self.x_copy(chunk, step).wait_send())


def store_part(part, k, cols, values, rows):
    for block in range(4):
        part[k, block % 2, block // 2, :, cols] = values[block * rows : (block + 1) * rows].astype(
            BF
        )


def masked_scores(query, key_rows, same_seq):
    return jnp.where(
        same_seq, dot(query, key_rows, NT) * (LOG2E / math.sqrt(HD)), NEG
    )


def forward_kernel(
    tokens, time_embed, cot, to_owner, from_owner, seg, shard, biases, gain, offset, up_bias,
    out_w, out_act, out_qkv, out_att, out_nrm, out_std, out_hid, out_glu, out_dglu, out_lse,
    out_u, out_cot, out_gain, out_pick_out, out_pick_in,
    w, act, qkv, att, nrm, std, hid, glu, dglu, lse, u, h, part, from_sib, to_peer, from_peer,
    slots, arrived, cot_part, cot_rows, u_low,
    bias_full, gain_full, offset_full, pick_out, pick_in, given,
    out_sem, rs_send, rs_recv, ag_send, ag_recv, z_send, z_recv, x_send, x_recv, own,
    ex_send, ex_recv, tr_send, tr_recv, given_sem,
):
    layers, packs, rows, width = act.shape
    sends = slots.shape[2] // packs
    local_width = slots.shape[3]
    mine = rows // 4
    heads_width = att.shape[3]
    chunks = shard.shape[0]
    lk = Links()
    lk.barrier()
    rs = RowSum(lk, part, from_sib, to_peer, from_peer, rs_send, rs_recv)
    ag = RowGather(lk, mine, ag_send, ag_recv)
    wg = WeightGather(lk, shard, w, z_send, z_recv, x_send, x_recv, own)
    pending = []

    def save(src, dst):
        copy = pltpu.make_async_copy(src, dst, out_sem.at[len(pending)])
        copy.start()
        pending.append(copy)

    my_rows = part_of(mine, lk.t)
    my_cols = part_of(local_width, lk.t)
    swaps = [
        Exchange(
            lk, lambda g, i=i: slots.at[i, g], lambda g, i=i: arrived.at[i, g],
            ex_send.at[i], ex_recv.at[i],
        )
        for i in range(2)
    ]

    def send_slots(which, values):
        for c in range(2):
            for k in range(packs):
                m = c * packs + k
                picked = dot(pick_out[m * held : (m + 1) * held], values(m), NN)
                for f in range(picked.shape[0] // sends):
                    slots[which, 2 * f + c, k * sends : (k + 1) * sends] = picked[
                        f * sends : (f + 1) * sends
                    ].astype(BF)
        swaps[which].first()

    def placed_rows(which, k):
        blocks = [
            arrived[which, g, k * sends : (k + 1) * sends] for g in range(arrived.shape[1])
        ]
        return dot(
            pick_in[k * rows : (k + 1) * rows], jnp.concatenate(blocks, axis=0), TN
        ).astype(BF)

    def weights_next(chunk):
        if chunk < chunks:
            for part in range(chunk * HALVES, (chunk + 1) * HALVES):
                if part + HALVES < chunks * HALVES:
                    wg.start(part + HALVES)
                wg.forward(part)

    def weights_ready(chunk):
        for part in range(chunk * HALVES, (chunk + 1) * HALVES):
            wg.finish(part)
        save(w.at[chunk], out_w.at[chunk])

    for half in range(HALVES):
        wg.start(half)
    give = remote(
        from_owner, given.at[lk.c], given_sem.at[0], given_sem.at[1], lk.across
    )
    give.start()
    params = [
        Trade(
            lk, lambda t, src=src: src, lambda t, full=full: full.at[:, :, part_of(local_width, t)],
            tr_send.at[1 + i], tr_recv.at[1 + i],
        )
        for i, (src, full) in enumerate(
            ((biases, bias_full), (gain, gain_full), (offset, offset_full))
        )
    ]
    for param in params:
        param.first()
    held = tokens.shape[1]
    for m in range(tokens.shape[0]):
        pick_out[m * held : (m + 1) * held] = leaving_slots(
            to_owner[m : m + 1], held // sends, rows, sends
        )
    send_slots(0, lambda m: (tokens[m].astype(F32) + time_embed[m].astype(F32)).astype(BF))
    lse[...] = jnp.zeros_like(lse)
    first_ag = RowGather(lk, local_width, ag_send, ag_recv, by_columns=True)
    given[lk.c] = from_owner[...]
    give.wait_recv()
    give.wait_send()
    for k in range(packs):
        m = pl.ds(lk.c * packs + k, 1)
        row = jnp.concatenate([given[c, m] for c in range(2)], axis=1)
        pick_in[k * rows : (k + 1) * rows] = coming_slots(
            row, arrived.shape[1], held, sends
        )
    for param in params:
        param.last()
    save(gain_full, out_gain)
    save(pick_out, out_pick_out)
    save(pick_in, out_pick_in)
    swaps[0].last()
    for k in range(packs):
        act[0, k, :, my_cols] = placed_rows(0, k)
        first_ag.first(act.at[0, k], k)
    for half in range(HALVES):
        wg.forward(half)
        wg.start(HALVES + half)
    for k in range(packs):
        first_ag.second(act.at[0, k], k)
    for k in range(packs):
        first_ag.last(act.at[0, k], k)
        u[k] = act[0, k, my_rows].astype(F32)
        save(act.at[0, k], out_act.at[0, k])
    weights_ready(0)

    def project(layer, k):
        for j in range(3):
            cols = slice(j * heads_width, (j + 1) * heads_width)
            acc = dot(act[layer, k], w[3 * layer, :, cols], NN)
            if j != 1:
                acc = acc + biases[layer, j // 2 : j // 2 + 1]
            qkv[layer, k, :, cols] = acc.astype(BF)
        save(qkv.at[layer, k], out_qkv.at[layer, k])

    def attention(layer, k):
        same_seq = same_sequence(seg, lk.c * packs + k)
        for head in range(heads_width // HD):
            cols = [slice(j * heads_width + head * HD, j * heads_width + (head + 1) * HD) for j in range(3)]
            scores = masked_scores(qkv[layer, k, :, cols[0]], qkv[layer, k, :, cols[1]], same_seq)
            top = jnp.max(scores, axis=1, keepdims=True)
            weighted = jnp.exp2(scores - top)
            total = jnp.sum(weighted, axis=1, keepdims=True)
            lse[layer, k, :, head : head + 1] = top + jnp.log2(total)
            probs = (weighted * (1.0 / total)).astype(BF)
            att[layer, k, :, cols[0]] = dot(probs, qkv[layer, k, :, cols[2]], NN).astype(BF)
        save(lse.at[layer, k], out_lse.at[layer, k])
        save(att.at[layer, k], out_att.at[layer, k])
        for j in range(width // 256):
            cols = slice(j * 256, (j + 1) * 256)
            acc = dot(att[layer, k], w[3 * layer, cols, 3 * heads_width :], NT)
            store_part(part, k, cols, acc, mine)
        rs.first(k)

    def normalize(layer, which, k, resid):
        mean = jnp.mean(resid, axis=1, keepdims=True)
        centred = resid - mean
        scale = lax.rsqrt(jnp.mean(centred * centred, axis=1, keepdims=True) + EPS)
        normed = centred * scale
        nrm[layer, which, k] = normed
        std[layer, which, k] = jnp.broadcast_to(scale, std.shape[3:])
        save(nrm.at[layer, which, k], out_nrm.at[layer, which, k])
        save(std.at[layer, which, k], out_std.at[layer, which, k])
        return (
            normed * gain_full[layer, which : which + 1] + offset_full[layer, which : which + 1]
        )

    def norm_one(layer, k):
        hidden = normalize(layer, 0, k, u[k] + rs.last(k) + bias_full[layer, 2:3])
        h[k] = hidden
        hid[layer, k, my_rows] = hidden.astype(BF)
        ag.first(hid.at[layer, k], k)

    def expand(layer, k):
        def tile(j, carry):
            cols = pl.ds(pl.multiple_of(j * 256, 256), 256)
            acc = dot(hid[layer, k], w[3 * layer + 1, :, cols], NN) + up_bias[layer : layer + 1, cols]
            value, slope = gelu_pair(acc)
            glu[layer, k, :, cols] = value.astype(BF)
            dglu[layer, k, :, cols] = slope.astype(BF)
            return carry

        lax.fori_loop(0, width // 256, tile, 0)
        save(glu.at[layer, k], out_glu.at[layer, k])
        save(dglu.at[layer, k], out_dglu.at[layer, k])

    def contract(layer, k):
        def tile(j, carry):
            cols = pl.ds(pl.multiple_of(j * 256, 256), 256)
            acc = dot(glu[layer, k], w[3 * layer + 2, cols, :], NT)
            store_part(part, k, cols, acc, mine)
            return carry

        lax.fori_loop(0, width // 256, tile, 0)
        rs.first(k)

    def norm_two(layer, k):
        out = normalize(layer, 1, k, h[k] + rs.last(k) + bias_full[layer, 3:4])
        u[k] = out
        if layer + 1 < layers:
            act[layer + 1, k, my_rows] = out.astype(BF)
            ag.first(act.at[layer + 1, k], k)
        else:
            u_low[k] = out.astype(BF)
            save(u_low.at[k], out_u.at[k])

    trade = Trade(
        lk, lambda t: cot_part.at[:, part_of(mine, t)],
        lambda t: cot_rows.at[:, :, part_of(local_width, t)], tr_send.at[0], tr_recv.at[0],
    )
    for layer in range(layers):
        base = 3 * layer
        more = layer + 1 < layers
        if layer:
            weights_ready(base)
            ag.last(act.at[layer, 0], 0)
            save(act.at[layer, 0], out_act.at[layer, 0])
        project(layer, 0)
        if layer:
            ag.second(act.at[layer, 1], 1)
        attention(layer, 0)
        weights_next(base + 1)
        if layer:
            ag.last(act.at[layer, 1], 1)
            save(act.at[layer, 1], out_act.at[layer, 1])
        project(layer, 1)
        rs.second(0)
        attention(layer, 1)
        norm_one(layer, 0)
        rs.second(1)
        ag.second(hid.at[layer, 0], 0)
        norm_one(layer, 1)
        weights_ready(base + 1)
        weights_next(base + 2)
        ag.last(hid.at[layer, 0], 0)
        save(hid.at[layer, 0], out_hid.at[layer, 0])
        expand(layer, 0)
        ag.second(hid.at[layer, 1], 1)
        weights_ready(base + 2)
        contract(layer, 0)
        weights_next(base + 3)
        if not more:
            send_slots(1, lambda m: cot[m])
        ag.last(hid.at[layer, 1], 1)
        save(hid.at[layer, 1], out_hid.at[layer, 1])
        expand(layer, 1)
        rs.second(0)
        contract(layer, 1)
        if not more:
            swaps[1].last()
            for k in range(packs):
                cot_part[k] = placed_rows(1, k)
            trade.first()
        norm_two(layer, 0)
        rs.second(1)
        if more:
            ag.second(act.at[layer + 1, 0], 0)
        norm_two(layer, 1)
    trade.last()
    save(cot_rows, out_cot)
    for part in range(chunks * HALVES):
        wg.drain(part)
    for swap in swaps:
        swap.drain()
    for copy in pending:
        copy.wait()


def forward(
    tokens, time_embed, cot, to_owner, from_owner, seg, shard, biases, gain, offset, up_bias
):
    rows = seg.shape[1]
    packs = tokens.shape[0] // lax.axis_size("ctx")
    width = shard.shape[2]
    local_width = tokens.shape[2]
    chunks = shard.shape[0]
    layers = chunks // 3
    mine = rows // 4
    heads = biases.shape[2]
    fs, cx = lax.axis_size("fsdp"), lax.axis_size("ctx")
    groups = fs * cx
    sends = tokens.shape[1] // fs
    parts = chunks * HALVES
    shapes = dict(
        w=((chunks, width, width), BF),
        act=((layers, packs, rows, width), BF),
        qkv=((layers, packs, rows, 3 * heads), BF),
        att=((layers, packs, rows, heads), BF),
        nrm=((layers, 2, packs, mine, width), F32),
        std=((layers, 2, packs, mine, 128), F32),
        hid=((layers, packs, rows, width), BF),
        glu=((layers, packs, rows, width), BF),
        dglu=((layers, packs, rows, width), BF),
        lse=((layers, packs, rows, 128), F32),
        u=((packs, mine, width), F32),
    )
    outs = {name: jax.ShapeDtypeStruct(*shape) for name, shape in shapes.items()}
    outs["u"] = jax.ShapeDtypeStruct((packs, mine, width), BF)
    outs["cot"] = jax.ShapeDtypeStruct((packs, mine, width), BF)
    outs["gain"] = jax.ShapeDtypeStruct((layers, 2, width), F32)
    given = tokens.shape[0] * tokens.shape[1]
    outs["pick_out"] = jax.ShapeDtypeStruct((given, tokens.shape[1]), BF)
    outs["pick_in"] = jax.ShapeDtypeStruct((packs * rows, rows), BF)
    copies = chunks + layers * packs * 11 + packs + 4
    dma = pltpu.SemaphoreType.DMA
    whole = pl.BlockSpec(memory_space=pl.ANY)
    vmem = pl.BlockSpec(memory_space=pltpu.VMEM)
    return pl.pallas_call(
        forward_kernel,
        in_specs=[vmem] * 6 + [whole] + [vmem] * 4,
        out_specs=[whole] * len(outs),
        out_shape=list(outs.values()),
        scratch_shapes=[pltpu.VMEM(*shape) for shape in shapes.values()]
        + [
            pltpu.VMEM((packs, mine, width), F32),
            pltpu.VMEM((packs, 2, 2, mine, width), BF),
            pltpu.VMEM((packs, 2, mine, width), BF),
            pltpu.VMEM((packs, mine, width), BF),
            pltpu.VMEM((packs, mine, width), BF),
            pltpu.VMEM((2, groups, packs * sends, local_width), BF),
            pltpu.VMEM((2, groups, packs * sends, local_width), BF),
            pltpu.VMEM((packs, rows, local_width), BF),
            pltpu.VMEM((packs, mine, width), BF),
            pltpu.VMEM((packs, mine, width), BF),
            pltpu.VMEM((layers, 4, width), F32),
            pltpu.VMEM((layers, 2, width), F32),
            pltpu.VMEM((layers, 2, width), F32),
            pltpu.VMEM((given, tokens.shape[1]), BF),
            pltpu.VMEM((packs * rows, rows), BF),
            pltpu.VMEM((2,) + from_owner.shape, jnp.int32),
            dma((copies,)),
            dma((packs, 2)), dma((packs, 2)), dma((packs, 3)), dma((packs, 3)),
            dma((parts, fs)), dma((parts, fs)), dma((parts, fs)), dma((parts, fs)),
            dma((parts,)),
            dma((2, 2, fs)), dma((2, 2, fs)), dma((4, 3)), dma((4, 3)), dma((2,)),
        ],
        compiler_params=pltpu.CompilerParams(
            collective_id=0, has_side_effects=True, vmem_limit_bytes=60 << 20
        ),
        name="forward",
    )(
        tokens, time_embed, cot, to_owner, from_owner, seg, shard, biases, gain, offset, up_bias
    )


class GradScatter:
    def __init__(self, lk, grad, from_x, from_z, x_send, x_recv, z_send, z_recv):
        self.lk, self.grad, self.from_x, self.from_z = lk, grad, from_x, from_z
        self.x_send, self.x_recv, self.z_send, self.z_recv = x_send, x_recv, z_send, z_recv
        self.rows = from_x.shape[2]

    def block(self, chunk, step, c):
        f = lax.rem(self.lk.f + step, self.lk.fs)
        first = pl.multiple_of((f * self.lk.cx + c) * self.rows, self.rows)
        return self.grad.at[chunk, pl.ds(first, self.rows)]

    def x_copy(self, chunk, step):
        return remote(
            self.block(chunk, step, 1 - self.lk.c), self.from_x.at[chunk, step],
            self.x_send.at[chunk, step], self.x_recv.at[chunk, step], self.lk.across,
        )

    def z_copy(self, chunk, step):
        slot = self.lk.fs - step
        return remote(
            self.block(chunk, step, self.lk.c), self.from_z.at[chunk, slot - 1],
            self.z_send.at[chunk, step], self.z_recv.at[chunk, slot], self.lk.away(step),
        )

    def each(self, first, work, last=None):
        def body(step, carry):
            work(step)
            return carry

        lax.fori_loop(first, self.lk.fs if last is None else last, body, 0)

    def first(self, chunk):
        self.each(1, lambda step: self.x_copy(chunk, step).start())
        self.x_copy(chunk, 0).start()

    def second(self, chunk, part):
        def work(step):
            self.x_copy(chunk, step).wait_recv()
            own = self.block(chunk, step, self.lk.c)
            own[...] = (own[...].astype(F32) + self.from_x[chunk, step].astype(F32)).astype(BF)
            self.z_copy(chunk, step).start()

        first, last = third(self.lk.fs, part)
        self.each(first, work, last)

    def last(self, chunk, out):
        self.x_copy(chunk, 0).wait_recv()
        out[...] = self.block(chunk, 0, self.lk.c)[...].astype(F32) + self.from_x[chunk, 0].astype(F32)

        def work(step):
            self.z_copy(chunk, self.lk.fs - step).wait_recv()
            out[...] = out[...] + self.from_z[chunk, step - 1].astype(F32)

        self.each(1, work)

    def drain(self, chunk):
        self.each(0, lambda step: self.x_copy(chunk, step).wait_send())
        self.each(1, lambda step: self.z_copy(chunk, step).wait_send())


def backward_kernel(
    up_in, u_in, pick_out, pick_in, act_in, w_in, qkv_in, att_in, nrm_in, std_in, hid_in, glu_in, dglu_in,
    lse_in, gain, seg,
    out_qkv, out_out, out_up, out_down, out_ret, out_sums,
    w, qkv, att, nrm, std, hid, glu, dglu, lse, up, gtwo, gl, gm, gup, gqkv, gatt,
    part, from_sib, to_peer, from_peer, grad, from_x, from_z, gsum, low, ret_in,
    out_vec, out_head, out_bias, vec_parts, sums,
    in_sem, out_sem, rs_send, rs_recv, ag_send, ag_recv, x_send, x_recv, z_send, z_recv,
    ex_send, ex_recv, tr_send, tr_recv, pick_sem,
):
    packs, rows, width = hid.shape
    layers = gain.shape[0]
    mine = rows // 4
    heads_width = att.shape[2]
    lk = Links()
    sources = dict(
        nrm1=lambda layer: (nrm_in.at[layer, 1], nrm.at[1]),
        std1=lambda layer: (std_in.at[layer, 1], std.at[1]),
        nrm0=lambda layer: (nrm_in.at[layer, 0], nrm.at[0]),
        std0=lambda layer: (std_in.at[layer, 0], std.at[0]),
        w2=lambda layer: (w_in.at[3 * layer + 2], w.at[2]),
        dglu=lambda layer: (dglu_in.at[layer], dglu),
        w1=lambda layer: (w_in.at[3 * layer + 1], w.at[1]),
        glu=lambda layer: (glu_in.at[layer], glu),
        hid=lambda layer: (hid_in.at[layer], hid),
        w0=lambda layer: (w_in.at[3 * layer], w.at[0]),
        qkv=lambda layer: (qkv_in.at[layer], qkv),
        lse=lambda layer: (lse_in.at[layer], lse),
        att=lambda layer: (att_in.at[layer], att),
        act=lambda layer: (act_in.at[layer], hid),
    )
    order = {name: index for index, name in enumerate(sources)}

    def fetch(name, layer):
        if layer >= 0:
            src, dst = sources[name](layer)
            pltpu.make_async_copy(src, dst, in_sem.at[order[name]]).start()

    def ready(name, layer):
        src, dst = sources[name](layer)
        pltpu.make_async_copy(src, dst, in_sem.at[order[name]]).wait()

    loads = [
        pltpu.make_async_copy(up_in, to_peer, in_sem.at[len(order)]),
        pltpu.make_async_copy(u_in, low, in_sem.at[len(order) + 1]),
    ]
    for load in loads:
        load.start()
    for name in sources:
        if name != "act":
            fetch(name, layers - 1)
    lk.barrier()
    rs = RowSum(lk, part, from_sib, to_peer, from_peer, rs_send, rs_recv)
    ag = RowGather(lk, mine, ag_send, ag_recv)
    gs = GradScatter(lk, grad, from_x, from_z, x_send, x_recv, z_send, z_recv)
    my_rows = pl.ds(pl.multiple_of(lk.t * mine, mine), mine)
    pending = []
    held = {}
    local_width = ret_in.shape[1]
    swap_rows = width // (lk.fs * lk.cx)
    sends = swap_rows // packs
    low_cols, next_cols, third_cols, last_cols = (
        slice(i * local_width, (i + 1) * local_width) for i in range(4)
    )

    class Return:
        def __init__(self, index, first, second, landed):
            self.index, self.first_buf, self.second_buf, self.landed = index, first, second, landed
            self.trade = Trade(
                lk, lambda t: low.at[:, :, part_of(local_width, t)],
                lambda t: gup.at[:, part_of(mine, t), low_cols],
                tr_send.at[index], tr_recv.at[index],
            )
            self.swap = Exchange(
                lk, lambda g: first.at[part_of(swap_rows, g), low_cols],
                lambda g: landed.at[part_of(swap_rows, g)], ex_send.at[index], ex_recv.at[index],
            )
            self.picks = [
                pltpu.make_async_copy(
                    pick_in, second.at[:, : 2 * local_width], pick_sem.at[index, 0]
                ),
                pltpu.make_async_copy(pick_out, second.at[:, third_cols], pick_sem.at[index, 1]),
            ]

        def load(self):
            for copy in self.picks:
                copy.start()

        def middle(self):
            self.trade.last()
            self.picks[0].wait()
            for k in range(packs):
                pick = self.second_buf[k * rows : (k + 1) * rows, : 2 * local_width]
                values = dot(pick, gup[k, :, low_cols], NN).astype(BF)
                for g in range(rows // sends):
                    first = g * swap_rows + k * sends
                    self.first_buf[first : first + sends, low_cols] = values[
                        g * sends : (g + 1) * sends
                    ]
            self.swap.first()

        def last(self):
            self.swap.last()
            self.picks[1].wait()
            given = pick_out.shape[1]
            for c in range(2):
                for k in range(packs):
                    m = c * packs + k
                    blocks = [
                        self.landed[
                            (2 * f + c) * swap_rows + k * sends :
                            (2 * f + c) * swap_rows + (k + 1) * sends
                        ]
                        for f in range(given // sends)
                    ]
                    pick = self.second_buf[m * given : (m + 1) * given, third_cols]
                    values = dot(pick, jnp.concatenate(blocks, axis=0), TN)
                    self.second_buf[m * given : (m + 1) * given, last_cols] = values.astype(BF)
            save(self.second_buf.at[:, last_cols], out_ret.at[self.index])
            self.saved = pending.pop()

        def finish(self):
            self.swap.drain()
            self.saved.wait()

    give_back = [
        Return(0, grad.at[0], grad.at[1], grad.at[0, :, next_cols]),
        Return(1, grad.at[3 * layers - 1], grad.at[3 * layers - 2], ret_in),
    ]
    vec_trade = Trade(
        lk, lambda t: out_vec.at[:, :, part_of(local_width, t)], lambda t: vec_parts.at[t],
        tr_send.at[2], tr_recv.at[2],
    )
    vec_swap = Exchange(
        lk, lambda g: sums.at[lk.g], lambda g: sums.at[g], ex_send.at[2], ex_recv.at[2],
        in_place=True,
    )

    def vec_middle():
        vec_trade.last()
        total = vec_parts[0]
        for t in range(1, 4):
            total = total + vec_parts[t]
        sums[lk.g, :, 0:6] = total
        sums[lk.g, :, 6:8] = out_head[...]
        for j in range(4):
            sums[lk.g, :, 8 + j : 9 + j] = out_bias[:, :, j * local_width : (j + 1) * local_width]
        vec_swap.first()

    def vec_last():
        vec_swap.last()

        def add(g, total):
            return total + sums[g]

        out_sums[...] = lax.fori_loop(1, sums.shape[0], add, sums[0])

    used = []

    def save(src, dst):
        copy = pltpu.make_async_copy(src, dst, out_sem.at[len(used)])
        copy.start()
        used.append(1)
        pending.append(copy)

    out_vec[...] = jnp.zeros_like(out_vec)
    out_head[...] = jnp.zeros_like(out_head)
    out_bias[...] = jnp.zeros_like(out_bias)

    def norm_back(layer, which, k, upstream):
        normed = nrm[which, k]
        scale = std[which, k][:, 0:1]
        out_vec[layer, 2 + which : 3 + which] += jnp.sum(upstream * normed, axis=0, keepdims=True)
        out_vec[layer, 4 + which : 5 + which] += jnp.sum(upstream, axis=0, keepdims=True)
        scaled = upstream * gain[layer, which : which + 1]
        first = jnp.mean(scaled, axis=1, keepdims=True)
        second = jnp.mean(scaled * normed, axis=1, keepdims=True)
        result = scale * (scaled - first - normed * second)
        out_vec[layer, which : which + 1] += jnp.sum(result, axis=0, keepdims=True)
        return result

    def norm_two(layer, k):
        result = norm_back(layer, 1, k, up[k])
        gtwo[k] = result
        gl[k, my_rows] = result.astype(BF)
        ag.first(gl.at[k], k)

    def norm_one(layer, k):
        result = norm_back(layer, 0, k, gtwo[k] + rs.last(k))
        up[k] = result
        gm[k, my_rows] = result.astype(BF)
        ag.first(gm.at[k], k)

    def tiles(work):
        def body(j, carry):
            work(pl.ds(pl.multiple_of(j * 256, 256), 256))
            return carry

        lax.fori_loop(0, width // 256, body, 0)

    def through_down(layer, k):
        def tile(cols):
            grad_gelu = dot(gl[k], w[2, :, cols], NN).astype(BF).astype(F32)
            result = (grad_gelu * dglu[k, :, cols].astype(F32)).astype(BF)
            gup[k, :, cols] = result
            out_bias[layer, :, cols] += jnp.sum(result.astype(F32), axis=0, keepdims=True)

        tiles(tile)

    def through_up(layer, k):
        tiles(lambda cols: store_part(part, k, cols, dot(gup[k], w[1, cols, :], NT), mine))
        rs.first(k)

    def through_out(k):
        gatt[k] = dot(gm[k], w[0, :, 3 * heads_width :], NN).astype(BF)

    def attention(layer, k):
        same_seq = same_sequence(seg, lk.c * packs + k)
        scale = 1.0 / math.sqrt(HD)
        for head in range(heads_width // HD):
            cols = [slice(j * heads_width + head * HD, j * heads_width + (head + 1) * HD) for j in range(3)]
            query, keys, values = (qkv[k, :, c] for c in cols)
            grads = gatt[k, :, cols[0]]
            probs = jnp.exp2(masked_scores(query, keys, same_seq) - lse[k, :, head : head + 1])
            grad_probs = dot(grads, values, NT)
            delta = jnp.sum(probs * grad_probs, axis=1, keepdims=True)
            grad_scores = (probs * (grad_probs - delta)).astype(BF)
            gqkv[k, :, cols[0]] = (dot(grad_scores, keys, NN) * scale).astype(BF)
            gqkv[k, :, cols[1]] = (dot(grad_scores, query, TN) * scale).astype(BF)
            gqkv[k, :, cols[2]] = dot(probs.astype(BF), grads, TN).astype(BF)
        for j in range(2):
            cols = slice(2 * j * heads_width, (2 * j + 1) * heads_width)
            out_head[layer, j : j + 1] += jnp.sum(
                gqkv[k, :, cols].astype(F32), axis=0, keepdims=True
            )

    def through_qkv(k):
        tiles(
            lambda cols: store_part(
                part, k, cols, dot(gqkv[k], w[0, cols, : 3 * heads_width], NT), mine
            )
        )
        rs.first(k)

    def product(left, right, cols, right_cols=slice(None)):
        total = dot(left[0, :, cols], right[0, :, right_cols], TN)
        for k in range(1, packs):
            total = total + dot(left[k, :, cols], right[k, :, right_cols], TN)
        return total.astype(BF)

    def down_grad(layer):
        def tile(cols):
            grad[3 * layer + 2, cols, :] = product(gl, glu, cols)

        tiles(tile)
        gs.first(3 * layer + 2)

    def up_grad(layer):
        def tile(cols):
            grad[3 * layer + 1, cols, :] = product(hid, gup, cols)

        tiles(tile)
        gs.first(3 * layer + 1)

    def first_grad(layer):
        def tile(cols):
            grad[3 * layer, cols, : 3 * heads_width] = product(hid, gqkv, cols)
            grad[3 * layer, cols, 3 * heads_width :] = product(gm, att, cols)

        tiles(tile)
        gs.first(3 * layer)

    def emit(layer, which):
        chunk = 3 * layer + which
        out = gsum.at[which]
        while held.get(which):
            held[which].pop().wait()
        gs.last(chunk, out)
        held[which] = []
        saved = len(pending)
        if which == 2:
            save(out, out_down.at[layer])
        elif which == 1:
            save(out, out_up.at[layer])
        else:
            for c in range(3):
                save(out.at[:, c * heads_width : (c + 1) * heads_width], out_qkv.at[layer, c])
            save(out.at[:, 3 * heads_width :], out_out.at[layer])
        held[which] = [pending.pop() for _ in range(len(pending) - saved)]

    give_back[0].load()
    for load in loads:
        load.wait()
    top = layers - 1
    ready("nrm1", top)
    ready("std1", top)
    for k in range(packs):
        up[k] = to_peer[k].astype(F32)
        norm_two(top, k)
    give_back[0].trade.first()
    fetch("nrm1", top - 1)
    fetch("std1", top - 1)
    for layer in reversed(range(layers)):
        base = 3 * layer
        later = layer < top
        ag.second(gl.at[0], 0)
        if layer == top:
            give_back[0].middle()
        else:
            gs.second(base + 3 + 1, 1)
        ready("w2", layer)
        ready("dglu", layer)
        ag.last(gl.at[0], 0)
        through_down(layer, 0)
        ag.second(gl.at[1], 1)
        ready("w1", layer)
        through_up(layer, 0)
        ag.last(gl.at[1], 1)
        through_down(layer, 1)
        fetch("w2", layer - 1)
        fetch("dglu", layer - 1)
        rs.second(0)
        through_up(layer, 1)
        fetch("w1", layer - 1)
        if later:
            gs.second(base + 3 + 1, 2)
        ready("glu", layer)
        down_grad(layer)
        fetch("glu", layer - 1)
        rs.second(1)
        ready("nrm0", layer)
        ready("std0", layer)
        norm_one(layer, 0)
        if later:
            gs.second(base + 3, 0)
        ready("hid", layer)
        up_grad(layer)
        fetch("act", layer)
        ag.second(gm.at[0], 0)
        norm_one(layer, 1)
        fetch("nrm0", layer - 1)
        fetch("std0", layer - 1)
        if later:
            gs.second(base + 3, 1)
        ready("w0", layer)
        ready("qkv", layer)
        ready("lse", layer)
        ag.last(gm.at[0], 0)
        through_out(0)
        ag.second(gm.at[1], 1)
        attention(layer, 0)
        through_qkv(0)
        if later:
            gs.second(base + 3, 2)
        else:
            gs.second(base + 2, 0)
            gs.second(base + 2, 1)
        ag.last(gm.at[1], 1)
        through_out(1)
        rs.second(0)
        attention(layer, 1)
        fetch("qkv", layer - 1)
        fetch("lse", layer - 1)
        through_qkv(1)
        fetch("w0", layer - 1)
        if later:
            gs.second(base + 2, 0)
        else:
            gs.second(base + 2, 2)
            gs.second(base + 1, 0)
        rs.second(1)
        ready("att", layer)
        ready("act", layer)
        first_grad(layer)
        if layer:
            fetch("att", layer - 1)
            fetch("hid", layer - 1)
        for k in range(packs):
            up[k] = rs.last(k) + up[k]
            if layer:
                if k == 0:
                    ready("nrm1", layer - 1)
                    ready("std1", layer - 1)
                norm_two(layer - 1, k)
            else:
                low[k] = up[k].astype(BF)
        if layer == top:
            give_back[0].last()
            give_back[0].finish()
        if layer:
            fetch("nrm1", layer - 2)
            fetch("std1", layer - 2)
    give_back[1].trade.first()
    vec_trade.first()
    gs.second(2, 1)
    emit(1, 2)
    emit(1, 1)
    for chunk in (3 * layers - 1, 3 * layers - 2):
        gs.drain(chunk)
    give_back[1].load()
    gs.second(2, 2)
    give_back[1].middle()
    vec_middle()
    emit(1, 0)
    gs.second(1, 0)
    gs.second(1, 1)
    gs.second(1, 2)
    emit(0, 2)
    gs.second(0, 0)
    give_back[1].last()
    vec_last()
    gs.second(0, 1)
    gs.second(0, 2)
    emit(0, 1)
    emit(0, 0)
    for chunk in range(3 * layers - 2):
        gs.drain(chunk)
    give_back[1].finish()
    vec_swap.drain()
    for copy in pending + sum(held.values(), []):
        copy.wait()


def backward(upstream, u, pick_out, pick_in, saved, gain, seg):
    full_w, o_act, o_qkv, o_att, o_nrm, o_std, o_hid, o_glu, o_dglu, o_lse = saved
    layers, packs, rows, width = o_act.shape
    mine = rows // 4
    chunks = 3 * layers
    heads = o_att.shape[3]
    local_width = width // 4
    fs, cx = lax.axis_size("fsdp"), lax.axis_size("ctx")
    groups = fs * cx
    shard = width // groups
    given = pick_out.shape[0]
    outs = [
        jax.ShapeDtypeStruct((layers, 3, shard, heads), F32),
        jax.ShapeDtypeStruct((layers, shard, heads), F32),
        jax.ShapeDtypeStruct((layers, shard, width), F32),
        jax.ShapeDtypeStruct((layers, shard, width), F32),
        jax.ShapeDtypeStruct((2, given, local_width), BF),
        jax.ShapeDtypeStruct((layers, 12, local_width), F32),
    ]
    dma = pltpu.SemaphoreType.DMA
    whole = pl.BlockSpec(memory_space=pl.ANY)
    vmem = pl.BlockSpec(memory_space=pltpu.VMEM)
    full = pltpu.VMEM((packs, rows, width), BF)
    rowed = pltpu.VMEM((packs, mine, width), F32)
    return pl.pallas_call(
        backward_kernel,
        in_specs=[whole] * 14 + [vmem] * 2,
        out_specs=[whole] * 5 + [vmem],
        out_shape=outs,
        scratch_shapes=[
            pltpu.VMEM((3, width, width), BF),
            pltpu.VMEM((packs, rows, 3 * heads), BF),
            pltpu.VMEM((packs, rows, heads), BF),
            pltpu.VMEM((2, packs, mine, width), F32),
            pltpu.VMEM((2, packs, mine, 128), F32),
            full, full, full,
            pltpu.VMEM((packs, rows, 128), F32),
            rowed, rowed,
            full, full, full,
            pltpu.VMEM((packs, rows, 3 * heads), BF),
            pltpu.VMEM((packs, rows, heads), BF),
            pltpu.VMEM((packs, 2, 2, mine, width), BF),
            pltpu.VMEM((packs, 2, mine, width), BF),
            pltpu.VMEM((packs, mine, width), BF),
            pltpu.VMEM((packs, mine, width), BF),
            pltpu.VMEM((chunks, width, width), BF),
            pltpu.VMEM((chunks, fs, shard, width), BF),
            pltpu.VMEM((chunks, fs - 1, shard, width), BF),
            pltpu.VMEM((3, shard, width), F32),
            pltpu.VMEM((packs, mine, width), BF),
            pltpu.VMEM((given, local_width), BF),
            pltpu.VMEM((layers, 6, width), F32),
            pltpu.VMEM((layers, 2, heads), F32),
            pltpu.VMEM((layers, 1, width), F32),
            pltpu.VMEM((4, layers, 6, local_width), F32),
            pltpu.VMEM((groups, layers, 12, local_width), F32),
            dma((16,)), dma((packs + 6 * layers + 2,)),
            dma((packs, 2)), dma((packs, 2)), dma((packs, 3)), dma((packs, 3)),
            dma((chunks, fs)), dma((chunks, fs)), dma((chunks, fs)), dma((chunks, fs)),
            dma((3, 2, fs)), dma((3, 2, fs)), dma((3, 3)), dma((3, 3)), dma((2, 2)),
        ],
        compiler_params=pltpu.CompilerParams(
            collective_id=1, has_side_effects=True, vmem_limit_bytes=62 << 20
        ),
        name="backward",
    )(
        upstream, u, pick_out, pick_in, o_act, full_w, o_qkv, o_att, o_nrm, o_std, o_hid,
        o_glu, o_dglu, o_lse, gain, seg,
    )


def local(
    tokens, time_embed, cotangent, segment_ids, to_owner, from_owner,
    w_qkv, w_out, w_up, w_down, biases, norm_gain, norm_bias, up_bias,
):
    micro, rows, width = tokens.shape
    layers = w_qkv.shape[0]
    shard = jnp.concatenate(
        [w_qkv[:, 0], w_qkv[:, 1], w_qkv[:, 2], w_out, w_up, w_down], axis=2
    )
    shard = shard.reshape(layers, shard.shape[1], 3, -1).transpose(0, 2, 1, 3)
    shard = shard.reshape(layers * 3, shard.shape[2], -1)
    *saved, u, upstream, gain, pick_out, pick_in = forward(
        tokens, time_embed, cotangent, to_owner, from_owner, segment_ids, shard, biases,
        norm_gain, norm_bias, up_bias,
    )
    g_qkv, g_out, g_up, g_down, returned, sums = backward(
        upstream, u, pick_out, pick_in, saved, gain, segment_ids
    )
    returned = returned.reshape(2, micro, rows, width).astype(F32)
    return (
        returned[0],
        returned[1],
        g_qkv, g_out, g_up, g_down,
        jnp.concatenate([sums[:, 6:8], sums[:, 0:2]], axis=1),
        sums[:, 2:4],
        sums[:, 4:6],
        sums[:, 8:12].reshape(layers, -1),
    )


def solution(mesh):
    wide = P(None, GRP, "tp")
    vec = P(None, None, "tp")
    qkv = P(None, None, GRP, "tp")
    owner = P(None, GRP)
    return jax.shard_map(
        local,
        mesh=mesh,
        in_specs=(
            wide, wide, wide, P(None, "fsdp"), owner, owner, qkv, wide, wide, wide,
            vec, vec, vec, P(None, "tp"),
        ),
        out_specs=(wide, wide, qkv, wide, wide, wide, vec, vec, vec, P(None, "tp")),
        check_vma=False,
    )
```

```python
import functools
import math

import jax
import jax.numpy as jnp
from jax import lax
from jax.experimental import pallas as pl
from jax.experimental.pallas import tpu as pltpu
from jax.sharding import PartitionSpec as P

HD = 64
NEG = -1e30
EPS = 1e-05
BF = jnp.bfloat16
F32 = jnp.float32
GRP = ("fsdp", "ctx")


def dot(left, right, dims):
    return lax.dot_general(left, right, (dims, ((), ())), preferred_element_type=F32)


NN = ((1,), (0,))
NT = ((1,), (1,))
TN = ((0,), (0,))

MESH = pl.DeviceIdType.MESH
LOG2E = 1.4426950408889634
HALVES = 1


def gelu_pair(values):
    bell = jnp.exp2(values * values * (-0.5 * LOG2E))
    t = 1.0 / (1.0 + (0.3275911 * math.sqrt(0.5)) * jnp.abs(values))
    poly = t * (
        0.127414796 + t * (-0.142248368 + t * (0.7107068705 + t * (-0.7265760135 + t * 0.5307027145)))
    )
    tail = poly * bell
    phi = jnp.where(values < 0, tail, 1.0 - tail)
    return values * phi, phi + values * bell * (1.0 / math.sqrt(2.0 * math.pi))


class Links:
    def __init__(self):
        self.fs, self.cx = lax.axis_size("fsdp"), lax.axis_size("ctx")
        self.f, self.c, self.t = (lax.axis_index(a) for a in ("fsdp", "ctx", "tp"))
        self.core, self.chip = lax.rem(self.t, 2), self.t // 2
        self.sib_t = self.t + 1 - 2 * self.core
        self.peer_t = lax.rem(self.t + 2, 4)
        self.sib = (self.f, self.c, self.sib_t)
        self.peer = (self.f, self.c, self.peer_t)
        self.diag_t = 3 - self.t
        self.diag = (self.f, self.c, self.diag_t)
        self.across = (self.f, 1 - self.c, self.t)
        self.g = self.f * self.cx + self.c

    def away(self, step, c=None):
        return (lax.rem(self.f + step, self.fs), self.c if c is None else c, self.t)

    def barrier(self):
        sem = pltpu.get_barrier_semaphore()
        for target in (self.sib, self.peer, self.diag, self.across):
            pl.semaphore_signal(sem, inc=1, device_id=target, device_id_type=MESH)

        def greet(step, carry):
            for c in (self.c, 1 - self.c):
                pl.semaphore_signal(
                    sem, inc=1, device_id=self.away(step, c), device_id_type=MESH
                )
            return carry

        lax.fori_loop(1, self.fs, greet, 0)
        pl.semaphore_wait(sem, 2 + 2 * self.fs)


def remote(src, dst, send, recv, target):
    return pltpu.make_async_remote_copy(
        src_ref=src, dst_ref=dst, send_sem=send, recv_sem=recv,
        device_id=target, device_id_type=MESH,
    )


class RowSum:
    def __init__(self, lk, part, from_sib, to_peer, from_peer, send, recv):
        self.lk, self.part, self.from_sib = lk, part, from_sib
        self.to_peer, self.from_peer, self.send, self.recv = to_peer, from_peer, send, recv

    def sib_copy(self, k):
        return remote(
            self.part.at[k, 1 - self.lk.core], self.from_sib.at[k],
            self.send.at[k, 0], self.recv.at[k, 0], self.lk.sib,
        )

    def peer_copy(self, k):
        return remote(
            self.to_peer.at[k], self.from_peer.at[k],
            self.send.at[k, 1], self.recv.at[k, 1], self.lk.peer,
        )

    def first(self, k):
        self.sib_copy(k).start()

    def second(self, k):
        self.sib_copy(k).wait_recv()
        other = 1 - self.lk.chip
        total = self.part[k, self.lk.core, other].astype(F32) + self.from_sib[k, other].astype(F32)
        self.to_peer[k] = total.astype(BF)
        self.peer_copy(k).start()

    def last(self, k):
        own = self.part[k, self.lk.core, self.lk.chip].astype(F32)
        own = own + self.from_sib[k, self.lk.chip].astype(F32)
        self.peer_copy(k).wait_recv()
        self.sib_copy(k).wait_send()
        self.peer_copy(k).wait_send()
        return own + self.from_peer[k].astype(F32)


class RowGather:
    def __init__(self, lk, rows, send, recv, by_columns=False):
        self.lk, self.rows, self.send, self.recv = lk, rows, send, recv
        self.by_columns = by_columns

    def block(self, ref, index):
        part = part_of(self.rows, index)
        return ref.at[:, part] if self.by_columns else ref.at[part]

    def copy(self, ref, k, which):
        index = self.lk.t if which < 2 else self.lk.peer_t
        part = self.block(ref, index)
        target = self.lk.peer if which == 0 else self.lk.sib
        return remote(part, part, self.send.at[k, which], self.recv.at[k, which], target)

    def first(self, ref, k):
        self.copy(ref, k, 0).start()
        self.copy(ref, k, 1).start()

    def second(self, ref, k):
        self.copy(ref, k, 0).wait_recv()
        self.copy(ref, k, 2).start()

    def last(self, ref, k):
        self.copy(ref, k, 1).wait_recv()
        self.copy(ref, k, 2).wait_recv()
        for which in range(3):
            self.copy(ref, k, which).wait_send()


class Exchange:
    def __init__(self, lk, src, dst, send, recv, in_place=False):
        self.lk, self.src, self.dst, self.send, self.recv = lk, src, dst, send, recv
        self.in_place = in_place

    def copy(self, other, step):
        lk = self.lk
        c = 1 - lk.c if other else lk.c
        target = lax.rem(lk.f + step, lk.fs) * lk.cx + c
        return remote(
            self.src(target), self.dst(lk.g), self.send.at[other, step],
            self.recv.at[other, lax.rem(lk.fs - step, lk.fs)], lk.away(step, c),
        )

    def each(self, work):
        def body(step, carry):
            work(1, step)
            work(0, step)
            return carry

        work(1, 0)
        lax.fori_loop(1, self.lk.fs, body, 0)

    def first(self):
        self.each(lambda other, step: self.copy(other, step).start())
        if not self.in_place:
            self.dst(self.lk.g)[...] = self.src(self.lk.g)[...]

    def last(self):
        def work(other, step):
            self.copy(other, lax.rem(self.lk.fs - step, self.lk.fs)).wait_recv()

        self.each(work)

    def drain(self):
        self.each(lambda other, step: self.copy(other, step).wait_send())


class Trade:
    def __init__(self, lk, src, dst, send, recv):
        self.lk, self.src, self.dst, self.send, self.recv = lk, src, dst, send, recv

    def copies(self):
        lk = self.lk
        pairs = ((lk.peer_t, lk.peer), (lk.diag_t, lk.diag), (lk.sib_t, lk.sib))
        return [
            remote(self.src(index), self.dst(lk.t), self.send.at[i], self.recv.at[i], target)
            for i, (index, target) in enumerate(pairs)
        ]

    def first(self):
        for copy in self.copies():
            copy.start()
        self.dst(self.lk.t)[...] = self.src(self.lk.t)[...]

    def last(self):
        for copy in self.copies():
            copy.wait_recv()
            copy.wait_send()


def third(count, part):
    return 1 + (count - 1) * part // 3, 1 + (count - 1) * (part + 1) // 3


def part_of(size, index):
    return pl.ds(pl.multiple_of(index * size, size), size)


def stored_slots(dst, values, first, count, sends, block):
    for i in range(count):
        dst(i)[block * sends : (block + 1) * sends] = values[
            (first + i) * sends : (first + i + 1) * sends
        ].astype(BF)


def one_hot(rows, values):
    return (lax.broadcasted_iota(jnp.int32, (rows, values.shape[1]), 0) == values).astype(BF)


def counts_before(present):
    size = present.shape[1]
    earlier = lax.broadcasted_iota(jnp.int32, (size, size), 0) < lax.broadcasted_iota(
        jnp.int32, (size, size), 1
    )
    return dot(present, earlier.astype(BF), NN)


def leaving_slots(to_row, packs_total, pack, sends):
    groups = one_hot(packs_total, to_row // pack)
    base = lax.broadcasted_iota(jnp.int32, groups.shape, 0) * sends
    slot = (counts_before(groups) + base.astype(F32)) * groups.astype(F32)
    return one_hot(to_row.shape[1], jnp.sum(slot, axis=0, keepdims=True).astype(jnp.int32))


def coming_slots(given, groups, rows, sends):
    source = one_hot(groups, given // rows)
    within = one_hot(rows, lax.rem(given, rows))
    ranks = counts_before(dot(source, within, NT).astype(BF)).astype(BF)
    base = lax.broadcasted_iota(jnp.int32, source.shape, 0) * sends
    slot = (dot(ranks, within, NN) + base.astype(F32)) * source.astype(F32)
    return one_hot(groups * sends, jnp.sum(slot, axis=0, keepdims=True).astype(jnp.int32))


def same_sequence(seg_ref, row):
    member = one_hot(8, lax.rem(seg_ref[pl.ds(row, 1)], 8))
    return dot(member, member, TN) > 0.5


class WeightGather:
    def __init__(self, lk, shard, full, z_send, z_recv, x_send, x_recv, own):
        self.lk, self.shard, self.full = lk, shard, full
        self.z_send, self.z_recv, self.x_send, self.x_recv = z_send, z_recv, x_send, x_recv
        self.own = own
        self.rows = shard.shape[1]
        self.cols = shard.shape[2] // HALVES

    def part(self, chunk):
        return slice(chunk % HALVES * self.cols, (chunk % HALVES + 1) * self.cols)

    def mine(self, chunk):
        return self.shard.at[chunk // HALVES, :, self.part(chunk)]

    def block(self, chunk, f, c):
        rows = part_of(self.rows, f * self.lk.cx + c)
        return self.full.at[chunk // HALVES, rows, self.part(chunk)]

    def z_copy(self, chunk, step):
        return remote(
            self.mine(chunk), self.block(chunk, self.lk.f, self.lk.c),
            self.z_send.at[chunk, step], self.z_recv.at[chunk, self.lk.fs - step],
            self.lk.away(step),
        )

    def far(self, step):
        return jnp.abs(lax.rem(self.lk.f + step, self.lk.fs) - self.lk.f) == 3

    def relay(self, chunk):
        f = self.lk.f
        part = self.block(chunk, 3 * (2 - f), self.lk.c)
        return remote(
            part, part, self.z_send.at[chunk, 0], self.z_recv.at[chunk, 5 - 2 * f],
            (3 * (f - 1), self.lk.c, self.lk.t),
        )

    def inner(self):
        return (self.lk.f == 1) | (self.lk.f == 2)

    def x_copy(self, chunk, step):
        f = lax.rem(self.lk.f + step, self.lk.fs)
        part = self.block(chunk, f, self.lk.c)
        return remote(
            part, part, self.x_send.at[chunk, step], self.x_recv.at[chunk, step], self.lk.across
        )

    def x_own(self, chunk):
        return remote(
            self.mine(chunk), self.block(chunk, self.lk.f, self.lk.c),
            self.x_send.at[chunk, 0], self.x_recv.at[chunk, 0], self.lk.across,
        )

    def own_copy(self, chunk):
        return pltpu.make_async_copy(
            self.mine(chunk), self.block(chunk, self.lk.f, self.lk.c), self.own.at[chunk]
        )

    def each(self, first, work):
        def body(step, carry):
            work(step)
            return carry

        lax.fori_loop(first, self.lk.fs, body, 0)

    def own_first(self, chunk):
        self.own_copy(chunk).start()
        self.x_own(chunk).start()

    def start(self, chunk):
        if self.lk.fs == 4:
            for step in (2, 1, 3):
                pl.when(jnp.logical_not(self.far(step)))(self.z_copy(chunk, step).start)
        else:
            self.each(1, lambda step: self.z_copy(chunk, step).start())

    def forward(self, chunk):
        def work(step):
            self.z_copy(chunk, self.lk.fs - step).wait_recv()
            self.x_copy(chunk, step).start()

        if self.lk.fs == 4:
            work(2)
            pl.when(self.inner())(self.relay(chunk).start)
            work(1)
            work(3)
        else:
            self.each(1, work)

    def finish(self, chunk):
        self.own_copy(chunk).wait()
        self.each(0, lambda step: self.x_copy(chunk, step).wait_recv())

    def drain(self, chunk):
        if self.lk.fs == 4:
            for step in (2, 1, 3):
                pl.when(jnp.logical_not(self.far(step)))(self.z_copy(chunk, step).wait_send)
            pl.when(self.inner())(self.relay(chunk).wait_send)
        else:
            self.each(1, lambda step: self.z_copy(chunk, step).wait_send())
        self.each(0, lambda step: self.x_copy(chunk, step).wait_send())


def store_part(part, k, cols, values, rows):
    for block in range(4):
        part[k, block % 2, block // 2, :, cols] = values[block * rows : (block + 1) * rows].astype(
            BF
        )


def masked_scores(query, key_rows, same_seq):
    return jnp.where(
        same_seq, dot(query, key_rows, NT) * (LOG2E / math.sqrt(HD)), NEG
    )


def forward_kernel(
    tokens, time_embed, cot, to_owner, from_owner, seg, shard, biases, gain, offset, up_bias,
    out_w, out_act, out_qkv, out_att, out_nrm, out_std, out_hid, out_glu, out_dglu, out_lse,
    out_u, out_cot, out_gain, out_pick_out, out_pick_in,
    w, act, qkv, att, nrm, std, hid, glu, dglu, lse, u, h, part, from_sib, to_peer, from_peer,
    slots, arrived, cot_part, cot_rows, u_low,
    bias_full, gain_full, offset_full, pick_out, pick_in, given,
    out_sem, rs_send, rs_recv, ag_send, ag_recv, z_send, z_recv, x_send, x_recv, own,
    ex_send, ex_recv, tr_send, tr_recv, given_sem,
):
    layers, packs, rows, width = act.shape
    sends = slots.shape[2] // packs
    local_width = slots.shape[3]
    mine = rows // 4
    heads_width = att.shape[3]
    chunks = shard.shape[0]
    lk = Links()
    lk.barrier()
    rs = RowSum(lk, part, from_sib, to_peer, from_peer, rs_send, rs_recv)
    ag = RowGather(lk, mine, ag_send, ag_recv)
    wg = WeightGather(lk, shard, w, z_send, z_recv, x_send, x_recv, own)
    pending = []

    def save(src, dst):
        copy = pltpu.make_async_copy(src, dst, out_sem.at[len(pending)])
        copy.start()
        pending.append(copy)

    my_rows = part_of(mine, lk.t)
    my_cols = part_of(local_width, lk.t)
    swaps = [
        Exchange(
            lk, lambda g, i=i: slots.at[i, g], lambda g, i=i: arrived.at[i, g],
            ex_send.at[i], ex_recv.at[i],
        )
        for i in range(2)
    ]

    def send_slots(which, values):
        for c in range(2):
            for k in range(packs):
                m = c * packs + k
                picked = dot(pick_out[m * held : (m + 1) * held], values(m), NN)
                for f in range(picked.shape[0] // sends):
                    slots[which, 2 * f + c, k * sends : (k + 1) * sends] = picked[
                        f * sends : (f + 1) * sends
                    ].astype(BF)
        swaps[which].first()

    def placed_rows(which, k):
        blocks = [
            arrived[which, g, k * sends : (k + 1) * sends] for g in range(arrived.shape[1])
        ]
        return dot(
            pick_in[k * rows : (k + 1) * rows], jnp.concatenate(blocks, axis=0), TN
        ).astype(BF)

    def weights_next(chunk):
        if chunk < chunks:
            for part in range(chunk * HALVES, (chunk + 1) * HALVES):
                wg.forward(part)
                if part + HALVES < chunks * HALVES:
                    wg.start(part + HALVES)
                if part + 3 * HALVES < chunks * HALVES:
                    wg.own_first(part + 3 * HALVES)

    def weights_ready(chunk):
        for part in range(chunk * HALVES, (chunk + 1) * HALVES):
            wg.finish(part)
        save(w.at[chunk], out_w.at[chunk])

    give = remote(
        from_owner, given.at[lk.c], given_sem.at[0], given_sem.at[1], lk.across
    )
    give.start()
    params = [
        Trade(
            lk, lambda t, src=src: src, lambda t, full=full: full.at[:, :, part_of(local_width, t)],
            tr_send.at[1 + i], tr_recv.at[1 + i],
        )
        for i, (src, full) in enumerate(
            ((biases, bias_full), (gain, gain_full), (offset, offset_full))
        )
    ]
    for param in params:
        param.first()
    held = tokens.shape[1]
    for m in range(tokens.shape[0]):
        pick_out[m * held : (m + 1) * held] = leaving_slots(
            to_owner[m : m + 1], held // sends, rows, sends
        )
    send_slots(0, lambda m: (tokens[m].astype(F32) + time_embed[m].astype(F32)).astype(BF))
    lse[...] = jnp.zeros_like(lse)
    first_ag = RowGather(lk, local_width, ag_send, ag_recv, by_columns=True)
    for half in range(HALVES):
        wg.start(half)
    for half in range(3 * HALVES):
        wg.own_first(half)
    given[lk.c] = from_owner[...]
    give.wait_recv()
    give.wait_send()
    for k in range(packs):
        m = pl.ds(lk.c * packs + k, 1)
        row = jnp.concatenate([given[c, m] for c in range(2)], axis=1)
        pick_in[k * rows : (k + 1) * rows] = coming_slots(
            row, arrived.shape[1], held, sends
        )
    for param in params:
        param.last()
    save(gain_full, out_gain)
    save(pick_out, out_pick_out)
    save(pick_in, out_pick_in)
    swaps[0].last()
    for k in range(packs):
        act[0, k, :, my_cols] = placed_rows(0, k)
        first_ag.first(act.at[0, k], k)
    for k in range(packs):
        first_ag.second(act.at[0, k], k)
    weights_next(0)
    for k in range(packs):
        first_ag.last(act.at[0, k], k)
        u[k] = act[0, k, my_rows].astype(F32)
        save(act.at[0, k], out_act.at[0, k])

    def project(layer, k):
        for j in range(3):
            cols = slice(j * heads_width, (j + 1) * heads_width)
            acc = dot(act[layer, k], w[3 * layer, :, cols], NN)
            if j != 1:
                acc = acc + biases[layer, j // 2 : j // 2 + 1]
            qkv[layer, k, :, cols] = acc.astype(BF)
        save(qkv.at[layer, k], out_qkv.at[layer, k])

    def attention(layer, k):
        same_seq = same_sequence(seg, lk.c * packs + k)
        for head in range(heads_width // HD):
            cols = [slice(j * heads_width + head * HD, j * heads_width + (head + 1) * HD) for j in range(3)]
            scores = masked_scores(qkv[layer, k, :, cols[0]], qkv[layer, k, :, cols[1]], same_seq)
            top = jnp.max(scores, axis=1, keepdims=True)
            weighted = jnp.exp2(scores - top)
            total = jnp.sum(weighted, axis=1, keepdims=True)
            lse[layer, k, :, head : head + 1] = top + jnp.log2(total)
            probs = (weighted * (1.0 / total)).astype(BF)
            att[layer, k, :, cols[0]] = dot(probs, qkv[layer, k, :, cols[2]], NN).astype(BF)
        save(lse.at[layer, k], out_lse.at[layer, k])
        save(att.at[layer, k], out_att.at[layer, k])
        for j in range(width // 256):
            cols = slice(j * 256, (j + 1) * 256)
            acc = dot(att[layer, k], w[3 * layer, cols, 3 * heads_width :], NT)
            store_part(part, k, cols, acc, mine)
        rs.first(k)

    def normalize(layer, which, k, resid):
        mean = jnp.mean(resid, axis=1, keepdims=True)
        centred = resid - mean
        scale = lax.rsqrt(jnp.mean(centred * centred, axis=1, keepdims=True) + EPS)
        normed = centred * scale
        nrm[layer, which, k] = normed
        std[layer, which, k] = jnp.broadcast_to(scale, std.shape[3:])
        save(nrm.at[layer, which, k], out_nrm.at[layer, which, k])
        save(std.at[layer, which, k], out_std.at[layer, which, k])
        return (
            normed * gain_full[layer, which : which + 1] + offset_full[layer, which : which + 1]
        )

    def norm_one(layer, k):
        hidden = normalize(layer, 0, k, u[k] + rs.last(k) + bias_full[layer, 2:3])
        h[k] = hidden
        hid[layer, k, my_rows] = hidden.astype(BF)
        ag.first(hid.at[layer, k], k)

    def expand(layer, k):
        def tile(j, carry):
            cols = pl.ds(pl.multiple_of(j * 256, 256), 256)
            acc = dot(hid[layer, k], w[3 * layer + 1, :, cols], NN) + up_bias[layer : layer + 1, cols]
            value, slope = gelu_pair(acc)
            glu[layer, k, :, cols] = value.astype(BF)
            dglu[layer, k, :, cols] = slope.astype(BF)
            return carry

        lax.fori_loop(0, width // 256, tile, 0)
        save(glu.at[layer, k], out_glu.at[layer, k])
        save(dglu.at[layer, k], out_dglu.at[layer, k])

    def contract(layer, k):
        def tile(j, carry):
            cols = pl.ds(pl.multiple_of(j * 256, 256), 256)
            acc = dot(glu[layer, k], w[3 * layer + 2, cols, :], NT)
            store_part(part, k, cols, acc, mine)
            return carry

        lax.fori_loop(0, width // 256, tile, 0)
        rs.first(k)

    def norm_two(layer, k):
        out = normalize(layer, 1, k, h[k] + rs.last(k) + bias_full[layer, 3:4])
        u[k] = out
        if layer + 1 < layers:
            act[layer + 1, k, my_rows] = out.astype(BF)
            ag.first(act.at[layer + 1, k], k)
        else:
            u_low[k] = out.astype(BF)
            save(u_low.at[k], out_u.at[k])

    trade = Trade(
        lk, lambda t: cot_part.at[:, part_of(mine, t)],
        lambda t: cot_rows.at[:, :, part_of(local_width, t)], tr_send.at[0], tr_recv.at[0],
    )
    for layer in range(layers):
        base = 3 * layer
        more = layer + 1 < layers
        weights_ready(base)
        if layer:
            ag.last(act.at[layer, 0], 0)
            save(act.at[layer, 0], out_act.at[layer, 0])
        project(layer, 0)
        if layer:
            ag.second(act.at[layer, 1], 1)
        attention(layer, 0)
        weights_next(base + 1)
        if layer:
            ag.last(act.at[layer, 1], 1)
            save(act.at[layer, 1], out_act.at[layer, 1])
        project(layer, 1)
        rs.second(0)
        attention(layer, 1)
        norm_one(layer, 0)
        rs.second(1)
        ag.second(hid.at[layer, 0], 0)
        weights_next(base + 2)
        norm_one(layer, 1)
        weights_ready(base + 1)
        ag.last(hid.at[layer, 0], 0)
        save(hid.at[layer, 0], out_hid.at[layer, 0])
        expand(layer, 0)
        ag.second(hid.at[layer, 1], 1)
        if not more:
            send_slots(1, lambda m: cot[m])
        ag.last(hid.at[layer, 1], 1)
        save(hid.at[layer, 1], out_hid.at[layer, 1])
        expand(layer, 1)
        weights_ready(base + 2)
        contract(layer, 0)
        contract(layer, 1)
        rs.second(0)
        weights_next(base + 3)
        if not more:
            swaps[1].last()
            for k in range(packs):
                cot_part[k] = placed_rows(1, k)
            trade.first()
        norm_two(layer, 0)
        rs.second(1)
        if more:
            ag.second(act.at[layer + 1, 0], 0)
        norm_two(layer, 1)
    trade.last()
    save(cot_rows, out_cot)
    for part in range(chunks * HALVES):
        wg.drain(part)
    for swap in swaps:
        swap.drain()
    for copy in pending:
        copy.wait()


def forward(
    tokens, time_embed, cot, to_owner, from_owner, seg, shard, biases, gain, offset, up_bias
):
    rows = seg.shape[1]
    packs = tokens.shape[0] // lax.axis_size("ctx")
    width = shard.shape[2]
    local_width = tokens.shape[2]
    chunks = shard.shape[0]
    layers = chunks // 3
    mine = rows // 4
    heads = biases.shape[2]
    fs, cx = lax.axis_size("fsdp"), lax.axis_size("ctx")
    groups = fs * cx
    sends = tokens.shape[1] // fs
    parts = chunks * HALVES
    shapes = dict(
        w=((chunks, width, width), BF),
        act=((layers, packs, rows, width), BF),
        qkv=((layers, packs, rows, 3 * heads), BF),
        att=((layers, packs, rows, heads), BF),
        nrm=((layers, 2, packs, mine, width), F32),
        std=((layers, 2, packs, mine, 128), F32),
        hid=((layers, packs, rows, width), BF),
        glu=((layers, packs, rows, width), BF),
        dglu=((layers, packs, rows, width), BF),
        lse=((layers, packs, rows, 128), F32),
        u=((packs, mine, width), F32),
    )
    outs = {name: jax.ShapeDtypeStruct(*shape) for name, shape in shapes.items()}
    outs["u"] = jax.ShapeDtypeStruct((packs, mine, width), BF)
    outs["cot"] = jax.ShapeDtypeStruct((packs, mine, width), BF)
    outs["gain"] = jax.ShapeDtypeStruct((layers, 2, width), F32)
    given = tokens.shape[0] * tokens.shape[1]
    outs["pick_out"] = jax.ShapeDtypeStruct((given, tokens.shape[1]), BF)
    outs["pick_in"] = jax.ShapeDtypeStruct((packs * rows, rows), BF)
    copies = chunks + layers * packs * 11 + packs + 4
    dma = pltpu.SemaphoreType.DMA
    whole = pl.BlockSpec(memory_space=pl.ANY)
    vmem = pl.BlockSpec(memory_space=pltpu.VMEM)
    return pl.pallas_call(
        forward_kernel,
        in_specs=[vmem] * 6 + [whole] + [vmem] * 4,
        out_specs=[whole] * len(outs),
        out_shape=list(outs.values()),
        scratch_shapes=[pltpu.VMEM(*shape) for shape in shapes.values()]
        + [
            pltpu.VMEM((packs, mine, width), F32),
            pltpu.VMEM((packs, 2, 2, mine, width), BF),
            pltpu.VMEM((packs, 2, mine, width), BF),
            pltpu.VMEM((packs, mine, width), BF),
            pltpu.VMEM((packs, mine, width), BF),
            pltpu.VMEM((2, groups, packs * sends, local_width), BF),
            pltpu.VMEM((2, groups, packs * sends, local_width), BF),
            pltpu.VMEM((packs, rows, local_width), BF),
            pltpu.VMEM((packs, mine, width), BF),
            pltpu.VMEM((packs, mine, width), BF),
            pltpu.VMEM((layers, 4, width), F32),
            pltpu.VMEM((layers, 2, width), F32),
            pltpu.VMEM((layers, 2, width), F32),
            pltpu.VMEM((given, tokens.shape[1]), BF),
            pltpu.VMEM((packs * rows, rows), BF),
            pltpu.VMEM((2,) + from_owner.shape, jnp.int32),
            dma((copies,)),
            dma((packs, 2)), dma((packs, 2)), dma((packs, 3)), dma((packs, 3)),
            dma((parts, fs)), dma((parts, fs)), dma((parts, fs)), dma((parts, fs)),
            dma((parts,)),
            dma((2, 2, fs)), dma((2, 2, fs)), dma((4, 3)), dma((4, 3)), dma((2,)),
        ],
        compiler_params=pltpu.CompilerParams(
            collective_id=0, has_side_effects=True, vmem_limit_bytes=60 << 20
        ),
        name="forward",
    )(
        tokens, time_embed, cot, to_owner, from_owner, seg, shard, biases, gain, offset, up_bias
    )


class GradScatter:
    def __init__(self, lk, grad, from_x, from_z, relayed, x_send, x_recv, z_send, z_recv):
        self.lk, self.grad, self.from_x, self.from_z = lk, grad, from_x, from_z
        self.relayed = relayed
        self.x_send, self.x_recv, self.z_send, self.z_recv = x_send, x_recv, z_send, z_recv
        self.rows = from_x.shape[2]

    def block(self, chunk, step, c):
        f = lax.rem(self.lk.f + step, self.lk.fs)
        first = pl.multiple_of((f * self.lk.cx + c) * self.rows, self.rows)
        return self.grad.at[chunk, pl.ds(first, self.rows)]

    def x_copy(self, chunk, step):
        return remote(
            self.block(chunk, step, 1 - self.lk.c), self.from_x.at[chunk, step],
            self.x_send.at[chunk, step], self.x_recv.at[chunk, step], self.lk.across,
        )

    def z_copy(self, chunk, step):
        slot = self.lk.fs - step
        return remote(
            self.block(chunk, step, self.lk.c), self.from_z.at[chunk, slot - 1],
            self.z_send.at[chunk, step], self.z_recv.at[chunk, slot], self.lk.away(step),
        )

    def each(self, first, work, last=None):
        def body(step, carry):
            work(step)
            return carry

        lax.fori_loop(first, self.lk.fs if last is None else last, body, 0)

    def far(self, step):
        return jnp.abs(lax.rem(self.lk.f + step, self.lk.fs) - self.lk.f) == 3

    def inner(self):
        return (self.lk.f == 1) | (self.lk.f == 2)

    def relay(self, chunk, step):
        f = self.lk.f
        return remote(
            self.block(chunk, step, self.lk.c), self.relayed.at[chunk],
            self.z_send.at[chunk, 0], self.z_recv.at[chunk, 0],
            (lax.select(f == 0, 1, 2), self.lk.c, self.lk.t),
        )

    def first(self, chunk):
        if self.lk.fs == 4:
            for step in (1, 3, 2):
                self.x_copy(chunk, step).start()
        else:
            self.each(1, lambda step: self.x_copy(chunk, step).start())
        self.x_copy(chunk, 0).start()

    def second(self, chunk, part):
        def work(step):
            self.x_copy(chunk, step).wait_recv()
            own = self.block(chunk, step, self.lk.c)
            own[...] = (own[...].astype(F32) + self.from_x[chunk, step].astype(F32)).astype(BF)
            if self.lk.fs == 4:
                pl.when(self.far(step))(self.relay(chunk, step).start)
                if step == 2:

                    @pl.when(self.inner())
                    def _():
                        self.relay(chunk, step).wait_recv()
                        own[...] = (
                            own[...].astype(F32) + self.relayed[chunk].astype(F32)
                        ).astype(BF)

                pl.when(jnp.logical_not(self.far(step)))(self.z_copy(chunk, step).start)
            else:
                self.z_copy(chunk, step).start()

        if self.lk.fs == 4:
            work((1, 3, 2)[part])
            return
        first, last = third(self.lk.fs, part)
        self.each(first, work, last)

    def last(self, chunk, out):
        self.x_copy(chunk, 0).wait_recv()
        out[...] = self.block(chunk, 0, self.lk.c)[...].astype(F32) + self.from_x[chunk, 0].astype(F32)

        def work(step):
            self.z_copy(chunk, self.lk.fs - step).wait_recv()
            out[...] = out[...] + self.from_z[chunk, step - 1].astype(F32)

        if self.lk.fs == 4:
            for step in (1, 2, 3):
                pl.when(jnp.logical_not(self.far(step)))(functools.partial(work, step))
        else:
            self.each(1, work)

    def drain(self, chunk):
        self.each(0, lambda step: self.x_copy(chunk, step).wait_send())
        if self.lk.fs == 4:
            for step in (1, 2, 3):
                pl.when(self.far(step))(self.relay(chunk, step).wait_send)
                pl.when(jnp.logical_not(self.far(step)))(self.z_copy(chunk, step).wait_send)
        else:
            self.each(1, lambda step: self.z_copy(chunk, step).wait_send())


def backward_kernel(
    up_in, u_in, pick_out, pick_in, act_in, w_in, qkv_in, att_in, nrm_in, std_in, hid_in, glu_in, dglu_in,
    lse_in, gain, seg,
    out_qkv, out_out, out_up, out_down, out_ret, out_sums,
    w, qkv, att, nrm, std, hid, glu, dglu, lse, up, gtwo, gl, gm, gup, gqkv, gatt,
    part, from_sib, to_peer, from_peer, grad, from_x, from_z, relayed, gsum, low, ret_in,
    out_vec, out_head, out_bias, vec_parts, sums,
    in_sem, out_sem, rs_send, rs_recv, ag_send, ag_recv, x_send, x_recv, z_send, z_recv,
    ex_send, ex_recv, tr_send, tr_recv, pick_sem,
):
    packs, rows, width = hid.shape
    layers = gain.shape[0]
    mine = rows // 4
    heads_width = att.shape[2]
    lk = Links()
    sources = dict(
        nrm1=lambda layer: (nrm_in.at[layer, 1], nrm.at[1]),
        std1=lambda layer: (std_in.at[layer, 1], std.at[1]),
        nrm0=lambda layer: (nrm_in.at[layer, 0], nrm.at[0]),
        std0=lambda layer: (std_in.at[layer, 0], std.at[0]),
        w2=lambda layer: (w_in.at[3 * layer + 2], w.at[2]),
        dglu=lambda layer: (dglu_in.at[layer], dglu),
        w1=lambda layer: (w_in.at[3 * layer + 1], w.at[1]),
        glu=lambda layer: (glu_in.at[layer], glu),
        hid=lambda layer: (hid_in.at[layer], hid),
        w0=lambda layer: (w_in.at[3 * layer], w.at[0]),
        qkv=lambda layer: (qkv_in.at[layer], qkv),
        lse=lambda layer: (lse_in.at[layer], lse),
        att=lambda layer: (att_in.at[layer], att),
        act=lambda layer: (act_in.at[layer], hid),
    )
    order = {name: index for index, name in enumerate(sources)}

    def fetch(name, layer):
        if layer >= 0:
            src, dst = sources[name](layer)
            pltpu.make_async_copy(src, dst, in_sem.at[order[name]]).start()

    def ready(name, layer):
        src, dst = sources[name](layer)
        pltpu.make_async_copy(src, dst, in_sem.at[order[name]]).wait()

    loads = [
        pltpu.make_async_copy(up_in, to_peer, in_sem.at[len(order)]),
        pltpu.make_async_copy(u_in, low, in_sem.at[len(order) + 1]),
    ]
    for load in loads:
        load.start()
    for name in sources:
        if name != "act":
            fetch(name, layers - 1)
    lk.barrier()
    rs = RowSum(lk, part, from_sib, to_peer, from_peer, rs_send, rs_recv)
    ag = RowGather(lk, mine, ag_send, ag_recv)
    gs = GradScatter(lk, grad, from_x, from_z, relayed, x_send, x_recv, z_send, z_recv)
    my_rows = pl.ds(pl.multiple_of(lk.t * mine, mine), mine)
    pending = []
    held = {}
    local_width = ret_in.shape[1]
    swap_rows = width // (lk.fs * lk.cx)
    sends = swap_rows // packs
    low_cols, next_cols, third_cols, last_cols = (
        slice(i * local_width, (i + 1) * local_width) for i in range(4)
    )

    class Return:
        def __init__(self, index, first, second, landed):
            self.index, self.first_buf, self.second_buf, self.landed = index, first, second, landed
            self.trade = Trade(
                lk, lambda t: low.at[:, :, part_of(local_width, t)],
                lambda t: gup.at[:, part_of(mine, t), low_cols],
                tr_send.at[index], tr_recv.at[index],
            )
            self.swap = Exchange(
                lk, lambda g: first.at[part_of(swap_rows, g), low_cols],
                lambda g: landed.at[part_of(swap_rows, g)], ex_send.at[index], ex_recv.at[index],
            )
            self.picks = [
                pltpu.make_async_copy(
                    pick_in, second.at[:, : 2 * local_width], pick_sem.at[index, 0]
                ),
                pltpu.make_async_copy(pick_out, second.at[:, third_cols], pick_sem.at[index, 1]),
            ]

        def load(self):
            for copy in self.picks:
                copy.start()

        def middle(self):
            self.trade.last()
            self.picks[0].wait()
            for k in range(packs):
                pick = self.second_buf[k * rows : (k + 1) * rows, : 2 * local_width]
                values = dot(pick, gup[k, :, low_cols], NN).astype(BF)
                for g in range(rows // sends):
                    first = g * swap_rows + k * sends
                    self.first_buf[first : first + sends, low_cols] = values[
                        g * sends : (g + 1) * sends
                    ]
            self.swap.first()

        def last(self):
            self.swap.last()
            self.picks[1].wait()
            given = pick_out.shape[1]
            for c in range(2):
                for k in range(packs):
                    m = c * packs + k
                    blocks = [
                        self.landed[
                            (2 * f + c) * swap_rows + k * sends :
                            (2 * f + c) * swap_rows + (k + 1) * sends
                        ]
                        for f in range(given // sends)
                    ]
                    pick = self.second_buf[m * given : (m + 1) * given, third_cols]
                    values = dot(pick, jnp.concatenate(blocks, axis=0), TN)
                    self.second_buf[m * given : (m + 1) * given, last_cols] = values.astype(BF)
            save(self.second_buf.at[:, last_cols], out_ret.at[self.index])
            self.saved = pending.pop()

        def finish(self):
            self.swap.drain()
            self.saved.wait()

    give_back = [
        Return(0, grad.at[0], grad.at[1], grad.at[0, :, next_cols]),
        Return(1, grad.at[3 * layers - 1], grad.at[3 * layers - 2], ret_in),
    ]
    vec_trade = Trade(
        lk, lambda t: out_vec.at[:, :, part_of(local_width, t)], lambda t: vec_parts.at[t],
        tr_send.at[2], tr_recv.at[2],
    )
    vec_swap = Exchange(
        lk, lambda g: sums.at[lk.g], lambda g: sums.at[g], ex_send.at[2], ex_recv.at[2],
        in_place=True,
    )

    def vec_middle():
        vec_trade.last()
        total = vec_parts[0]
        for t in range(1, 4):
            total = total + vec_parts[t]
        sums[lk.g, :, 0:6] = total
        sums[lk.g, :, 6:8] = out_head[...]
        for j in range(4):
            sums[lk.g, :, 8 + j : 9 + j] = out_bias[:, :, j * local_width : (j + 1) * local_width]
        vec_swap.first()

    def vec_last():
        vec_swap.last()

        def add(g, total):
            return total + sums[g]

        out_sums[...] = lax.fori_loop(1, sums.shape[0], add, sums[0])

    used = []

    def save(src, dst):
        copy = pltpu.make_async_copy(src, dst, out_sem.at[len(used)])
        copy.start()
        used.append(1)
        pending.append(copy)

    out_vec[...] = jnp.zeros_like(out_vec)
    out_head[...] = jnp.zeros_like(out_head)
    out_bias[...] = jnp.zeros_like(out_bias)

    def norm_back(layer, which, k, upstream):
        normed = nrm[which, k]
        scale = std[which, k][:, 0:1]
        out_vec[layer, 2 + which : 3 + which] += jnp.sum(upstream * normed, axis=0, keepdims=True)
        out_vec[layer, 4 + which : 5 + which] += jnp.sum(upstream, axis=0, keepdims=True)
        scaled = upstream * gain[layer, which : which + 1]
        first = jnp.mean(scaled, axis=1, keepdims=True)
        second = jnp.mean(scaled * normed, axis=1, keepdims=True)
        result = scale * (scaled - first - normed * second)
        out_vec[layer, which : which + 1] += jnp.sum(result, axis=0, keepdims=True)
        return result

    def norm_two(layer, k):
        result = norm_back(layer, 1, k, up[k])
        gtwo[k] = result
        gl[k, my_rows] = result.astype(BF)
        ag.first(gl.at[k], k)

    def norm_one(layer, k):
        result = norm_back(layer, 0, k, gtwo[k] + rs.last(k))
        up[k] = result
        gm[k, my_rows] = result.astype(BF)
        ag.first(gm.at[k], k)

    def tiles(work):
        def body(j, carry):
            work(pl.ds(pl.multiple_of(j * 256, 256), 256))
            return carry

        lax.fori_loop(0, width // 256, body, 0)

    def through_down(layer, k):
        def tile(cols):
            grad_gelu = dot(gl[k], w[2, :, cols], NN).astype(BF).astype(F32)
            result = (grad_gelu * dglu[k, :, cols].astype(F32)).astype(BF)
            gup[k, :, cols] = result
            out_bias[layer, :, cols] += jnp.sum(result.astype(F32), axis=0, keepdims=True)

        tiles(tile)

    def through_up(layer, k):
        tiles(lambda cols: store_part(part, k, cols, dot(gup[k], w[1, cols, :], NT), mine))
        rs.first(k)

    def through_out(k):
        gatt[k] = dot(gm[k], w[0, :, 3 * heads_width :], NN).astype(BF)

    def attention(layer, k):
        same_seq = same_sequence(seg, lk.c * packs + k)
        scale = 1.0 / math.sqrt(HD)
        for head in range(heads_width // HD):
            cols = [slice(j * heads_width + head * HD, j * heads_width + (head + 1) * HD) for j in range(3)]
            query, keys, values = (qkv[k, :, c] for c in cols)
            grads = gatt[k, :, cols[0]]
            probs = jnp.exp2(masked_scores(query, keys, same_seq) - lse[k, :, head : head + 1])
            grad_probs = dot(grads, values, NT)
            delta = jnp.sum(probs * grad_probs, axis=1, keepdims=True)
            grad_scores = (probs * (grad_probs - delta)).astype(BF)
            gqkv[k, :, cols[0]] = (dot(grad_scores, keys, NN) * scale).astype(BF)
            gqkv[k, :, cols[1]] = (dot(grad_scores, query, TN) * scale).astype(BF)
            gqkv[k, :, cols[2]] = dot(probs.astype(BF), grads, TN).astype(BF)
        for j in range(2):
            cols = slice(2 * j * heads_width, (2 * j + 1) * heads_width)
            out_head[layer, j : j + 1] += jnp.sum(
                gqkv[k, :, cols].astype(F32), axis=0, keepdims=True
            )

    def through_qkv(k):
        tiles(
            lambda cols: store_part(
                part, k, cols, dot(gqkv[k], w[0, cols, : 3 * heads_width], NT), mine
            )
        )
        rs.first(k)

    def product(left, right, cols, right_cols=slice(None)):
        total = dot(left[0, :, cols], right[0, :, right_cols], TN)
        for k in range(1, packs):
            total = total + dot(left[k, :, cols], right[k, :, right_cols], TN)
        return total.astype(BF)

    def down_grad(layer):
        def tile(cols):
            grad[3 * layer + 2, cols, :] = product(gl, glu, cols)

        tiles(tile)
        gs.first(3 * layer + 2)

    def up_grad(layer):
        def tile(cols):
            grad[3 * layer + 1, cols, :] = product(hid, gup, cols)

        tiles(tile)
        gs.first(3 * layer + 1)

    def first_grad(layer):
        def tile(cols):
            grad[3 * layer, cols, : 3 * heads_width] = product(hid, gqkv, cols)
            grad[3 * layer, cols, 3 * heads_width :] = product(gm, att, cols)

        tiles(tile)
        gs.first(3 * layer)

    def emit(layer, which):
        chunk = 3 * layer + which
        out = gsum.at[0]
        while held.get(0):
            held[0].pop().wait()
        gs.last(chunk, out)
        held[0] = []
        saved = len(pending)
        if which == 2:
            save(out, out_down.at[layer])
        elif which == 1:
            save(out, out_up.at[layer])
        else:
            for c in range(3):
                save(out.at[:, c * heads_width : (c + 1) * heads_width], out_qkv.at[layer, c])
            save(out.at[:, 3 * heads_width :], out_out.at[layer])
        held[0] = [pending.pop() for _ in range(len(pending) - saved)]

    give_back[0].load()
    for load in loads:
        load.wait()
    top = layers - 1
    ready("nrm1", top)
    ready("std1", top)
    for k in range(packs):
        up[k] = to_peer[k].astype(F32)
        norm_two(top, k)
    give_back[0].trade.first()
    fetch("nrm1", top - 1)
    fetch("std1", top - 1)
    def summed(chunk, *parts):
        for part in parts:
            gs.second(chunk, part)

    for layer in reversed(range(layers)):
        base = 3 * layer
        later = layer < top
        ag.second(gl.at[0], 0)
        if layer == top:
            give_back[0].middle()
        ready("w2", layer)
        ready("dglu", layer)
        ag.last(gl.at[0], 0)
        through_down(layer, 0)
        ag.second(gl.at[1], 1)
        ready("w1", layer)
        through_up(layer, 0)
        if later:
            summed(base + 3, 0)
        ag.last(gl.at[1], 1)
        through_down(layer, 1)
        fetch("w2", layer - 1)
        fetch("dglu", layer - 1)
        rs.second(0)
        through_up(layer, 1)
        fetch("w1", layer - 1)
        ready("glu", layer)
        down_grad(layer)
        fetch("glu", layer - 1)
        rs.second(1)
        ready("nrm0", layer)
        ready("std0", layer)
        norm_one(layer, 0)
        if later:
            summed(base + 3, 1)
        ready("hid", layer)
        up_grad(layer)
        fetch("act", layer)
        ag.second(gm.at[0], 0)
        if later:
            summed(base + 3, 2)
        else:
            summed(base + 2, 0)
        norm_one(layer, 1)
        fetch("nrm0", layer - 1)
        fetch("std0", layer - 1)
        ready("w0", layer)
        ready("qkv", layer)
        ready("lse", layer)
        ag.last(gm.at[0], 0)
        through_out(0)
        if later:
            summed(base + 2, 0)
        else:
            summed(base + 2, 1)
        ag.second(gm.at[1], 1)
        attention(layer, 0)
        through_qkv(0)
        if later:
            summed(base + 2, 1)
        else:
            summed(base + 2, 2)
            summed(base + 1, 0)
        ag.last(gm.at[1], 1)
        through_out(1)
        rs.second(0)
        attention(layer, 1)
        fetch("qkv", layer - 1)
        fetch("lse", layer - 1)
        through_qkv(1)
        fetch("w0", layer - 1)
        rs.second(1)
        ready("att", layer)
        ready("act", layer)
        first_grad(layer)
        if later:
            summed(base + 2, 2)
        else:
            summed(base + 1, 1)
        if layer:
            fetch("att", layer - 1)
            fetch("hid", layer - 1)
        for k in range(packs):
            up[k] = rs.last(k) + up[k]
            if layer:
                if k == 0:
                    ready("nrm1", layer - 1)
                    ready("std1", layer - 1)
                norm_two(layer - 1, k)
            else:
                low[k] = up[k].astype(BF)
        if layer == top:
            summed(base + 1, 2)
            give_back[0].last()
            give_back[0].finish()
        if layer:
            fetch("nrm1", layer - 2)
            fetch("std1", layer - 2)
    give_back[1].trade.first()
    vec_trade.first()
    summed(1, 0)
    emit(1, 2)
    emit(1, 1)
    for chunk in (3 * layers - 1, 3 * layers - 2):
        gs.drain(chunk)
    give_back[1].load()
    give_back[1].middle()
    vec_middle()
    summed(1, 1, 2)
    emit(1, 0)
    summed(0, 0, 1, 2)
    give_back[1].last()
    vec_last()
    emit(0, 2)
    emit(0, 1)
    emit(0, 0)
    for chunk in range(3 * layers - 2):
        gs.drain(chunk)
    give_back[1].finish()
    vec_swap.drain()
    for copy in pending + sum(held.values(), []):
        copy.wait()


def backward(upstream, u, pick_out, pick_in, saved, gain, seg):
    full_w, o_act, o_qkv, o_att, o_nrm, o_std, o_hid, o_glu, o_dglu, o_lse = saved
    layers, packs, rows, width = o_act.shape
    mine = rows // 4
    chunks = 3 * layers
    heads = o_att.shape[3]
    local_width = width // 4
    fs, cx = lax.axis_size("fsdp"), lax.axis_size("ctx")
    groups = fs * cx
    shard = width // groups
    given = pick_out.shape[0]
    outs = [
        jax.ShapeDtypeStruct((layers, 3, shard, heads), F32),
        jax.ShapeDtypeStruct((layers, shard, heads), F32),
        jax.ShapeDtypeStruct((layers, shard, width), F32),
        jax.ShapeDtypeStruct((layers, shard, width), F32),
        jax.ShapeDtypeStruct((2, given, local_width), BF),
        jax.ShapeDtypeStruct((layers, 12, local_width), F32),
    ]
    dma = pltpu.SemaphoreType.DMA
    whole = pl.BlockSpec(memory_space=pl.ANY)
    vmem = pl.BlockSpec(memory_space=pltpu.VMEM)
    full = pltpu.VMEM((packs, rows, width), BF)
    rowed = pltpu.VMEM((packs, mine, width), F32)
    return pl.pallas_call(
        backward_kernel,
        in_specs=[whole] * 14 + [vmem] * 2,
        out_specs=[whole] * 5 + [vmem],
        out_shape=outs,
        scratch_shapes=[
            pltpu.VMEM((3, width, width), BF),
            pltpu.VMEM((packs, rows, 3 * heads), BF),
            pltpu.VMEM((packs, rows, heads), BF),
            pltpu.VMEM((2, packs, mine, width), F32),
            pltpu.VMEM((2, packs, mine, 128), F32),
            full, full, full,
            pltpu.VMEM((packs, rows, 128), F32),
            rowed, rowed,
            full, full, full,
            pltpu.VMEM((packs, rows, 3 * heads), BF),
            pltpu.VMEM((packs, rows, heads), BF),
            pltpu.VMEM((packs, 2, 2, mine, width), BF),
            pltpu.VMEM((packs, 2, mine, width), BF),
            pltpu.VMEM((packs, mine, width), BF),
            pltpu.VMEM((packs, mine, width), BF),
            pltpu.VMEM((chunks, width, width), BF),
            pltpu.VMEM((chunks, fs, shard, width), BF),
            pltpu.VMEM((chunks, fs - 1, shard, width), BF),
            pltpu.VMEM((chunks if fs == 4 else 1, shard, width), BF),
            pltpu.VMEM((1, shard, width), F32),
            pltpu.VMEM((packs, mine, width), BF),
            pltpu.VMEM((given, local_width), BF),
            pltpu.VMEM((layers, 6, width), F32),
            pltpu.VMEM((layers, 2, heads), F32),
            pltpu.VMEM((layers, 1, width), F32),
            pltpu.VMEM((4, layers, 6, local_width), F32),
            pltpu.VMEM((groups, layers, 12, local_width), F32),
            dma((16,)), dma((packs + 6 * layers + 2,)),
            dma((packs, 2)), dma((packs, 2)), dma((packs, 3)), dma((packs, 3)),
            dma((chunks, fs)), dma((chunks, fs)), dma((chunks, fs)), dma((chunks, fs)),
            dma((3, 2, fs)), dma((3, 2, fs)), dma((3, 3)), dma((3, 3)), dma((2, 2)),
        ],
        compiler_params=pltpu.CompilerParams(
            collective_id=1, has_side_effects=True, vmem_limit_bytes=62 << 20
        ),
        name="backward",
    )(
        upstream, u, pick_out, pick_in, o_act, full_w, o_qkv, o_att, o_nrm, o_std, o_hid,
        o_glu, o_dglu, o_lse, gain, seg,
    )


def local(
    tokens, time_embed, cotangent, segment_ids, to_owner, from_owner,
    w_qkv, w_out, w_up, w_down, biases, norm_gain, norm_bias, up_bias,
):
    micro, rows, width = tokens.shape
    layers = w_qkv.shape[0]
    shard = jnp.concatenate(
        [w_qkv[:, 0], w_qkv[:, 1], w_qkv[:, 2], w_out, w_up, w_down], axis=2
    )
    shard = shard.reshape(layers, shard.shape[1], 3, -1).transpose(0, 2, 1, 3)
    shard = shard.reshape(layers * 3, shard.shape[2], -1)
    *saved, u, upstream, gain, pick_out, pick_in = forward(
        tokens, time_embed, cotangent, to_owner, from_owner, segment_ids, shard, biases,
        norm_gain, norm_bias, up_bias,
    )
    g_qkv, g_out, g_up, g_down, returned, sums = backward(
        upstream, u, pick_out, pick_in, saved, gain, segment_ids
    )
    returned = returned.reshape(2, micro, rows, width).astype(F32)
    return (
        returned[0],
        returned[1],
        g_qkv, g_out, g_up, g_down,
        jnp.concatenate([sums[:, 6:8], sums[:, 0:2]], axis=1),
        sums[:, 2:4],
        sums[:, 4:6],
        sums[:, 8:12].reshape(layers, -1),
    )


def solution(mesh):
    wide = P(None, GRP, "tp")
    vec = P(None, None, "tp")
    qkv = P(None, None, GRP, "tp")
    owner = P(None, GRP)
    return jax.shard_map(
        local,
        mesh=mesh,
        in_specs=(
            wide, wide, wide, P(None, "fsdp"), owner, owner, qkv, wide, wide, wide,
            vec, vec, vec, P(None, "tp"),
        ),
        out_specs=(wide, wide, qkv, wide, wide, wide, vec, vec, vec, P(None, "tp")),
        check_vma=False,
    )
```

```python
import functools
import math

import jax
import jax.numpy as jnp
from jax import lax
from jax.experimental import pallas as pl
from jax.experimental.pallas import tpu as pltpu
from jax.sharding import PartitionSpec as P

HD = 64
NEG = -1e30
EPS = 1e-05
BF = jnp.bfloat16
F32 = jnp.float32
GRP = ("fsdp", "ctx")


def dot(left, right, dims):
    return lax.dot_general(left, right, (dims, ((), ())), preferred_element_type=F32)


NN = ((1,), (0,))
NT = ((1,), (1,))
TN = ((0,), (0,))

MESH = pl.DeviceIdType.MESH
LOG2E = 1.4426950408889634
HALVES = 1


def gelu_pair(values):
    bell = jnp.exp2(values * values * (-0.5 * LOG2E))
    t = 1.0 / (1.0 + (0.3275911 * math.sqrt(0.5)) * jnp.abs(values))
    poly = t * (
        0.127414796 + t * (-0.142248368 + t * (0.7107068705 + t * (-0.7265760135 + t * 0.5307027145)))
    )
    tail = poly * bell
    phi = jnp.where(values < 0, tail, 1.0 - tail)
    return values * phi, phi + values * bell * (1.0 / math.sqrt(2.0 * math.pi))


class Links:
    def __init__(self):
        self.fs, self.cx = lax.axis_size("fsdp"), lax.axis_size("ctx")
        self.f, self.c, self.t = (lax.axis_index(a) for a in ("fsdp", "ctx", "tp"))
        self.core, self.chip = lax.rem(self.t, 2), self.t // 2
        self.sib_t = self.t + 1 - 2 * self.core
        self.peer_t = lax.rem(self.t + 2, 4)
        self.sib = (self.f, self.c, self.sib_t)
        self.peer = (self.f, self.c, self.peer_t)
        self.diag_t = 3 - self.t
        self.diag = (self.f, self.c, self.diag_t)
        self.across = (self.f, 1 - self.c, self.t)
        self.g = self.f * self.cx + self.c

    def away(self, step, c=None):
        return (lax.rem(self.f + step, self.fs), self.c if c is None else c, self.t)

    def barrier(self):
        sem = pltpu.get_barrier_semaphore()
        for target in (self.sib, self.peer, self.diag, self.across):
            pl.semaphore_signal(sem, inc=1, device_id=target, device_id_type=MESH)

        def greet(step, carry):
            for c in (self.c, 1 - self.c):
                pl.semaphore_signal(
                    sem, inc=1, device_id=self.away(step, c), device_id_type=MESH
                )
            return carry

        lax.fori_loop(1, self.fs, greet, 0)
        pl.semaphore_wait(sem, 2 + 2 * self.fs)


def remote(src, dst, send, recv, target):
    return pltpu.make_async_remote_copy(
        src_ref=src, dst_ref=dst, send_sem=send, recv_sem=recv,
        device_id=target, device_id_type=MESH,
    )


class RowSum:
    def __init__(self, lk, part, from_sib, to_peer, from_peer, send, recv):
        self.lk, self.part, self.from_sib = lk, part, from_sib
        self.to_peer, self.from_peer, self.send, self.recv = to_peer, from_peer, send, recv

    def sib_copy(self, k):
        return remote(
            self.part.at[k, 1 - self.lk.core], self.from_sib.at[k],
            self.send.at[k, 0], self.recv.at[k, 0], self.lk.sib,
        )

    def peer_copy(self, k):
        return remote(
            self.to_peer.at[k], self.from_peer.at[k],
            self.send.at[k, 1], self.recv.at[k, 1], self.lk.peer,
        )

    def first(self, k):
        self.sib_copy(k).start()

    def second(self, k):
        self.sib_copy(k).wait_recv()
        other = 1 - self.lk.chip
        total = self.part[k, self.lk.core, other].astype(F32) + self.from_sib[k, other].astype(F32)
        self.to_peer[k] = total.astype(BF)
        self.peer_copy(k).start()

    def last(self, k):
        own = self.part[k, self.lk.core, self.lk.chip].astype(F32)
        own = own + self.from_sib[k, self.lk.chip].astype(F32)
        self.peer_copy(k).wait_recv()
        self.sib_copy(k).wait_send()
        self.peer_copy(k).wait_send()
        return own + self.from_peer[k].astype(F32)


class RowGather:
    def __init__(self, lk, rows, send, recv, by_columns=False):
        self.lk, self.rows, self.send, self.recv = lk, rows, send, recv
        self.by_columns = by_columns

    def block(self, ref, index):
        part = part_of(self.rows, index)
        return ref.at[:, part] if self.by_columns else ref.at[part]

    def copy(self, ref, k, which):
        index = self.lk.t if which < 2 else self.lk.peer_t
        part = self.block(ref, index)
        target = self.lk.peer if which == 0 else self.lk.sib
        return remote(part, part, self.send.at[k, which], self.recv.at[k, which], target)

    def first(self, ref, k):
        self.copy(ref, k, 0).start()
        self.copy(ref, k, 1).start()

    def second(self, ref, k):
        self.copy(ref, k, 0).wait_recv()
        self.copy(ref, k, 2).start()

    def last(self, ref, k):
        self.copy(ref, k, 1).wait_recv()
        self.copy(ref, k, 2).wait_recv()
        for which in range(3):
            self.copy(ref, k, which).wait_send()


class Exchange:
    def __init__(self, lk, src, dst, send, recv, in_place=False):
        self.lk, self.src, self.dst, self.send, self.recv = lk, src, dst, send, recv
        self.in_place = in_place

    def copy(self, other, step):
        lk = self.lk
        c = 1 - lk.c if other else lk.c
        target = lax.rem(lk.f + step, lk.fs) * lk.cx + c
        return remote(
            self.src(target), self.dst(lk.g), self.send.at[other, step],
            self.recv.at[other, lax.rem(lk.fs - step, lk.fs)], lk.away(step, c),
        )

    def each(self, work):
        def body(step, carry):
            work(1, step)
            work(0, step)
            return carry

        work(1, 0)
        lax.fori_loop(1, self.lk.fs, body, 0)

    def first(self):
        self.each(lambda other, step: self.copy(other, step).start())
        if not self.in_place:
            self.dst(self.lk.g)[...] = self.src(self.lk.g)[...]

    def last(self):
        def work(other, step):
            self.copy(other, lax.rem(self.lk.fs - step, self.lk.fs)).wait_recv()

        self.each(work)

    def drain(self):
        self.each(lambda other, step: self.copy(other, step).wait_send())


class Trade:
    def __init__(self, lk, src, dst, send, recv):
        self.lk, self.src, self.dst, self.send, self.recv = lk, src, dst, send, recv

    def copies(self):
        lk = self.lk
        pairs = ((lk.peer_t, lk.peer), (lk.diag_t, lk.diag), (lk.sib_t, lk.sib))
        return [
            remote(self.src(index), self.dst(lk.t), self.send.at[i], self.recv.at[i], target)
            for i, (index, target) in enumerate(pairs)
        ]

    def first(self):
        for copy in self.copies():
            copy.start()
        self.dst(self.lk.t)[...] = self.src(self.lk.t)[...]

    def last(self):
        for copy in self.copies():
            copy.wait_recv()
            copy.wait_send()


def third(count, part):
    return 1 + (count - 1) * part // 3, 1 + (count - 1) * (part + 1) // 3


def part_of(size, index):
    return pl.ds(pl.multiple_of(index * size, size), size)


def stored_slots(dst, values, first, count, sends, block):
    for i in range(count):
        dst(i)[block * sends : (block + 1) * sends] = values[
            (first + i) * sends : (first + i + 1) * sends
        ].astype(BF)


def one_hot(rows, values):
    return (lax.broadcasted_iota(jnp.int32, (rows, values.shape[1]), 0) == values).astype(BF)


def counts_before(present):
    size = present.shape[1]
    earlier = lax.broadcasted_iota(jnp.int32, (size, size), 0) < lax.broadcasted_iota(
        jnp.int32, (size, size), 1
    )
    return dot(present, earlier.astype(BF), NN)


def leaving_slots(to_row, packs_total, pack, sends):
    groups = one_hot(packs_total, to_row // pack)
    base = lax.broadcasted_iota(jnp.int32, groups.shape, 0) * sends
    slot = (counts_before(groups) + base.astype(F32)) * groups.astype(F32)
    return one_hot(to_row.shape[1], jnp.sum(slot, axis=0, keepdims=True).astype(jnp.int32))


def coming_slots(given, groups, rows, sends):
    source = one_hot(groups, given // rows)
    within = one_hot(rows, lax.rem(given, rows))
    ranks = counts_before(dot(source, within, NT).astype(BF)).astype(BF)
    base = lax.broadcasted_iota(jnp.int32, source.shape, 0) * sends
    slot = (dot(ranks, within, NN) + base.astype(F32)) * source.astype(F32)
    return one_hot(groups * sends, jnp.sum(slot, axis=0, keepdims=True).astype(jnp.int32))


def same_sequence(seg_ref, row):
    member = one_hot(8, lax.rem(seg_ref[pl.ds(row, 1)], 8))
    return dot(member, member, TN) > 0.5


class WeightGather:
    def __init__(self, lk, shard, full, z_send, z_recv, x_send, x_recv, own):
        self.lk, self.shard, self.full = lk, shard, full
        self.z_send, self.z_recv, self.x_send, self.x_recv = z_send, z_recv, x_send, x_recv
        self.own = own
        self.rows = shard.shape[1]
        self.cols = shard.shape[2] // HALVES

    def part(self, chunk):
        return slice(chunk % HALVES * self.cols, (chunk % HALVES + 1) * self.cols)

    def mine(self, chunk):
        return self.shard.at[chunk // HALVES, :, self.part(chunk)]

    def block(self, chunk, f, c):
        rows = part_of(self.rows, f * self.lk.cx + c)
        return self.full.at[chunk // HALVES, rows, self.part(chunk)]

    def z_copy(self, chunk, step):
        return remote(
            self.mine(chunk), self.block(chunk, self.lk.f, self.lk.c),
            self.z_send.at[chunk, step], self.z_recv.at[chunk, self.lk.fs - step],
            self.lk.away(step),
        )

    def far(self, step):
        return jnp.abs(lax.rem(self.lk.f + step, self.lk.fs) - self.lk.f) == 3

    def relay(self, chunk):
        f = self.lk.f
        part = self.block(chunk, 3 * (2 - f), self.lk.c)
        return remote(
            part, part, self.z_send.at[chunk, 0], self.z_recv.at[chunk, 5 - 2 * f],
            (3 * (f - 1), self.lk.c, self.lk.t),
        )

    def inner(self):
        return (self.lk.f == 1) | (self.lk.f == 2)

    def x_copy(self, chunk, step):
        f = lax.rem(self.lk.f + step, self.lk.fs)
        part = self.block(chunk, f, self.lk.c)
        return remote(
            part, part, self.x_send.at[chunk, step], self.x_recv.at[chunk, step], self.lk.across
        )

    def x_own(self, chunk):
        return remote(
            self.mine(chunk), self.block(chunk, self.lk.f, self.lk.c),
            self.x_send.at[chunk, 0], self.x_recv.at[chunk, 0], self.lk.across,
        )

    def own_copy(self, chunk):
        return pltpu.make_async_copy(
            self.mine(chunk), self.block(chunk, self.lk.f, self.lk.c), self.own.at[chunk]
        )

    def each(self, first, work):
        def body(step, carry):
            work(step)
            return carry

        lax.fori_loop(first, self.lk.fs, body, 0)

    def own_first(self, chunk):
        self.own_copy(chunk).start()
        self.x_own(chunk).start()

    def start(self, chunk):
        if self.lk.fs == 4:
            for step in (2, 1, 3):
                pl.when(jnp.logical_not(self.far(step)))(self.z_copy(chunk, step).start)
        else:
            self.each(1, lambda step: self.z_copy(chunk, step).start())

    def forward(self, chunk):
        def work(step):
            self.z_copy(chunk, self.lk.fs - step).wait_recv()
            self.x_copy(chunk, step).start()

        if self.lk.fs == 4:
            work(2)
            pl.when(self.inner())(self.relay(chunk).start)
            work(1)
            work(3)
        else:
            self.each(1, work)

    def finish(self, chunk):
        self.own_copy(chunk).wait()
        self.each(0, lambda step: self.x_copy(chunk, step).wait_recv())

    def drain(self, chunk):
        if self.lk.fs == 4:
            for step in (2, 1, 3):
                pl.when(jnp.logical_not(self.far(step)))(self.z_copy(chunk, step).wait_send)
            pl.when(self.inner())(self.relay(chunk).wait_send)
        else:
            self.each(1, lambda step: self.z_copy(chunk, step).wait_send())
        self.each(0, lambda step: self.x_copy(chunk, step).wait_send())


def store_part(part, k, cols, values, rows):
    for block in range(4):
        part[k, block % 2, block // 2, :, cols] = values[block * rows : (block + 1) * rows].astype(
            BF
        )


def masked_scores(query, key_rows, same_seq):
    return jnp.where(
        same_seq, dot(query, key_rows, NT) * (LOG2E / math.sqrt(HD)), NEG
    )


def forward_kernel(
    tokens, time_embed, cot, to_owner, from_owner, seg, shard, biases, gain, offset, up_bias,
    out_w, out_act, out_qkv, out_att, out_nrm, out_std, out_hid, out_glu, out_dglu, out_lse,
    out_u, out_cot, out_gain, out_pick_out, out_pick_in,
    w, act, qkv, att, nrm, std, hid, glu, dglu, lse, u, h, part, from_sib, to_peer, from_peer,
    slots, arrived, cot_part, cot_rows, u_low,
    bias_full, gain_full, offset_full, pick_out, pick_in, given,
    out_sem, rs_send, rs_recv, ag_send, ag_recv, z_send, z_recv, x_send, x_recv, own,
    ex_send, ex_recv, tr_send, tr_recv, given_sem,
):
    layers, packs, rows, width = act.shape
    sends = slots.shape[2] // packs
    local_width = slots.shape[3]
    mine = rows // 4
    heads_width = att.shape[3]
    chunks = shard.shape[0]
    lk = Links()
    lk.barrier()
    rs = RowSum(lk, part, from_sib, to_peer, from_peer, rs_send, rs_recv)
    ag = RowGather(lk, mine, ag_send, ag_recv)
    wg = WeightGather(lk, shard, w, z_send, z_recv, x_send, x_recv, own)
    pending = []

    def save(src, dst):
        copy = pltpu.make_async_copy(src, dst, out_sem.at[len(pending)])
        copy.start()
        pending.append(copy)

    my_rows = part_of(mine, lk.t)
    my_cols = part_of(local_width, lk.t)
    swaps = [
        Exchange(
            lk, lambda g, i=i: slots.at[i, g], lambda g, i=i: arrived.at[i, g],
            ex_send.at[i], ex_recv.at[i],
        )
        for i in range(2)
    ]

    def send_slots(which, values):
        for c in range(2):
            for k in range(packs):
                m = c * packs + k
                picked = dot(pick_out[m * held : (m + 1) * held], values(m), NN)
                for f in range(picked.shape[0] // sends):
                    slots[which, 2 * f + c, k * sends : (k + 1) * sends] = picked[
                        f * sends : (f + 1) * sends
                    ].astype(BF)
        swaps[which].first()

    def placed_rows(which, k):
        blocks = [
            arrived[which, g, k * sends : (k + 1) * sends] for g in range(arrived.shape[1])
        ]
        return dot(
            pick_in[k * rows : (k + 1) * rows], jnp.concatenate(blocks, axis=0), TN
        ).astype(BF)

    def weights_next(chunk):
        if chunk < chunks:
            for part in range(chunk * HALVES, (chunk + 1) * HALVES):
                wg.forward(part)
                if part + HALVES < chunks * HALVES:
                    wg.start(part + HALVES)
                if part + 3 * HALVES < chunks * HALVES:
                    wg.own_first(part + 3 * HALVES)

    def weights_ready(chunk):
        for part in range(chunk * HALVES, (chunk + 1) * HALVES):
            wg.finish(part)
        save(w.at[chunk], out_w.at[chunk])

    for half in range(HALVES):
        wg.own_first(half)
    give = remote(
        from_owner, given.at[lk.c], given_sem.at[0], given_sem.at[1], lk.across
    )
    give.start()
    params = [
        Trade(
            lk, lambda t, src=src: src, lambda t, full=full: full.at[:, :, part_of(local_width, t)],
            tr_send.at[1 + i], tr_recv.at[1 + i],
        )
        for i, (src, full) in enumerate(
            ((biases, bias_full), (gain, gain_full), (offset, offset_full))
        )
    ]
    for param in params:
        param.first()
    held = tokens.shape[1]
    for m in range(tokens.shape[0]):
        pick_out[m * held : (m + 1) * held] = leaving_slots(
            to_owner[m : m + 1], held // sends, rows, sends
        )
    send_slots(0, lambda m: (tokens[m].astype(F32) + time_embed[m].astype(F32)).astype(BF))
    lse[...] = jnp.zeros_like(lse)
    first_ag = RowGather(lk, local_width, ag_send, ag_recv, by_columns=True)
    for half in range(HALVES):
        wg.start(half)
    for half in range(HALVES, 3 * HALVES):
        wg.own_first(half)
    given[lk.c] = from_owner[...]
    give.wait_recv()
    give.wait_send()
    for k in range(packs):
        m = pl.ds(lk.c * packs + k, 1)
        row = jnp.concatenate([given[c, m] for c in range(2)], axis=1)
        pick_in[k * rows : (k + 1) * rows] = coming_slots(
            row, arrived.shape[1], held, sends
        )
    for param in params:
        param.last()
    save(gain_full, out_gain)
    save(pick_out, out_pick_out)
    save(pick_in, out_pick_in)
    swaps[0].last()
    for k in range(packs):
        act[0, k, :, my_cols] = placed_rows(0, k)
        first_ag.first(act.at[0, k], k)
    for k in range(packs):
        first_ag.second(act.at[0, k], k)
    weights_next(0)
    for k in range(packs):
        first_ag.last(act.at[0, k], k)
        u[k] = act[0, k, my_rows].astype(F32)
        save(act.at[0, k], out_act.at[0, k])

    def project(layer, k):
        for j in range(3):
            cols = slice(j * heads_width, (j + 1) * heads_width)
            acc = dot(act[layer, k], w[3 * layer, :, cols], NN)
            if j != 1:
                acc = acc + biases[layer, j // 2 : j // 2 + 1]
            qkv[layer, k, :, cols] = acc.astype(BF)
        save(qkv.at[layer, k], out_qkv.at[layer, k])

    def attention(layer, k):
        same_seq = same_sequence(seg, lk.c * packs + k)
        for head in range(heads_width // HD):
            cols = [slice(j * heads_width + head * HD, j * heads_width + (head + 1) * HD) for j in range(3)]
            scores = masked_scores(qkv[layer, k, :, cols[0]], qkv[layer, k, :, cols[1]], same_seq)
            top = jnp.max(scores, axis=1, keepdims=True)
            weighted = jnp.exp2(scores - top)
            total = jnp.sum(weighted, axis=1, keepdims=True)
            lse[layer, k, :, head : head + 1] = top + jnp.log2(total)
            probs = (weighted * (1.0 / total)).astype(BF)
            att[layer, k, :, cols[0]] = dot(probs, qkv[layer, k, :, cols[2]], NN).astype(BF)
        save(lse.at[layer, k], out_lse.at[layer, k])
        save(att.at[layer, k], out_att.at[layer, k])
        for j in range(width // 256):
            cols = slice(j * 256, (j + 1) * 256)
            acc = dot(att[layer, k], w[3 * layer, cols, 3 * heads_width :], NT)
            store_part(part, k, cols, acc, mine)
        rs.first(k)

    def normalize(layer, which, k, resid):
        mean = jnp.mean(resid, axis=1, keepdims=True)
        centred = resid - mean
        scale = lax.rsqrt(jnp.mean(centred * centred, axis=1, keepdims=True) + EPS)
        normed = centred * scale
        nrm[layer, which, k] = normed
        std[layer, which, k] = jnp.broadcast_to(scale, std.shape[3:])
        save(nrm.at[layer, which, k], out_nrm.at[layer, which, k])
        save(std.at[layer, which, k], out_std.at[layer, which, k])
        return (
            normed * gain_full[layer, which : which + 1] + offset_full[layer, which : which + 1]
        )

    def norm_one(layer, k):
        hidden = normalize(layer, 0, k, u[k] + rs.last(k) + bias_full[layer, 2:3])
        h[k] = hidden
        hid[layer, k, my_rows] = hidden.astype(BF)
        ag.first(hid.at[layer, k], k)

    def expand(layer, k):
        def tile(j, carry):
            cols = pl.ds(pl.multiple_of(j * 256, 256), 256)
            acc = dot(hid[layer, k], w[3 * layer + 1, :, cols], NN) + up_bias[layer : layer + 1, cols]
            value, slope = gelu_pair(acc)
            glu[layer, k, :, cols] = value.astype(BF)
            dglu[layer, k, :, cols] = slope.astype(BF)
            return carry

        lax.fori_loop(0, width // 256, tile, 0)
        save(glu.at[layer, k], out_glu.at[layer, k])
        save(dglu.at[layer, k], out_dglu.at[layer, k])

    def contract(layer, k):
        def tile(j, carry):
            cols = pl.ds(pl.multiple_of(j * 256, 256), 256)
            acc = dot(glu[layer, k], w[3 * layer + 2, cols, :], NT)
            store_part(part, k, cols, acc, mine)
            return carry

        lax.fori_loop(0, width // 256, tile, 0)
        rs.first(k)

    def norm_two(layer, k):
        out = normalize(layer, 1, k, h[k] + rs.last(k) + bias_full[layer, 3:4])
        u[k] = out
        if layer + 1 < layers:
            act[layer + 1, k, my_rows] = out.astype(BF)
            ag.first(act.at[layer + 1, k], k)
        else:
            u_low[k] = out.astype(BF)
            save(u_low.at[k], out_u.at[k])

    trade = Trade(
        lk, lambda t: cot_part.at[:, part_of(mine, t)],
        lambda t: cot_rows.at[:, :, part_of(local_width, t)], tr_send.at[0], tr_recv.at[0],
    )
    for layer in range(layers):
        base = 3 * layer
        more = layer + 1 < layers
        weights_ready(base)
        if layer:
            ag.last(act.at[layer, 0], 0)
            save(act.at[layer, 0], out_act.at[layer, 0])
        project(layer, 0)
        if layer:
            ag.second(act.at[layer, 1], 1)
        attention(layer, 0)
        weights_next(base + 1)
        if layer:
            ag.last(act.at[layer, 1], 1)
            save(act.at[layer, 1], out_act.at[layer, 1])
        project(layer, 1)
        rs.second(0)
        attention(layer, 1)
        norm_one(layer, 0)
        rs.second(1)
        ag.second(hid.at[layer, 0], 0)
        weights_next(base + 2)
        norm_one(layer, 1)
        weights_ready(base + 1)
        ag.last(hid.at[layer, 0], 0)
        save(hid.at[layer, 0], out_hid.at[layer, 0])
        expand(layer, 0)
        ag.second(hid.at[layer, 1], 1)
        if not more:
            send_slots(1, lambda m: cot[m])
        ag.last(hid.at[layer, 1], 1)
        save(hid.at[layer, 1], out_hid.at[layer, 1])
        expand(layer, 1)
        weights_ready(base + 2)
        contract(layer, 0)
        contract(layer, 1)
        rs.second(0)
        weights_next(base + 3)
        if not more:
            swaps[1].last()
            for k in range(packs):
                cot_part[k] = placed_rows(1, k)
            trade.first()
        norm_two(layer, 0)
        rs.second(1)
        if more:
            ag.second(act.at[layer + 1, 0], 0)
        norm_two(layer, 1)
    trade.last()
    save(cot_rows, out_cot)
    for part in range(chunks * HALVES):
        wg.drain(part)
    for swap in swaps:
        swap.drain()
    for copy in pending:
        copy.wait()


def forward(
    tokens, time_embed, cot, to_owner, from_owner, seg, shard, biases, gain, offset, up_bias
):
    rows = seg.shape[1]
    packs = tokens.shape[0] // lax.axis_size("ctx")
    width = shard.shape[2]
    local_width = tokens.shape[2]
    chunks = shard.shape[0]
    layers = chunks // 3
    mine = rows // 4
    heads = biases.shape[2]
    fs, cx = lax.axis_size("fsdp"), lax.axis_size("ctx")
    groups = fs * cx
    sends = tokens.shape[1] // fs
    parts = chunks * HALVES
    shapes = dict(
        w=((chunks, width, width), BF),
        act=((layers, packs, rows, width), BF),
        qkv=((layers, packs, rows, 3 * heads), BF),
        att=((layers, packs, rows, heads), BF),
        nrm=((layers, 2, packs, mine, width), F32),
        std=((layers, 2, packs, mine, 128), F32),
        hid=((layers, packs, rows, width), BF),
        glu=((layers, packs, rows, width), BF),
        dglu=((layers, packs, rows, width), BF),
        lse=((layers, packs, rows, 128), F32),
        u=((packs, mine, width), F32),
    )
    outs = {name: jax.ShapeDtypeStruct(*shape) for name, shape in shapes.items()}
    outs["u"] = jax.ShapeDtypeStruct((packs, mine, width), BF)
    outs["cot"] = jax.ShapeDtypeStruct((packs, mine, width), BF)
    outs["gain"] = jax.ShapeDtypeStruct((layers, 2, width), F32)
    given = tokens.shape[0] * tokens.shape[1]
    outs["pick_out"] = jax.ShapeDtypeStruct((given, tokens.shape[1]), BF)
    outs["pick_in"] = jax.ShapeDtypeStruct((packs * rows, rows), BF)
    copies = chunks + layers * packs * 11 + packs + 4
    dma = pltpu.SemaphoreType.DMA
    whole = pl.BlockSpec(memory_space=pl.ANY)
    vmem = pl.BlockSpec(memory_space=pltpu.VMEM)
    return pl.pallas_call(
        forward_kernel,
        in_specs=[vmem] * 6 + [whole] + [vmem] * 4,
        out_specs=[whole] * len(outs),
        out_shape=list(outs.values()),
        scratch_shapes=[pltpu.VMEM(*shape) for shape in shapes.values()]
        + [
            pltpu.VMEM((packs, mine, width), F32),
            pltpu.VMEM((packs, 2, 2, mine, width), BF),
            pltpu.VMEM((packs, 2, mine, width), BF),
            pltpu.VMEM((packs, mine, width), BF),
            pltpu.VMEM((packs, mine, width), BF),
            pltpu.VMEM((2, groups, packs * sends, local_width), BF),
            pltpu.VMEM((2, groups, packs * sends, local_width), BF),
            pltpu.VMEM((packs, rows, local_width), BF),
            pltpu.VMEM((packs, mine, width), BF),
            pltpu.VMEM((packs, mine, width), BF),
            pltpu.VMEM((layers, 4, width), F32),
            pltpu.VMEM((layers, 2, width), F32),
            pltpu.VMEM((layers, 2, width), F32),
            pltpu.VMEM((given, tokens.shape[1]), BF),
            pltpu.VMEM((packs * rows, rows), BF),
            pltpu.VMEM((2,) + from_owner.shape, jnp.int32),
            dma((copies,)),
            dma((packs, 2)), dma((packs, 2)), dma((packs, 3)), dma((packs, 3)),
            dma((parts, fs)), dma((parts, fs)), dma((parts, fs)), dma((parts, fs)),
            dma((parts,)),
            dma((2, 2, fs)), dma((2, 2, fs)), dma((4, 3)), dma((4, 3)), dma((2,)),
        ],
        compiler_params=pltpu.CompilerParams(
            collective_id=0, has_side_effects=True, vmem_limit_bytes=60 << 20
        ),
        name="forward",
    )(
        tokens, time_embed, cot, to_owner, from_owner, seg, shard, biases, gain, offset, up_bias
    )


class GradScatter:
    def __init__(self, lk, grad, from_x, from_z, relayed, x_send, x_recv, z_send, z_recv):
        self.lk, self.grad, self.from_x, self.from_z = lk, grad, from_x, from_z
        self.relayed = relayed
        self.x_send, self.x_recv, self.z_send, self.z_recv = x_send, x_recv, z_send, z_recv
        self.rows = from_x.shape[2]

    def block(self, chunk, step, c):
        f = lax.rem(self.lk.f + step, self.lk.fs)
        first = pl.multiple_of((f * self.lk.cx + c) * self.rows, self.rows)
        return self.grad.at[chunk, pl.ds(first, self.rows)]

    def x_copy(self, chunk, step):
        return remote(
            self.block(chunk, step, 1 - self.lk.c), self.from_x.at[chunk, step],
            self.x_send.at[chunk, step], self.x_recv.at[chunk, step], self.lk.across,
        )

    def z_copy(self, chunk, step):
        slot = self.lk.fs - step
        return remote(
            self.block(chunk, step, self.lk.c), self.from_z.at[chunk, slot - 1],
            self.z_send.at[chunk, step], self.z_recv.at[chunk, slot], self.lk.away(step),
        )

    def each(self, first, work, last=None):
        def body(step, carry):
            work(step)
            return carry

        lax.fori_loop(first, self.lk.fs if last is None else last, body, 0)

    def far(self, step):
        return jnp.abs(lax.rem(self.lk.f + step, self.lk.fs) - self.lk.f) == 3

    def inner(self):
        return (self.lk.f == 1) | (self.lk.f == 2)

    def relay(self, chunk, step):
        f = self.lk.f
        return remote(
            self.block(chunk, step, self.lk.c), self.relayed.at[chunk],
            self.z_send.at[chunk, 0], self.z_recv.at[chunk, 0],
            (lax.select(f == 0, 1, 2), self.lk.c, self.lk.t),
        )

    def first(self, chunk):
        if self.lk.fs == 4:
            for step in (1, 3, 2):
                self.x_copy(chunk, step).start()
        else:
            self.each(1, lambda step: self.x_copy(chunk, step).start())
        self.x_copy(chunk, 0).start()

    def second(self, chunk, part):
        def work(step):
            self.x_copy(chunk, step).wait_recv()
            own = self.block(chunk, step, self.lk.c)
            own[...] = (own[...].astype(F32) + self.from_x[chunk, step].astype(F32)).astype(BF)
            if self.lk.fs == 4:
                pl.when(self.far(step))(self.relay(chunk, step).start)
                if step == 2:

                    @pl.when(self.inner())
                    def _():
                        self.relay(chunk, step).wait_recv()
                        own[...] = (
                            own[...].astype(F32) + self.relayed[chunk].astype(F32)
                        ).astype(BF)

                pl.when(jnp.logical_not(self.far(step)))(self.z_copy(chunk, step).start)
            else:
                self.z_copy(chunk, step).start()

        if self.lk.fs == 4:
            work((1, 3, 2)[part])
            return
        first, last = third(self.lk.fs, part)
        self.each(first, work, last)

    def last(self, chunk, out):
        self.x_copy(chunk, 0).wait_recv()
        out[...] = self.block(chunk, 0, self.lk.c)[...].astype(F32) + self.from_x[chunk, 0].astype(F32)

        def work(step):
            self.z_copy(chunk, self.lk.fs - step).wait_recv()
            out[...] = out[...] + self.from_z[chunk, step - 1].astype(F32)

        if self.lk.fs == 4:
            for step in (1, 2, 3):
                pl.when(jnp.logical_not(self.far(step)))(functools.partial(work, step))
        else:
            self.each(1, work)

    def drain(self, chunk):
        self.each(0, lambda step: self.x_copy(chunk, step).wait_send())
        if self.lk.fs == 4:
            for step in (1, 2, 3):
                pl.when(self.far(step))(self.relay(chunk, step).wait_send)
                pl.when(jnp.logical_not(self.far(step)))(self.z_copy(chunk, step).wait_send)
        else:
            self.each(1, lambda step: self.z_copy(chunk, step).wait_send())


def backward_kernel(
    up_in, u_in, pick_out, pick_in, act_in, w_in, qkv_in, att_in, nrm_in, std_in, hid_in, glu_in, dglu_in,
    lse_in, gain, seg,
    out_qkv, out_out, out_up, out_down, out_ret, out_sums,
    w, qkv, att, nrm, std, hid, glu, dglu, lse, up, gtwo, gl, gm, gup, gqkv, gatt,
    part, from_sib, to_peer, from_peer, grad, from_x, from_z, relayed, gsum, low, ret_in,
    out_vec, out_head, out_bias, vec_parts, sums,
    in_sem, out_sem, rs_send, rs_recv, ag_send, ag_recv, x_send, x_recv, z_send, z_recv,
    ex_send, ex_recv, tr_send, tr_recv, pick_sem,
):
    packs, rows, width = hid.shape
    layers = gain.shape[0]
    mine = rows // 4
    heads_width = att.shape[2]
    lk = Links()
    sources = dict(
        nrm1=lambda layer: (nrm_in.at[layer, 1], nrm.at[1]),
        std1=lambda layer: (std_in.at[layer, 1], std.at[1]),
        nrm0=lambda layer: (nrm_in.at[layer, 0], nrm.at[0]),
        std0=lambda layer: (std_in.at[layer, 0], std.at[0]),
        w2=lambda layer: (w_in.at[3 * layer + 2], w.at[2]),
        dglu=lambda layer: (dglu_in.at[layer], dglu),
        w1=lambda layer: (w_in.at[3 * layer + 1], w.at[1]),
        glu=lambda layer: (glu_in.at[layer], glu),
        hid=lambda layer: (hid_in.at[layer], hid),
        w0=lambda layer: (w_in.at[3 * layer], w.at[0]),
        qkv=lambda layer: (qkv_in.at[layer], qkv),
        lse=lambda layer: (lse_in.at[layer], lse),
        att=lambda layer: (att_in.at[layer], att),
        act=lambda layer: (act_in.at[layer], hid),
    )
    order = {name: index for index, name in enumerate(sources)}

    def fetch(name, layer):
        if layer >= 0:
            src, dst = sources[name](layer)
            pltpu.make_async_copy(src, dst, in_sem.at[order[name]]).start()

    def ready(name, layer):
        src, dst = sources[name](layer)
        pltpu.make_async_copy(src, dst, in_sem.at[order[name]]).wait()

    loads = [
        pltpu.make_async_copy(up_in, to_peer, in_sem.at[len(order)]),
        pltpu.make_async_copy(u_in, low, in_sem.at[len(order) + 1]),
    ]
    for load in loads:
        load.start()
    for name in sources:
        if name != "act":
            fetch(name, layers - 1)
    lk.barrier()
    rs = RowSum(lk, part, from_sib, to_peer, from_peer, rs_send, rs_recv)
    ag = RowGather(lk, mine, ag_send, ag_recv)
    gs = GradScatter(lk, grad, from_x, from_z, relayed, x_send, x_recv, z_send, z_recv)
    my_rows = pl.ds(pl.multiple_of(lk.t * mine, mine), mine)
    pending = []
    held = {}
    local_width = ret_in.shape[1]
    swap_rows = width // (lk.fs * lk.cx)
    sends = swap_rows // packs
    low_cols, next_cols, third_cols, last_cols = (
        slice(i * local_width, (i + 1) * local_width) for i in range(4)
    )

    class Return:
        def __init__(self, index, first, second, landed):
            self.index, self.first_buf, self.second_buf, self.landed = index, first, second, landed
            self.trade = Trade(
                lk, lambda t: low.at[:, :, part_of(local_width, t)],
                lambda t: (gm, gup)[index].at[:, part_of(mine, t), low_cols],
                tr_send.at[index], tr_recv.at[index],
            )
            self.swap = Exchange(
                lk, lambda g: first.at[part_of(swap_rows, g), low_cols],
                lambda g: landed.at[part_of(swap_rows, g)], ex_send.at[index], ex_recv.at[index],
            )
            self.picks = [
                pltpu.make_async_copy(
                    pick_in, second.at[:, : 2 * local_width], pick_sem.at[index, 0]
                ),
                pltpu.make_async_copy(pick_out, second.at[:, third_cols], pick_sem.at[index, 1]),
            ]

        def load(self):
            for copy in self.picks:
                copy.start()

        def middle(self):
            self.trade.last()
            self.picks[0].wait()
            for k in range(packs):
                pick = self.second_buf[k * rows : (k + 1) * rows, : 2 * local_width]
                values = dot(pick, (gm, gup)[self.index][k, :, low_cols], NN).astype(BF)
                for g in range(rows // sends):
                    first = g * swap_rows + k * sends
                    self.first_buf[first : first + sends, low_cols] = values[
                        g * sends : (g + 1) * sends
                    ]
            self.swap.first()

        def last(self):
            self.swap.last()
            self.picks[1].wait()
            given = pick_out.shape[1]
            for c in range(2):
                for k in range(packs):
                    m = c * packs + k
                    blocks = [
                        self.landed[
                            (2 * f + c) * swap_rows + k * sends :
                            (2 * f + c) * swap_rows + (k + 1) * sends
                        ]
                        for f in range(given // sends)
                    ]
                    pick = self.second_buf[m * given : (m + 1) * given, third_cols]
                    values = dot(pick, jnp.concatenate(blocks, axis=0), TN)
                    self.second_buf[m * given : (m + 1) * given, last_cols] = values.astype(BF)
            save(self.second_buf.at[:, last_cols], out_ret.at[self.index])
            self.saved = pending.pop()

        def finish(self):
            self.swap.drain()
            self.saved.wait()

    give_back = [
        Return(0, grad.at[0], grad.at[1], grad.at[0, :, next_cols]),
        Return(1, grad.at[3 * layers - 1], grad.at[3 * layers - 2], ret_in),
    ]
    vec_trade = Trade(
        lk, lambda t: out_vec.at[:, :, part_of(local_width, t)], lambda t: vec_parts.at[t],
        tr_send.at[2], tr_recv.at[2],
    )
    vec_swap = Exchange(
        lk, lambda g: sums.at[lk.g], lambda g: sums.at[g], ex_send.at[2], ex_recv.at[2],
        in_place=True,
    )

    def vec_middle():
        vec_trade.last()
        total = vec_parts[0]
        for t in range(1, 4):
            total = total + vec_parts[t]
        sums[lk.g, :, 0:6] = total
        sums[lk.g, :, 6:8] = out_head[...]
        for j in range(4):
            sums[lk.g, :, 8 + j : 9 + j] = out_bias[:, :, j * local_width : (j + 1) * local_width]
        vec_swap.first()

    def vec_last():
        vec_swap.last()

        def add(g, total):
            return total + sums[g]

        out_sums[...] = lax.fori_loop(1, sums.shape[0], add, sums[0])

    used = []

    def save(src, dst):
        copy = pltpu.make_async_copy(src, dst, out_sem.at[len(used)])
        copy.start()
        used.append(1)
        pending.append(copy)

    out_vec[...] = jnp.zeros_like(out_vec)
    out_head[...] = jnp.zeros_like(out_head)
    out_bias[...] = jnp.zeros_like(out_bias)

    def norm_back(layer, which, k, upstream):
        normed = nrm[which, k]
        scale = std[which, k][:, 0:1]
        out_vec[layer, 2 + which : 3 + which] += jnp.sum(upstream * normed, axis=0, keepdims=True)
        out_vec[layer, 4 + which : 5 + which] += jnp.sum(upstream, axis=0, keepdims=True)
        scaled = upstream * gain[layer, which : which + 1]
        first = jnp.mean(scaled, axis=1, keepdims=True)
        second = jnp.mean(scaled * normed, axis=1, keepdims=True)
        result = scale * (scaled - first - normed * second)
        out_vec[layer, which : which + 1] += jnp.sum(result, axis=0, keepdims=True)
        return result

    def norm_two(layer, k):
        result = norm_back(layer, 1, k, up[k])
        gtwo[k] = result
        gl[k, my_rows] = result.astype(BF)
        ag.first(gl.at[k], k)

    def norm_one(layer, k):
        result = norm_back(layer, 0, k, gtwo[k] + rs.last(k))
        up[k] = result
        gm[k, my_rows] = result.astype(BF)
        ag.first(gm.at[k], k)

    def tiles(work):
        def body(j, carry):
            work(pl.ds(pl.multiple_of(j * 256, 256), 256))
            return carry

        lax.fori_loop(0, width // 256, body, 0)

    def through_down(layer, k):
        def tile(cols):
            grad_gelu = dot(gl[k], w[2, :, cols], NN).astype(BF).astype(F32)
            result = (grad_gelu * dglu[k, :, cols].astype(F32)).astype(BF)
            gup[k, :, cols] = result
            out_bias[layer, :, cols] += jnp.sum(result.astype(F32), axis=0, keepdims=True)

        tiles(tile)

    def through_up(layer, k):
        tiles(lambda cols: store_part(part, k, cols, dot(gup[k], w[1, cols, :], NT), mine))
        rs.first(k)

    def through_out(k):
        gatt[k] = dot(gm[k], w[0, :, 3 * heads_width :], NN).astype(BF)

    def attention(layer, k):
        same_seq = same_sequence(seg, lk.c * packs + k)
        scale = 1.0 / math.sqrt(HD)
        for head in range(heads_width // HD):
            cols = [slice(j * heads_width + head * HD, j * heads_width + (head + 1) * HD) for j in range(3)]
            query, keys, values = (qkv[k, :, c] for c in cols)
            grads = gatt[k, :, cols[0]]
            probs = jnp.exp2(masked_scores(query, keys, same_seq) - lse[k, :, head : head + 1])
            grad_probs = dot(grads, values, NT)
            delta = jnp.sum(probs * grad_probs, axis=1, keepdims=True)
            grad_scores = (probs * (grad_probs - delta)).astype(BF)
            gqkv[k, :, cols[0]] = (dot(grad_scores, keys, NN) * scale).astype(BF)
            gqkv[k, :, cols[1]] = (dot(grad_scores, query, TN) * scale).astype(BF)
            gqkv[k, :, cols[2]] = dot(probs.astype(BF), grads, TN).astype(BF)
        for j in range(2):
            cols = slice(2 * j * heads_width, (2 * j + 1) * heads_width)
            out_head[layer, j : j + 1] += jnp.sum(
                gqkv[k, :, cols].astype(F32), axis=0, keepdims=True
            )

    def through_qkv(k):
        tiles(
            lambda cols: store_part(
                part, k, cols, dot(gqkv[k], w[0, cols, : 3 * heads_width], NT), mine
            )
        )
        rs.first(k)

    def product(left, right, cols, right_cols=slice(None)):
        total = dot(left[0, :, cols], right[0, :, right_cols], TN)
        for k in range(1, packs):
            total = total + dot(left[k, :, cols], right[k, :, right_cols], TN)
        return total.astype(BF)

    def down_grad(layer):
        def tile(cols):
            grad[3 * layer + 2, cols, :] = product(gl, glu, cols)

        tiles(tile)
        gs.first(3 * layer + 2)

    def up_grad(layer):
        def tile(cols):
            grad[3 * layer + 1, cols, :] = product(hid, gup, cols)

        tiles(tile)
        gs.first(3 * layer + 1)

    def first_grad(layer):
        def tile(cols):
            grad[3 * layer, cols, : 3 * heads_width] = product(hid, gqkv, cols)
            grad[3 * layer, cols, 3 * heads_width :] = product(gm, att, cols)

        tiles(tile)
        gs.first(3 * layer)

    def emit(layer, which):
        chunk = 3 * layer + which
        out = gsum.at[0]
        while held.get(0):
            held[0].pop().wait()
        gs.last(chunk, out)
        held[0] = []
        saved = len(pending)
        if which == 2:
            save(out, out_down.at[layer])
        elif which == 1:
            save(out, out_up.at[layer])
        else:
            for c in range(3):
                save(out.at[:, c * heads_width : (c + 1) * heads_width], out_qkv.at[layer, c])
            save(out.at[:, 3 * heads_width :], out_out.at[layer])
        held[0] = [pending.pop() for _ in range(len(pending) - saved)]

    give_back[0].load()
    for load in loads:
        load.wait()
    top = layers - 1
    ready("nrm1", top)
    ready("std1", top)
    for k in range(packs):
        up[k] = to_peer[k].astype(F32)
        norm_two(top, k)
    give_back[0].trade.first()
    fetch("nrm1", top - 1)
    fetch("std1", top - 1)
    def summed(chunk, *parts):
        for part in parts:
            gs.second(chunk, part)

    for layer in reversed(range(layers)):
        base = 3 * layer
        later = layer < top
        ag.second(gl.at[0], 0)
        ready("w2", layer)
        ready("dglu", layer)
        ag.last(gl.at[0], 0)
        through_down(layer, 0)
        ag.second(gl.at[1], 1)
        if layer == top:
            give_back[0].middle()
        ready("w1", layer)
        through_up(layer, 0)
        if later:
            summed(base + 3, 0)
        ag.last(gl.at[1], 1)
        through_down(layer, 1)
        fetch("w2", layer - 1)
        fetch("dglu", layer - 1)
        rs.second(0)
        through_up(layer, 1)
        fetch("w1", layer - 1)
        ready("glu", layer)
        down_grad(layer)
        fetch("glu", layer - 1)
        rs.second(1)
        ready("nrm0", layer)
        ready("std0", layer)
        norm_one(layer, 0)
        if later:
            summed(base + 3, 1)
        ready("hid", layer)
        up_grad(layer)
        fetch("act", layer)
        ag.second(gm.at[0], 0)
        if later:
            summed(base + 3, 2)
        else:
            summed(base + 2, 0)
        norm_one(layer, 1)
        fetch("nrm0", layer - 1)
        fetch("std0", layer - 1)
        ready("w0", layer)
        ready("qkv", layer)
        ready("lse", layer)
        ag.last(gm.at[0], 0)
        through_out(0)
        if later:
            summed(base + 2, 0)
        else:
            summed(base + 2, 1)
        ag.second(gm.at[1], 1)
        attention(layer, 0)
        through_qkv(0)
        if later:
            summed(base + 2, 1)
        else:
            summed(base + 2, 2)
            summed(base + 1, 0)
        ag.last(gm.at[1], 1)
        through_out(1)
        rs.second(0)
        attention(layer, 1)
        fetch("qkv", layer - 1)
        fetch("lse", layer - 1)
        through_qkv(1)
        fetch("w0", layer - 1)
        rs.second(1)
        ready("att", layer)
        ready("act", layer)
        first_grad(layer)
        if later:
            summed(base + 2, 2)
        else:
            summed(base + 1, 1)
        if layer:
            fetch("att", layer - 1)
            fetch("hid", layer - 1)
        for k in range(packs):
            up[k] = rs.last(k) + up[k]
            if layer:
                if k == 0:
                    ready("nrm1", layer - 1)
                    ready("std1", layer - 1)
                norm_two(layer - 1, k)
            else:
                low[k] = up[k].astype(BF)
        if layer == top:
            summed(base + 1, 2)
            give_back[0].last()
            give_back[0].finish()
        if layer:
            fetch("nrm1", layer - 2)
            fetch("std1", layer - 2)
    give_back[1].trade.first()
    vec_trade.first()
    summed(1, 0)
    emit(1, 2)
    emit(1, 1)
    for chunk in (3 * layers - 1, 3 * layers - 2):
        gs.drain(chunk)
    give_back[1].load()
    give_back[1].middle()
    vec_middle()
    summed(1, 1, 2)
    emit(1, 0)
    summed(0, 0, 1, 2)
    give_back[1].last()
    vec_last()
    emit(0, 2)
    emit(0, 1)
    emit(0, 0)
    for chunk in range(3 * layers - 2):
        gs.drain(chunk)
    give_back[1].finish()
    vec_swap.drain()
    for copy in pending + sum(held.values(), []):
        copy.wait()


def backward(upstream, u, pick_out, pick_in, saved, gain, seg):
    full_w, o_act, o_qkv, o_att, o_nrm, o_std, o_hid, o_glu, o_dglu, o_lse = saved
    layers, packs, rows, width = o_act.shape
    mine = rows // 4
    chunks = 3 * layers
    heads = o_att.shape[3]
    local_width = width // 4
    fs, cx = lax.axis_size("fsdp"), lax.axis_size("ctx")
    groups = fs * cx
    shard = width // groups
    given = pick_out.shape[0]
    outs = [
        jax.ShapeDtypeStruct((layers, 3, shard, heads), F32),
        jax.ShapeDtypeStruct((layers, shard, heads), F32),
        jax.ShapeDtypeStruct((layers, shard, width), F32),
        jax.ShapeDtypeStruct((layers, shard, width), F32),
        jax.ShapeDtypeStruct((2, given, local_width), BF),
        jax.ShapeDtypeStruct((layers, 12, local_width), F32),
    ]
    dma = pltpu.SemaphoreType.DMA
    whole = pl.BlockSpec(memory_space=pl.ANY)
    vmem = pl.BlockSpec(memory_space=pltpu.VMEM)
    full = pltpu.VMEM((packs, rows, width), BF)
    rowed = pltpu.VMEM((packs, mine, width), F32)
    return pl.pallas_call(
        backward_kernel,
        in_specs=[whole] * 14 + [vmem] * 2,
        out_specs=[whole] * 5 + [vmem],
        out_shape=outs,
        scratch_shapes=[
            pltpu.VMEM((3, width, width), BF),
            pltpu.VMEM((packs, rows, 3 * heads), BF),
            pltpu.VMEM((packs, rows, heads), BF),
            pltpu.VMEM((2, packs, mine, width), F32),
            pltpu.VMEM((2, packs, mine, 128), F32),
            full, full, full,
            pltpu.VMEM((packs, rows, 128), F32),
            rowed, rowed,
            full, full, full,
            pltpu.VMEM((packs, rows, 3 * heads), BF),
            pltpu.VMEM((packs, rows, heads), BF),
            pltpu.VMEM((packs, 2, 2, mine, width), BF),
            pltpu.VMEM((packs, 2, mine, width), BF),
            pltpu.VMEM((packs, mine, width), BF),
            pltpu.VMEM((packs, mine, width), BF),
            pltpu.VMEM((chunks, width, width), BF),
            pltpu.VMEM((chunks, fs, shard, width), BF),
            pltpu.VMEM((chunks, fs - 1, shard, width), BF),
            pltpu.VMEM((chunks if fs == 4 else 1, shard, width), BF),
            pltpu.VMEM((1, shard, width), F32),
            pltpu.VMEM((packs, mine, width), BF),
            pltpu.VMEM((given, local_width), BF),
            pltpu.VMEM((layers, 6, width), F32),
            pltpu.VMEM((layers, 2, heads), F32),
            pltpu.VMEM((layers, 1, width), F32),
            pltpu.VMEM((4, layers, 6, local_width), F32),
            pltpu.VMEM((groups, layers, 12, local_width), F32),
            dma((16,)), dma((packs + 6 * layers + 2,)),
            dma((packs, 2)), dma((packs, 2)), dma((packs, 3)), dma((packs, 3)),
            dma((chunks, fs)), dma((chunks, fs)), dma((chunks, fs)), dma((chunks, fs)),
            dma((3, 2, fs)), dma((3, 2, fs)), dma((3, 3)), dma((3, 3)), dma((2, 2)),
        ],
        compiler_params=pltpu.CompilerParams(
            collective_id=1, has_side_effects=True, vmem_limit_bytes=62 << 20
        ),
        name="backward",
    )(
        upstream, u, pick_out, pick_in, o_act, full_w, o_qkv, o_att, o_nrm, o_std, o_hid,
        o_glu, o_dglu, o_lse, gain, seg,
    )


def local(
    tokens, time_embed, cotangent, segment_ids, to_owner, from_owner,
    w_qkv, w_out, w_up, w_down, biases, norm_gain, norm_bias, up_bias,
):
    micro, rows, width = tokens.shape
    layers = w_qkv.shape[0]
    shard = jnp.concatenate(
        [w_qkv[:, 0], w_qkv[:, 1], w_qkv[:, 2], w_out, w_up, w_down], axis=2
    )
    shard = shard.reshape(layers, shard.shape[1], 3, -1).transpose(0, 2, 1, 3)
    shard = shard.reshape(layers * 3, shard.shape[2], -1)
    *saved, u, upstream, gain, pick_out, pick_in = forward(
        tokens, time_embed, cotangent, to_owner, from_owner, segment_ids, shard, biases,
        norm_gain, norm_bias, up_bias,
    )
    g_qkv, g_out, g_up, g_down, returned, sums = backward(
        upstream, u, pick_out, pick_in, saved, gain, segment_ids
    )
    returned = returned.reshape(2, micro, rows, width).astype(F32)
    return (
        returned[0],
        returned[1],
        g_qkv, g_out, g_up, g_down,
        jnp.concatenate([sums[:, 6:8], sums[:, 0:2]], axis=1),
        sums[:, 2:4],
        sums[:, 4:6],
        sums[:, 8:12].reshape(layers, -1),
    )


def solution(mesh):
    wide = P(None, GRP, "tp")
    vec = P(None, None, "tp")
    qkv = P(None, None, GRP, "tp")
    owner = P(None, GRP)
    return jax.shard_map(
        local,
        mesh=mesh,
        in_specs=(
            wide, wide, wide, P(None, "fsdp"), owner, owner, qkv, wide, wide, wide,
            vec, vec, vec, P(None, "tp"),
        ),
        out_specs=(wide, wide, qkv, wide, wide, wide, vec, vec, vec, P(None, "tp")),
        check_vma=False,
    )
```

```python
import functools
import math

import jax
import jax.numpy as jnp
from jax import lax
from jax.experimental import pallas as pl
from jax.experimental.pallas import tpu as pltpu
from jax.sharding import PartitionSpec as P

HD = 64
NEG = -1e30
EPS = 1e-05
BF = jnp.bfloat16
F32 = jnp.float32
GRP = ("fsdp", "ctx")


def dot(left, right, dims):
    return lax.dot_general(left, right, (dims, ((), ())), preferred_element_type=F32)


NN = ((1,), (0,))
NT = ((1,), (1,))
TN = ((0,), (0,))

MESH = pl.DeviceIdType.MESH
LOG2E = 1.4426950408889634
HALVES = 1


def gelu_pair(values):
    bell = jnp.exp2(values * values * (-0.5 * LOG2E))
    t = 1.0 / (1.0 + (0.3275911 * math.sqrt(0.5)) * jnp.abs(values))
    poly = t * (
        0.127414796 + t * (-0.142248368 + t * (0.7107068705 + t * (-0.7265760135 + t * 0.5307027145)))
    )
    tail = poly * bell
    phi = jnp.where(values < 0, tail, 1.0 - tail)
    return values * phi, phi + values * bell * (1.0 / math.sqrt(2.0 * math.pi))


class Links:
    def __init__(self):
        self.fs, self.cx = lax.axis_size("fsdp"), lax.axis_size("ctx")
        self.f, self.c, self.t = (lax.axis_index(a) for a in ("fsdp", "ctx", "tp"))
        self.core, self.chip = lax.rem(self.t, 2), self.t // 2
        self.sib_t = self.t + 1 - 2 * self.core
        self.peer_t = lax.rem(self.t + 2, 4)
        self.sib = (self.f, self.c, self.sib_t)
        self.peer = (self.f, self.c, self.peer_t)
        self.diag_t = 3 - self.t
        self.diag = (self.f, self.c, self.diag_t)
        self.across = (self.f, 1 - self.c, self.t)
        self.g = self.f * self.cx + self.c

    def away(self, step, c=None):
        return (lax.rem(self.f + step, self.fs), self.c if c is None else c, self.t)

    def barrier(self):
        sem = pltpu.get_barrier_semaphore()
        for target in (self.sib, self.peer, self.diag, self.across):
            pl.semaphore_signal(sem, inc=1, device_id=target, device_id_type=MESH)

        def greet(step, carry):
            for c in (self.c, 1 - self.c):
                pl.semaphore_signal(
                    sem, inc=1, device_id=self.away(step, c), device_id_type=MESH
                )
            return carry

        lax.fori_loop(1, self.fs, greet, 0)
        pl.semaphore_wait(sem, 2 + 2 * self.fs)


def remote(src, dst, send, recv, target):
    return pltpu.make_async_remote_copy(
        src_ref=src, dst_ref=dst, send_sem=send, recv_sem=recv,
        device_id=target, device_id_type=MESH,
    )


class RowSum:
    def __init__(self, lk, part, from_sib, to_peer, from_peer, send, recv):
        self.lk, self.part, self.from_sib = lk, part, from_sib
        self.to_peer, self.from_peer, self.send, self.recv = to_peer, from_peer, send, recv

    def sib_copy(self, k):
        return remote(
            self.part.at[k, 1 - self.lk.core], self.from_sib.at[k],
            self.send.at[k, 0], self.recv.at[k, 0], self.lk.sib,
        )

    def peer_copy(self, k):
        return remote(
            self.to_peer.at[k], self.from_peer.at[k],
            self.send.at[k, 1], self.recv.at[k, 1], self.lk.peer,
        )

    def first(self, k):
        self.sib_copy(k).start()

    def second(self, k):
        self.sib_copy(k).wait_recv()
        other = 1 - self.lk.chip
        total = self.part[k, self.lk.core, other].astype(F32) + self.from_sib[k, other].astype(F32)
        self.to_peer[k] = total.astype(BF)
        self.peer_copy(k).start()

    def last(self, k):
        own = self.part[k, self.lk.core, self.lk.chip].astype(F32)
        own = own + self.from_sib[k, self.lk.chip].astype(F32)
        self.peer_copy(k).wait_recv()
        self.sib_copy(k).wait_send()
        self.peer_copy(k).wait_send()
        return own + self.from_peer[k].astype(F32)


class RowGather:
    def __init__(self, lk, rows, send, recv, by_columns=False):
        self.lk, self.rows, self.send, self.recv = lk, rows, send, recv
        self.by_columns = by_columns

    def block(self, ref, index):
        part = part_of(self.rows, index)
        return ref.at[:, part] if self.by_columns else ref.at[part]

    def copy(self, ref, k, which):
        index = self.lk.t if which < 2 else self.lk.peer_t
        part = self.block(ref, index)
        target = self.lk.peer if which == 0 else self.lk.sib
        return remote(part, part, self.send.at[k, which], self.recv.at[k, which], target)

    def first(self, ref, k):
        self.copy(ref, k, 0).start()
        self.copy(ref, k, 1).start()

    def second(self, ref, k):
        self.copy(ref, k, 0).wait_recv()
        self.copy(ref, k, 2).start()

    def last(self, ref, k):
        self.copy(ref, k, 1).wait_recv()
        self.copy(ref, k, 2).wait_recv()
        for which in range(3):
            self.copy(ref, k, which).wait_send()


class Exchange:
    def __init__(self, lk, src, dst, send, recv, in_place=False):
        self.lk, self.src, self.dst, self.send, self.recv = lk, src, dst, send, recv
        self.in_place = in_place

    def copy(self, other, step):
        lk = self.lk
        c = 1 - lk.c if other else lk.c
        target = lax.rem(lk.f + step, lk.fs) * lk.cx + c
        return remote(
            self.src(target), self.dst(lk.g), self.send.at[other, step],
            self.recv.at[other, lax.rem(lk.fs - step, lk.fs)], lk.away(step, c),
        )

    def each(self, work):
        def body(step, carry):
            work(1, step)
            work(0, step)
            return carry

        work(1, 0)
        lax.fori_loop(1, self.lk.fs, body, 0)

    def first(self):
        self.each(lambda other, step: self.copy(other, step).start())
        if not self.in_place:
            self.dst(self.lk.g)[...] = self.src(self.lk.g)[...]

    def last(self):
        def work(other, step):
            self.copy(other, lax.rem(self.lk.fs - step, self.lk.fs)).wait_recv()

        self.each(work)

    def drain(self):
        self.each(lambda other, step: self.copy(other, step).wait_send())


class Trade:
    def __init__(self, lk, src, dst, send, recv):
        self.lk, self.src, self.dst, self.send, self.recv = lk, src, dst, send, recv

    def copies(self):
        lk = self.lk
        pairs = ((lk.peer_t, lk.peer), (lk.diag_t, lk.diag), (lk.sib_t, lk.sib))
        return [
            remote(self.src(index), self.dst(lk.t), self.send.at[i], self.recv.at[i], target)
            for i, (index, target) in enumerate(pairs)
        ]

    def first(self):
        for copy in self.copies():
            copy.start()
        self.dst(self.lk.t)[...] = self.src(self.lk.t)[...]

    def last(self):
        for copy in self.copies():
            copy.wait_recv()
            copy.wait_send()


def third(count, part):
    return 1 + (count - 1) * part // 3, 1 + (count - 1) * (part + 1) // 3


def part_of(size, index):
    return pl.ds(pl.multiple_of(index * size, size), size)


def stored_slots(dst, values, first, count, sends, block):
    for i in range(count):
        dst(i)[block * sends : (block + 1) * sends] = values[
            (first + i) * sends : (first + i + 1) * sends
        ].astype(BF)


def one_hot(rows, values):
    return (lax.broadcasted_iota(jnp.int32, (rows, values.shape[1]), 0) == values).astype(BF)


def counts_before(present):
    size = present.shape[1]
    earlier = lax.broadcasted_iota(jnp.int32, (size, size), 0) < lax.broadcasted_iota(
        jnp.int32, (size, size), 1
    )
    return dot(present, earlier.astype(BF), NN)


def leaving_slots(to_row, packs_total, pack, sends):
    groups = one_hot(packs_total, to_row // pack)
    base = lax.broadcasted_iota(jnp.int32, groups.shape, 0) * sends
    slot = (counts_before(groups) + base.astype(F32)) * groups.astype(F32)
    return one_hot(to_row.shape[1], jnp.sum(slot, axis=0, keepdims=True).astype(jnp.int32))


def coming_slots(given, groups, rows, sends):
    source = one_hot(groups, given // rows)
    within = one_hot(rows, lax.rem(given, rows))
    ranks = counts_before(dot(source, within, NT).astype(BF)).astype(BF)
    base = lax.broadcasted_iota(jnp.int32, source.shape, 0) * sends
    slot = (dot(ranks, within, NN) + base.astype(F32)) * source.astype(F32)
    return one_hot(groups * sends, jnp.sum(slot, axis=0, keepdims=True).astype(jnp.int32))


def same_sequence(seg_ref, row):
    member = one_hot(8, lax.rem(seg_ref[pl.ds(row, 1)], 8))
    return dot(member, member, TN) > 0.5


class WeightGather:
    def __init__(self, lk, shard, full, z_send, z_recv, x_send, x_recv, own):
        self.lk, self.shard, self.full = lk, shard, full
        self.z_send, self.z_recv, self.x_send, self.x_recv = z_send, z_recv, x_send, x_recv
        self.own = own
        self.rows = shard.shape[1]
        self.cols = shard.shape[2] // HALVES

    def part(self, chunk):
        return slice(chunk % HALVES * self.cols, (chunk % HALVES + 1) * self.cols)

    def mine(self, chunk):
        return self.shard.at[chunk // HALVES, :, self.part(chunk)]

    def block(self, chunk, f, c):
        rows = part_of(self.rows, f * self.lk.cx + c)
        return self.full.at[chunk // HALVES, rows, self.part(chunk)]

    def z_copy(self, chunk, step):
        return remote(
            self.mine(chunk), self.block(chunk, self.lk.f, self.lk.c),
            self.z_send.at[chunk, step], self.z_recv.at[chunk, self.lk.fs - step],
            self.lk.away(step),
        )

    def far(self, step):
        return jnp.abs(lax.rem(self.lk.f + step, self.lk.fs) - self.lk.f) == 3

    def relay(self, chunk):
        f = self.lk.f
        part = self.block(chunk, 3 * (2 - f), self.lk.c)
        return remote(
            part, part, self.z_send.at[chunk, 0], self.z_recv.at[chunk, 5 - 2 * f],
            (3 * (f - 1), self.lk.c, self.lk.t),
        )

    def inner(self):
        return (self.lk.f == 1) | (self.lk.f == 2)

    def x_copy(self, chunk, step):
        f = lax.rem(self.lk.f + step, self.lk.fs)
        part = self.block(chunk, f, self.lk.c)
        return remote(
            part, part, self.x_send.at[chunk, step], self.x_recv.at[chunk, step], self.lk.across
        )

    def x_own(self, chunk):
        return remote(
            self.mine(chunk), self.block(chunk, self.lk.f, self.lk.c),
            self.x_send.at[chunk, 0], self.x_recv.at[chunk, 0], self.lk.across,
        )

    def own_copy(self, chunk):
        return pltpu.make_async_copy(
            self.mine(chunk), self.block(chunk, self.lk.f, self.lk.c), self.own.at[chunk]
        )

    def each(self, first, work):
        def body(step, carry):
            work(step)
            return carry

        lax.fori_loop(first, self.lk.fs, body, 0)

    def own_first(self, chunk):
        self.own_copy(chunk).start()
        self.x_own(chunk).start()

    def start(self, chunk):
        if self.lk.fs == 4:
            for step in (2, 1, 3):
                pl.when(jnp.logical_not(self.far(step)))(self.z_copy(chunk, step).start)
        else:
            self.each(1, lambda step: self.z_copy(chunk, step).start())

    def forward(self, chunk):
        def work(step):
            self.z_copy(chunk, self.lk.fs - step).wait_recv()
            self.x_copy(chunk, step).start()

        if self.lk.fs == 4:
            work(2)
            pl.when(self.inner())(self.relay(chunk).start)
            work(1)
            work(3)
        else:
            self.each(1, work)

    def finish(self, chunk):
        self.own_copy(chunk).wait()
        self.each(0, lambda step: self.x_copy(chunk, step).wait_recv())

    def drain(self, chunk):
        if self.lk.fs == 4:
            for step in (2, 1, 3):
                pl.when(jnp.logical_not(self.far(step)))(self.z_copy(chunk, step).wait_send)
            pl.when(self.inner())(self.relay(chunk).wait_send)
        else:
            self.each(1, lambda step: self.z_copy(chunk, step).wait_send())
        self.each(0, lambda step: self.x_copy(chunk, step).wait_send())


def store_part(part, k, cols, values, rows):
    for block in range(4):
        part[k, block % 2, block // 2, :, cols] = values[block * rows : (block + 1) * rows].astype(
            BF
        )


def masked_scores(query, key_rows, same_seq):
    return jnp.where(
        same_seq, dot(query, key_rows, NT) * (LOG2E / math.sqrt(HD)), NEG
    )


def forward_kernel(
    tokens, time_embed, cot, to_owner, from_owner, seg, shard, biases, gain, offset, up_bias,
    out_w, out_act, out_qkv, out_att, out_nrm, out_std, out_hid, out_glu, out_dglu, out_lse,
    out_u, out_cot, out_gain, out_pick_out, out_pick_in,
    w, act, qkv, att, nrm, std, hid, glu, dglu, lse, u, h, part, from_sib, to_peer, from_peer,
    slots, arrived, cot_part, cot_rows, u_low,
    bias_full, gain_full, offset_full, pick_out, pick_in, given,
    out_sem, rs_send, rs_recv, ag_send, ag_recv, z_send, z_recv, x_send, x_recv, own,
    ex_send, ex_recv, tr_send, tr_recv, given_sem,
):
    layers, packs, rows, width = act.shape
    sends = slots.shape[2] // packs
    local_width = slots.shape[3]
    mine = rows // 4
    heads_width = att.shape[3]
    chunks = shard.shape[0]
    lk = Links()
    lk.barrier()
    rs = RowSum(lk, part, from_sib, to_peer, from_peer, rs_send, rs_recv)
    ag = RowGather(lk, mine, ag_send, ag_recv)
    wg = WeightGather(lk, shard, w, z_send, z_recv, x_send, x_recv, own)
    pending = []

    def save(src, dst):
        copy = pltpu.make_async_copy(src, dst, out_sem.at[len(pending)])
        copy.start()
        pending.append(copy)

    my_rows = part_of(mine, lk.t)
    my_cols = part_of(local_width, lk.t)
    swaps = [
        Exchange(
            lk, lambda g, i=i: slots.at[i, g], lambda g, i=i: arrived.at[i, g],
            ex_send.at[i], ex_recv.at[i],
        )
        for i in range(2)
    ]

    def send_slots(which, values):
        for c in range(2):
            for k in range(packs):
                m = c * packs + k
                picked = dot(pick_out[m * held : (m + 1) * held], values(m), NN)
                for f in range(picked.shape[0] // sends):
                    slots[which, 2 * f + c, k * sends : (k + 1) * sends] = picked[
                        f * sends : (f + 1) * sends
                    ].astype(BF)
        swaps[which].first()

    def placed_rows(which, k):
        blocks = [
            arrived[which, g, k * sends : (k + 1) * sends] for g in range(arrived.shape[1])
        ]
        return dot(
            pick_in[k * rows : (k + 1) * rows], jnp.concatenate(blocks, axis=0), TN
        ).astype(BF)

    def weights_next(chunk):
        if chunk < chunks:
            for part in range(chunk * HALVES, (chunk + 1) * HALVES):
                wg.forward(part)
                if part + HALVES < chunks * HALVES:
                    wg.start(part + HALVES)
                if part + 3 * HALVES < chunks * HALVES:
                    wg.own_first(part + 3 * HALVES)

    def weights_ready(chunk):
        for part in range(chunk * HALVES, (chunk + 1) * HALVES):
            wg.finish(part)
        save(w.at[chunk], out_w.at[chunk])

    for half in range(HALVES):
        wg.own_first(half)
    give = remote(
        from_owner, given.at[lk.c], given_sem.at[0], given_sem.at[1], lk.across
    )
    give.start()
    params = [
        Trade(
            lk, lambda t, src=src: src, lambda t, full=full: full.at[:, :, part_of(local_width, t)],
            tr_send.at[1 + i], tr_recv.at[1 + i],
        )
        for i, (src, full) in enumerate(
            ((biases, bias_full), (gain, gain_full), (offset, offset_full))
        )
    ]
    for param in params:
        param.first()
    held = tokens.shape[1]
    for m in range(tokens.shape[0]):
        pick_out[m * held : (m + 1) * held] = leaving_slots(
            to_owner[m : m + 1], held // sends, rows, sends
        )
    send_slots(0, lambda m: (tokens[m].astype(F32) + time_embed[m].astype(F32)).astype(BF))
    lse[...] = jnp.zeros_like(lse)
    first_ag = RowGather(lk, local_width, ag_send, ag_recv, by_columns=True)
    for half in range(HALVES):
        wg.start(half)
    for half in range(HALVES, 3 * HALVES):
        wg.own_first(half)
    given[lk.c] = from_owner[...]
    give.wait_recv()
    give.wait_send()
    for k in range(packs):
        m = pl.ds(lk.c * packs + k, 1)
        row = jnp.concatenate([given[c, m] for c in range(2)], axis=1)
        pick_in[k * rows : (k + 1) * rows] = coming_slots(
            row, arrived.shape[1], held, sends
        )
    for param in params:
        param.last()
    save(gain_full, out_gain)
    save(pick_out, out_pick_out)
    save(pick_in, out_pick_in)
    swaps[0].last()
    for k in range(packs):
        act[0, k, :, my_cols] = placed_rows(0, k)
        first_ag.first(act.at[0, k], k)
    for k in range(packs):
        first_ag.second(act.at[0, k], k)
    weights_next(0)
    for k in range(packs):
        first_ag.last(act.at[0, k], k)
        u[k] = act[0, k, my_rows].astype(F32)
        save(act.at[0, k], out_act.at[0, k])

    def project(layer, k):
        for j in range(3):
            cols = slice(j * heads_width, (j + 1) * heads_width)
            acc = dot(act[layer, k], w[3 * layer, :, cols], NN)
            if j != 1:
                acc = acc + biases[layer, j // 2 : j // 2 + 1]
            qkv[layer, k, :, cols] = acc.astype(BF)
        save(qkv.at[layer, k], out_qkv.at[layer, k])

    def attention(layer, k):
        same_seq = same_sequence(seg, lk.c * packs + k)
        for head in range(heads_width // HD):
            cols = [slice(j * heads_width + head * HD, j * heads_width + (head + 1) * HD) for j in range(3)]
            scores = masked_scores(qkv[layer, k, :, cols[0]], qkv[layer, k, :, cols[1]], same_seq)
            top = jnp.max(scores, axis=1, keepdims=True)
            weighted = jnp.exp2(scores - top)
            total = jnp.sum(weighted, axis=1, keepdims=True)
            lse[layer, k, :, head : head + 1] = top + jnp.log2(total)
            probs = (weighted * (1.0 / total)).astype(BF)
            att[layer, k, :, cols[0]] = dot(probs, qkv[layer, k, :, cols[2]], NN).astype(BF)
        save(lse.at[layer, k], out_lse.at[layer, k])
        save(att.at[layer, k], out_att.at[layer, k])
        for j in range(width // 256):
            cols = slice(j * 256, (j + 1) * 256)
            acc = dot(att[layer, k], w[3 * layer, cols, 3 * heads_width :], NT)
            store_part(part, k, cols, acc, mine)
        rs.first(k)

    def normalize(layer, which, k, resid):
        mean = jnp.mean(resid, axis=1, keepdims=True)
        centred = resid - mean
        scale = lax.rsqrt(jnp.mean(centred * centred, axis=1, keepdims=True) + EPS)
        normed = centred * scale
        nrm[layer, which, k] = normed
        std[layer, which, k] = jnp.broadcast_to(scale, std.shape[3:])
        save(nrm.at[layer, which, k], out_nrm.at[layer, which, k])
        save(std.at[layer, which, k], out_std.at[layer, which, k])
        return (
            normed * gain_full[layer, which : which + 1] + offset_full[layer, which : which + 1]
        )

    def norm_one(layer, k):
        hidden = normalize(layer, 0, k, u[k] + rs.last(k) + bias_full[layer, 2:3])
        h[k] = hidden
        hid[layer, k, my_rows] = hidden.astype(BF)
        ag.first(hid.at[layer, k], k)

    def expand(layer, k):
        def tile(j, carry):
            cols = pl.ds(pl.multiple_of(j * 256, 256), 256)
            acc = dot(hid[layer, k], w[3 * layer + 1, :, cols], NN) + up_bias[layer : layer + 1, cols]
            value, slope = gelu_pair(acc)
            glu[layer, k, :, cols] = value.astype(BF)
            dglu[layer, k, :, cols] = slope.astype(BF)
            return carry

        lax.fori_loop(0, width // 256, tile, 0)
        save(glu.at[layer, k], out_glu.at[layer, k])
        save(dglu.at[layer, k], out_dglu.at[layer, k])

    def contract(layer, k):
        def tile(j, carry):
            cols = pl.ds(pl.multiple_of(j * 256, 256), 256)
            acc = dot(glu[layer, k], w[3 * layer + 2, cols, :], NT)
            store_part(part, k, cols, acc, mine)
            return carry

        lax.fori_loop(0, width // 256, tile, 0)
        rs.first(k)

    def norm_two(layer, k):
        out = normalize(layer, 1, k, h[k] + rs.last(k) + bias_full[layer, 3:4])
        u[k] = out
        if layer + 1 < layers:
            act[layer + 1, k, my_rows] = out.astype(BF)
            ag.first(act.at[layer + 1, k], k)
        else:
            u_low[k] = out.astype(BF)
            save(u_low.at[k], out_u.at[k])

    trade = Trade(
        lk, lambda t: cot_part.at[:, part_of(mine, t)],
        lambda t: cot_rows.at[:, :, part_of(local_width, t)], tr_send.at[0], tr_recv.at[0],
    )
    for layer in range(layers):
        base = 3 * layer
        more = layer + 1 < layers
        weights_ready(base)
        if layer:
            ag.last(act.at[layer, 0], 0)
            save(act.at[layer, 0], out_act.at[layer, 0])
        project(layer, 0)
        if layer:
            ag.second(act.at[layer, 1], 1)
        attention(layer, 0)
        weights_next(base + 1)
        if layer:
            ag.last(act.at[layer, 1], 1)
            save(act.at[layer, 1], out_act.at[layer, 1])
        project(layer, 1)
        rs.second(0)
        attention(layer, 1)
        norm_one(layer, 0)
        rs.second(1)
        ag.second(hid.at[layer, 0], 0)
        weights_next(base + 2)
        norm_one(layer, 1)
        weights_ready(base + 1)
        ag.last(hid.at[layer, 0], 0)
        save(hid.at[layer, 0], out_hid.at[layer, 0])
        expand(layer, 0)
        ag.second(hid.at[layer, 1], 1)
        if not more:
            send_slots(1, lambda m: cot[m])
        ag.last(hid.at[layer, 1], 1)
        save(hid.at[layer, 1], out_hid.at[layer, 1])
        expand(layer, 1)
        weights_ready(base + 2)
        contract(layer, 0)
        contract(layer, 1)
        rs.second(0)
        weights_next(base + 3)
        if not more:
            swaps[1].last()
            for k in range(packs):
                cot_part[k] = placed_rows(1, k)
            trade.first()
        norm_two(layer, 0)
        rs.second(1)
        if more:
            ag.second(act.at[layer + 1, 0], 0)
        norm_two(layer, 1)
    trade.last()
    save(cot_rows, out_cot)
    for part in range(chunks * HALVES):
        wg.drain(part)
    for swap in swaps:
        swap.drain()
    for copy in pending:
        copy.wait()


def forward(
    tokens, time_embed, cot, to_owner, from_owner, seg, shard, biases, gain, offset, up_bias
):
    rows = seg.shape[1]
    packs = tokens.shape[0] // lax.axis_size("ctx")
    width = shard.shape[2]
    local_width = tokens.shape[2]
    chunks = shard.shape[0]
    layers = chunks // 3
    mine = rows // 4
    heads = biases.shape[2]
    fs, cx = lax.axis_size("fsdp"), lax.axis_size("ctx")
    groups = fs * cx
    sends = tokens.shape[1] // fs
    parts = chunks * HALVES
    shapes = dict(
        w=((chunks, width, width), BF),
        act=((layers, packs, rows, width), BF),
        qkv=((layers, packs, rows, 3 * heads), BF),
        att=((layers, packs, rows, heads), BF),
        nrm=((layers, 2, packs, mine, width), F32),
        std=((layers, 2, packs, mine, 128), F32),
        hid=((layers, packs, rows, width), BF),
        glu=((layers, packs, rows, width), BF),
        dglu=((layers, packs, rows, width), BF),
        lse=((layers, packs, rows, 128), F32),
        u=((packs, mine, width), F32),
    )
    outs = {name: jax.ShapeDtypeStruct(*shape) for name, shape in shapes.items()}
    outs["u"] = jax.ShapeDtypeStruct((packs, mine, width), BF)
    outs["cot"] = jax.ShapeDtypeStruct((packs, mine, width), BF)
    outs["gain"] = jax.ShapeDtypeStruct((layers, 2, width), F32)
    given = tokens.shape[0] * tokens.shape[1]
    outs["pick_out"] = jax.ShapeDtypeStruct((given, tokens.shape[1]), BF)
    outs["pick_in"] = jax.ShapeDtypeStruct((packs * rows, rows), BF)
    copies = chunks + layers * packs * 11 + packs + 4
    dma = pltpu.SemaphoreType.DMA
    whole = pl.BlockSpec(memory_space=pl.ANY)
    vmem = pl.BlockSpec(memory_space=pltpu.VMEM)
    return pl.pallas_call(
        forward_kernel,
        in_specs=[vmem] * 6 + [whole] + [vmem] * 4,
        out_specs=[whole] * len(outs),
        out_shape=list(outs.values()),
        scratch_shapes=[pltpu.VMEM(*shape) for shape in shapes.values()]
        + [
            pltpu.VMEM((packs, mine, width), F32),
            pltpu.VMEM((packs, 2, 2, mine, width), BF),
            pltpu.VMEM((packs, 2, mine, width), BF),
            pltpu.VMEM((packs, mine, width), BF),
            pltpu.VMEM((packs, mine, width), BF),
            pltpu.VMEM((2, groups, packs * sends, local_width), BF),
            pltpu.VMEM((2, groups, packs * sends, local_width), BF),
            pltpu.VMEM((packs, rows, local_width), BF),
            pltpu.VMEM((packs, mine, width), BF),
            pltpu.VMEM((packs, mine, width), BF),
            pltpu.VMEM((layers, 4, width), F32),
            pltpu.VMEM((layers, 2, width), F32),
            pltpu.VMEM((layers, 2, width), F32),
            pltpu.VMEM((given, tokens.shape[1]), BF),
            pltpu.VMEM((packs * rows, rows), BF),
            pltpu.VMEM((2,) + from_owner.shape, jnp.int32),
            dma((copies,)),
            dma((packs, 2)), dma((packs, 2)), dma((packs, 3)), dma((packs, 3)),
            dma((parts, fs)), dma((parts, fs)), dma((parts, fs)), dma((parts, fs)),
            dma((parts,)),
            dma((2, 2, fs)), dma((2, 2, fs)), dma((4, 3)), dma((4, 3)), dma((2,)),
        ],
        compiler_params=pltpu.CompilerParams(
            collective_id=0, has_side_effects=True, vmem_limit_bytes=60 << 20
        ),
        name="forward",
    )(
        tokens, time_embed, cot, to_owner, from_owner, seg, shard, biases, gain, offset, up_bias
    )


class GradScatter:
    def __init__(self, lk, grad, from_x, from_z, relayed, x_send, x_recv, z_send, z_recv):
        self.lk, self.grad, self.from_x, self.from_z = lk, grad, from_x, from_z
        self.relayed = relayed
        self.x_send, self.x_recv, self.z_send, self.z_recv = x_send, x_recv, z_send, z_recv
        self.rows = from_x.shape[2]

    def block(self, chunk, step, c):
        f = lax.rem(self.lk.f + step, self.lk.fs)
        first = pl.multiple_of((f * self.lk.cx + c) * self.rows, self.rows)
        return self.grad.at[chunk, pl.ds(first, self.rows)]

    def x_copy(self, chunk, step):
        return remote(
            self.block(chunk, step, 1 - self.lk.c), self.from_x.at[chunk, step],
            self.x_send.at[chunk, step], self.x_recv.at[chunk, step], self.lk.across,
        )

    def z_copy(self, chunk, step):
        slot = self.lk.fs - step
        return remote(
            self.block(chunk, step, self.lk.c), self.from_z.at[chunk, slot - 1],
            self.z_send.at[chunk, step], self.z_recv.at[chunk, slot], self.lk.away(step),
        )

    def each(self, first, work, last=None):
        def body(step, carry):
            work(step)
            return carry

        lax.fori_loop(first, self.lk.fs if last is None else last, body, 0)

    def far(self, step):
        return jnp.abs(lax.rem(self.lk.f + step, self.lk.fs) - self.lk.f) == 3

    def inner(self):
        return (self.lk.f == 1) | (self.lk.f == 2)

    def relay(self, chunk, step):
        f = self.lk.f
        return remote(
            self.block(chunk, step, self.lk.c), self.relayed.at[chunk],
            self.z_send.at[chunk, 0], self.z_recv.at[chunk, 0],
            (lax.select(f == 0, 1, 2), self.lk.c, self.lk.t),
        )

    def first(self, chunk):
        if self.lk.fs == 4:
            for step in (1, 3, 2):
                self.x_copy(chunk, step).start()
        else:
            self.each(1, lambda step: self.x_copy(chunk, step).start())
        self.x_copy(chunk, 0).start()

    def second(self, chunk, part):
        def work(step):
            self.x_copy(chunk, step).wait_recv()
            own = self.block(chunk, step, self.lk.c)
            own[...] = (own[...].astype(F32) + self.from_x[chunk, step].astype(F32)).astype(BF)
            if self.lk.fs == 4:
                pl.when(self.far(step))(self.relay(chunk, step).start)
                if step == 2:

                    @pl.when(self.inner())
                    def _():
                        self.relay(chunk, step).wait_recv()
                        own[...] = (
                            own[...].astype(F32) + self.relayed[chunk].astype(F32)
                        ).astype(BF)

                pl.when(jnp.logical_not(self.far(step)))(self.z_copy(chunk, step).start)
            else:
                self.z_copy(chunk, step).start()

        if self.lk.fs == 4:
            work((1, 3, 2)[part])
            return
        first, last = third(self.lk.fs, part)
        self.each(first, work, last)

    def last(self, chunk, out):
        self.x_copy(chunk, 0).wait_recv()
        out[...] = self.block(chunk, 0, self.lk.c)[...].astype(F32) + self.from_x[chunk, 0].astype(F32)

        def work(step):
            self.z_copy(chunk, self.lk.fs - step).wait_recv()
            out[...] = out[...] + self.from_z[chunk, step - 1].astype(F32)

        if self.lk.fs == 4:
            for step in (1, 2, 3):
                pl.when(jnp.logical_not(self.far(step)))(functools.partial(work, step))
        else:
            self.each(1, work)

    def drain(self, chunk):
        self.each(0, lambda step: self.x_copy(chunk, step).wait_send())
        if self.lk.fs == 4:
            for step in (1, 2, 3):
                pl.when(self.far(step))(self.relay(chunk, step).wait_send)
                pl.when(jnp.logical_not(self.far(step)))(self.z_copy(chunk, step).wait_send)
        else:
            self.each(1, lambda step: self.z_copy(chunk, step).wait_send())


def backward_kernel(
    up_in, u_in, pick_out, pick_in, act_in, w_in, qkv_in, att_in, nrm_in, std_in, hid_in, glu_in, dglu_in,
    lse_in, gain, seg,
    out_qkv, out_out, out_up, out_down, out_ret, out_sums,
    w, qkv, att, nrm, std, hid, glu, dglu, lse, up, gtwo, gl, gm, gup, gqkv, gatt,
    part, from_sib, to_peer, from_peer, grad, from_x, from_z, relayed, gsum, low, ret_in,
    out_vec, out_head, out_bias, vec_parts, sums,
    in_sem, out_sem, rs_send, rs_recv, ag_send, ag_recv, x_send, x_recv, z_send, z_recv,
    ex_send, ex_recv, tr_send, tr_recv, pick_sem,
):
    packs, rows, width = hid.shape
    layers = gain.shape[0]
    mine = rows // 4
    heads_width = att.shape[2]
    lk = Links()
    sources = dict(
        nrm1=lambda layer: (nrm_in.at[layer, 1], nrm.at[1]),
        std1=lambda layer: (std_in.at[layer, 1], std.at[1]),
        nrm0=lambda layer: (nrm_in.at[layer, 0], nrm.at[0]),
        std0=lambda layer: (std_in.at[layer, 0], std.at[0]),
        w2=lambda layer: (w_in.at[3 * layer + 2], w.at[2]),
        dglu=lambda layer: (dglu_in.at[layer], dglu),
        w1=lambda layer: (w_in.at[3 * layer + 1], w.at[1]),
        glu=lambda layer: (glu_in.at[layer], glu),
        hid=lambda layer: (hid_in.at[layer], hid),
        w0=lambda layer: (w_in.at[3 * layer], w.at[0]),
        qkv=lambda layer: (qkv_in.at[layer], qkv),
        lse=lambda layer: (lse_in.at[layer], lse),
        att=lambda layer: (att_in.at[layer], att),
        act=lambda layer: (act_in.at[layer], hid),
    )
    order = {name: index for index, name in enumerate(sources)}

    def fetch(name, layer):
        if layer >= 0:
            src, dst = sources[name](layer)
            pltpu.make_async_copy(src, dst, in_sem.at[order[name]]).start()

    def ready(name, layer):
        src, dst = sources[name](layer)
        pltpu.make_async_copy(src, dst, in_sem.at[order[name]]).wait()

    loads = [
        pltpu.make_async_copy(up_in, to_peer, in_sem.at[len(order)]),
        pltpu.make_async_copy(u_in, low, in_sem.at[len(order) + 1]),
    ]
    for load in loads:
        load.start()
    for name in sources:
        if name != "act":
            fetch(name, layers - 1)
    lk.barrier()
    rs = RowSum(lk, part, from_sib, to_peer, from_peer, rs_send, rs_recv)
    ag = RowGather(lk, mine, ag_send, ag_recv)
    gs = GradScatter(lk, grad, from_x, from_z, relayed, x_send, x_recv, z_send, z_recv)
    my_rows = pl.ds(pl.multiple_of(lk.t * mine, mine), mine)
    pending = []
    held = {}
    local_width = ret_in.shape[1]
    swap_rows = width // (lk.fs * lk.cx)
    sends = swap_rows // packs
    low_cols, next_cols, third_cols, last_cols = (
        slice(i * local_width, (i + 1) * local_width) for i in range(4)
    )

    class Return:
        def __init__(self, index, first, second, landed):
            self.index, self.first_buf, self.second_buf, self.landed = index, first, second, landed
            self.trade = Trade(
                lk, lambda t: low.at[:, :, part_of(local_width, t)],
                lambda t: (gm, gup)[index].at[:, part_of(mine, t), low_cols],
                tr_send.at[index], tr_recv.at[index],
            )
            self.swap = Exchange(
                lk, lambda g: first.at[part_of(swap_rows, g), low_cols],
                lambda g: landed.at[part_of(swap_rows, g)], ex_send.at[index], ex_recv.at[index],
            )
            self.picks = [
                pltpu.make_async_copy(
                    pick_in, second.at[:, : 2 * local_width], pick_sem.at[index, 0]
                ),
                pltpu.make_async_copy(pick_out, second.at[:, third_cols], pick_sem.at[index, 1]),
            ]

        def load(self):
            for copy in self.picks:
                copy.start()

        def middle(self):
            self.trade.last()
            self.picks[0].wait()
            for k in range(packs):
                pick = self.second_buf[k * rows : (k + 1) * rows, : 2 * local_width]
                values = dot(pick, (gm, gup)[self.index][k, :, low_cols], NN).astype(BF)
                for g in range(rows // sends):
                    first = g * swap_rows + k * sends
                    self.first_buf[first : first + sends, low_cols] = values[
                        g * sends : (g + 1) * sends
                    ]
            self.swap.first()

        def last(self):
            self.swap.last()
            self.picks[1].wait()
            given = pick_out.shape[1]
            for c in range(2):
                for k in range(packs):
                    m = c * packs + k
                    blocks = [
                        self.landed[
                            (2 * f + c) * swap_rows + k * sends :
                            (2 * f + c) * swap_rows + (k + 1) * sends
                        ]
                        for f in range(given // sends)
                    ]
                    pick = self.second_buf[m * given : (m + 1) * given, third_cols]
                    values = dot(pick, jnp.concatenate(blocks, axis=0), TN)
                    self.second_buf[m * given : (m + 1) * given, last_cols] = values.astype(BF)
            save(self.second_buf.at[:, last_cols], out_ret.at[self.index])
            self.saved = pending.pop()

        def finish(self):
            self.swap.drain()
            self.saved.wait()

    give_back = [
        Return(0, grad.at[0], grad.at[1], grad.at[0, :, next_cols]),
        Return(1, grad.at[3 * layers - 1], grad.at[3 * layers - 2], ret_in),
    ]
    vec_trade = Trade(
        lk, lambda t: out_vec.at[:, :, part_of(local_width, t)], lambda t: vec_parts.at[t],
        tr_send.at[2], tr_recv.at[2],
    )
    vec_swap = Exchange(
        lk, lambda g: sums.at[lk.g], lambda g: sums.at[g], ex_send.at[2], ex_recv.at[2],
        in_place=True,
    )

    def vec_middle():
        vec_trade.last()
        total = vec_parts[0]
        for t in range(1, 4):
            total = total + vec_parts[t]
        sums[lk.g, :, 0:6] = total
        sums[lk.g, :, 6:8] = out_head[...]
        for j in range(4):
            sums[lk.g, :, 8 + j : 9 + j] = out_bias[:, :, j * local_width : (j + 1) * local_width]
        vec_swap.first()

    def vec_last():
        vec_swap.last()

        def add(g, total):
            return total + sums[g]

        out_sums[...] = lax.fori_loop(1, sums.shape[0], add, sums[0])

    used = []

    def save(src, dst):
        copy = pltpu.make_async_copy(src, dst, out_sem.at[len(used)])
        copy.start()
        used.append(1)
        pending.append(copy)

    out_vec[...] = jnp.zeros_like(out_vec)
    out_head[...] = jnp.zeros_like(out_head)
    out_bias[...] = jnp.zeros_like(out_bias)

    def norm_back(layer, which, k, upstream):
        normed = nrm[which, k]
        scale = std[which, k][:, 0:1]
        out_vec[layer, 2 + which : 3 + which] += jnp.sum(upstream * normed, axis=0, keepdims=True)
        out_vec[layer, 4 + which : 5 + which] += jnp.sum(upstream, axis=0, keepdims=True)
        scaled = upstream * gain[layer, which : which + 1]
        first = jnp.mean(scaled, axis=1, keepdims=True)
        second = jnp.mean(scaled * normed, axis=1, keepdims=True)
        result = scale * (scaled - first - normed * second)
        out_vec[layer, which : which + 1] += jnp.sum(result, axis=0, keepdims=True)
        return result

    def norm_two(layer, k):
        result = norm_back(layer, 1, k, up[k])
        gtwo[k] = result
        gl[k, my_rows] = result.astype(BF)
        ag.first(gl.at[k], k)

    def norm_one(layer, k):
        result = norm_back(layer, 0, k, gtwo[k] + rs.last(k))
        up[k] = result
        gm[k, my_rows] = result.astype(BF)
        ag.first(gm.at[k], k)

    def tiles(work):
        def body(j, carry):
            work(pl.ds(pl.multiple_of(j * 256, 256), 256))
            return carry

        lax.fori_loop(0, width // 256, body, 0)

    def through_down(layer, k):
        def tile(cols):
            grad_gelu = dot(gl[k], w[2, :, cols], NN).astype(BF).astype(F32)
            result = (grad_gelu * dglu[k, :, cols].astype(F32)).astype(BF)
            gup[k, :, cols] = result
            out_bias[layer, :, cols] += jnp.sum(result.astype(F32), axis=0, keepdims=True)

        tiles(tile)

    def through_up(layer, k):
        tiles(lambda cols: store_part(part, k, cols, dot(gup[k], w[1, cols, :], NT), mine))
        rs.first(k)

    def through_out(k):
        gatt[k] = dot(gm[k], w[0, :, 3 * heads_width :], NN).astype(BF)

    def attention(layer, k):
        same_seq = same_sequence(seg, lk.c * packs + k)
        scale = 1.0 / math.sqrt(HD)
        for head in range(heads_width // HD):
            cols = [slice(j * heads_width + head * HD, j * heads_width + (head + 1) * HD) for j in range(3)]
            query, keys, values = (qkv[k, :, c] for c in cols)
            grads = gatt[k, :, cols[0]]
            probs = jnp.exp2(masked_scores(query, keys, same_seq) - lse[k, :, head : head + 1])
            grad_probs = dot(grads, values, NT)
            delta = jnp.sum(probs * grad_probs, axis=1, keepdims=True)
            grad_scores = (probs * (grad_probs - delta)).astype(BF)
            gqkv[k, :, cols[0]] = (dot(grad_scores, keys, NN) * scale).astype(BF)
            gqkv[k, :, cols[1]] = (dot(grad_scores, query, TN) * scale).astype(BF)
            gqkv[k, :, cols[2]] = dot(probs.astype(BF), grads, TN).astype(BF)
        for j in range(2):
            cols = slice(2 * j * heads_width, (2 * j + 1) * heads_width)
            out_head[layer, j : j + 1] += jnp.sum(
                gqkv[k, :, cols].astype(F32), axis=0, keepdims=True
            )

    def through_qkv(k):
        tiles(
            lambda cols: store_part(
                part, k, cols, dot(gqkv[k], w[0, cols, : 3 * heads_width], NT), mine
            )
        )
        rs.first(k)

    def product(left, right, cols, right_cols=slice(None)):
        total = dot(left[0, :, cols], right[0, :, right_cols], TN)
        for k in range(1, packs):
            total = total + dot(left[k, :, cols], right[k, :, right_cols], TN)
        return total.astype(BF)

    def down_grad(layer):
        def tile(cols):
            grad[3 * layer + 2, cols, :] = product(gl, glu, cols)

        tiles(tile)
        gs.first(3 * layer + 2)

    def up_grad(layer):
        def tile(cols):
            grad[3 * layer + 1, cols, :] = product(hid, gup, cols)

        tiles(tile)
        gs.first(3 * layer + 1)

    def first_grad(layer):
        def tile(cols):
            grad[3 * layer, cols, : 3 * heads_width] = product(hid, gqkv, cols)
            grad[3 * layer, cols, 3 * heads_width :] = product(gm, att, cols)

        tiles(tile)
        gs.first(3 * layer)

    def emit(layer, which):
        chunk = 3 * layer + which
        out = gsum.at[0]
        while held.get(0):
            held[0].pop().wait()
        gs.last(chunk, out)
        held[0] = []
        saved = len(pending)
        if which == 2:
            save(out, out_down.at[layer])
        elif which == 1:
            save(out, out_up.at[layer])
        else:
            for c in range(3):
                save(out.at[:, c * heads_width : (c + 1) * heads_width], out_qkv.at[layer, c])
            save(out.at[:, 3 * heads_width :], out_out.at[layer])
        held[0] = [pending.pop() for _ in range(len(pending) - saved)]

    give_back[0].load()
    for load in loads:
        load.wait()
    top = layers - 1
    ready("nrm1", top)
    ready("std1", top)
    for k in range(packs):
        up[k] = to_peer[k].astype(F32)
        norm_two(top, k)
    give_back[0].trade.first()
    fetch("nrm1", top - 1)
    fetch("std1", top - 1)
    def summed(chunk, *parts):
        for part in parts:
            gs.second(chunk, part)

    for layer in reversed(range(layers)):
        base = 3 * layer
        later = layer < top
        ag.second(gl.at[0], 0)
        ready("w2", layer)
        ready("dglu", layer)
        ag.last(gl.at[0], 0)
        through_down(layer, 0)
        ag.second(gl.at[1], 1)
        if layer == top:
            give_back[0].middle()
        ready("w1", layer)
        through_up(layer, 0)
        if later:
            summed(base + 3, 0)
        ag.last(gl.at[1], 1)
        through_down(layer, 1)
        fetch("w2", layer - 1)
        fetch("dglu", layer - 1)
        rs.second(0)
        through_up(layer, 1)
        fetch("w1", layer - 1)
        ready("glu", layer)
        down_grad(layer)
        fetch("glu", layer - 1)
        rs.second(1)
        ready("nrm0", layer)
        ready("std0", layer)
        norm_one(layer, 0)
        if later:
            summed(base + 3, 1)
        ready("hid", layer)
        up_grad(layer)
        fetch("act", layer)
        ag.second(gm.at[0], 0)
        if later:
            summed(base + 3, 2)
        else:
            summed(base + 2, 0)
        norm_one(layer, 1)
        fetch("nrm0", layer - 1)
        fetch("std0", layer - 1)
        ready("w0", layer)
        ready("qkv", layer)
        ready("lse", layer)
        ag.last(gm.at[0], 0)
        through_out(0)
        if later:
            summed(base + 2, 0)
        else:
            summed(base + 2, 1)
        ag.second(gm.at[1], 1)
        attention(layer, 0)
        through_qkv(0)
        ag.last(gm.at[1], 1)
        through_out(1)
        rs.second(0)
        if later:
            summed(base + 2, 1)
        else:
            summed(base + 2, 2)
            summed(base + 1, 0)
        attention(layer, 1)
        fetch("qkv", layer - 1)
        fetch("lse", layer - 1)
        through_qkv(1)
        fetch("w0", layer - 1)
        rs.second(1)
        ready("att", layer)
        ready("act", layer)
        first_grad(layer)
        if later:
            summed(base + 2, 2)
        else:
            summed(base + 1, 1)
        if layer:
            fetch("att", layer - 1)
            fetch("hid", layer - 1)
        for k in range(packs):
            up[k] = rs.last(k) + up[k]
            if layer:
                if k == 0:
                    ready("nrm1", layer - 1)
                    ready("std1", layer - 1)
                norm_two(layer - 1, k)
            else:
                low[k] = up[k].astype(BF)
        if layer == top:
            summed(base + 1, 2)
            give_back[0].last()
            give_back[0].finish()
        if layer:
            fetch("nrm1", layer - 2)
            fetch("std1", layer - 2)
    give_back[1].trade.first()
    vec_trade.first()
    summed(1, 0)
    emit(1, 2)
    emit(1, 1)
    for chunk in (3 * layers - 1, 3 * layers - 2):
        gs.drain(chunk)
    give_back[1].load()
    give_back[1].middle()
    vec_middle()
    summed(1, 1, 2)
    emit(1, 0)
    summed(0, 0, 1, 2)
    give_back[1].last()
    vec_last()
    emit(0, 2)
    emit(0, 1)
    emit(0, 0)
    for chunk in range(3 * layers - 2):
        gs.drain(chunk)
    give_back[1].finish()
    vec_swap.drain()
    for copy in pending + sum(held.values(), []):
        copy.wait()


def backward(upstream, u, pick_out, pick_in, saved, gain, seg):
    full_w, o_act, o_qkv, o_att, o_nrm, o_std, o_hid, o_glu, o_dglu, o_lse = saved
    layers, packs, rows, width = o_act.shape
    mine = rows // 4
    chunks = 3 * layers
    heads = o_att.shape[3]
    local_width = width // 4
    fs, cx = lax.axis_size("fsdp"), lax.axis_size("ctx")
    groups = fs * cx
    shard = width // groups
    given = pick_out.shape[0]
    outs = [
        jax.ShapeDtypeStruct((layers, 3, shard, heads), F32),
        jax.ShapeDtypeStruct((layers, shard, heads), F32),
        jax.ShapeDtypeStruct((layers, shard, width), F32),
        jax.ShapeDtypeStruct((layers, shard, width), F32),
        jax.ShapeDtypeStruct((2, given, local_width), BF),
        jax.ShapeDtypeStruct((layers, 12, local_width), F32),
    ]
    dma = pltpu.SemaphoreType.DMA
    whole = pl.BlockSpec(memory_space=pl.ANY)
    vmem = pl.BlockSpec(memory_space=pltpu.VMEM)
    full = pltpu.VMEM((packs, rows, width), BF)
    rowed = pltpu.VMEM((packs, mine, width), F32)
    return pl.pallas_call(
        backward_kernel,
        in_specs=[whole] * 14 + [vmem] * 2,
        out_specs=[whole] * 5 + [vmem],
        out_shape=outs,
        scratch_shapes=[
            pltpu.VMEM((3, width, width), BF),
            pltpu.VMEM((packs, rows, 3 * heads), BF),
            pltpu.VMEM((packs, rows, heads), BF),
            pltpu.VMEM((2, packs, mine, width), F32),
            pltpu.VMEM((2, packs, mine, 128), F32),
            full, full, full,
            pltpu.VMEM((packs, rows, 128), F32),
            rowed, rowed,
            full, full, full,
            pltpu.VMEM((packs, rows, 3 * heads), BF),
            pltpu.VMEM((packs, rows, heads), BF),
            pltpu.VMEM((packs, 2, 2, mine, width), BF),
            pltpu.VMEM((packs, 2, mine, width), BF),
            pltpu.VMEM((packs, mine, width), BF),
            pltpu.VMEM((packs, mine, width), BF),
            pltpu.VMEM((chunks, width, width), BF),
            pltpu.VMEM((chunks, fs, shard, width), BF),
            pltpu.VMEM((chunks, fs - 1, shard, width), BF),
            pltpu.VMEM((chunks if fs == 4 else 1, shard, width), BF),
            pltpu.VMEM((1, shard, width), F32),
            pltpu.VMEM((packs, mine, width), BF),
            pltpu.VMEM((given, local_width), BF),
            pltpu.VMEM((layers, 6, width), F32),
            pltpu.VMEM((layers, 2, heads), F32),
            pltpu.VMEM((layers, 1, width), F32),
            pltpu.VMEM((4, layers, 6, local_width), F32),
            pltpu.VMEM((groups, layers, 12, local_width), F32),
            dma((16,)), dma((packs + 6 * layers + 2,)),
            dma((packs, 2)), dma((packs, 2)), dma((packs, 3)), dma((packs, 3)),
            dma((chunks, fs)), dma((chunks, fs)), dma((chunks, fs)), dma((chunks, fs)),
            dma((3, 2, fs)), dma((3, 2, fs)), dma((3, 3)), dma((3, 3)), dma((2, 2)),
        ],
        compiler_params=pltpu.CompilerParams(
            collective_id=1, has_side_effects=True, vmem_limit_bytes=62 << 20
        ),
        name="backward",
    )(
        upstream, u, pick_out, pick_in, o_act, full_w, o_qkv, o_att, o_nrm, o_std, o_hid,
        o_glu, o_dglu, o_lse, gain, seg,
    )


def local(
    tokens, time_embed, cotangent, segment_ids, to_owner, from_owner,
    w_qkv, w_out, w_up, w_down, biases, norm_gain, norm_bias, up_bias,
):
    micro, rows, width = tokens.shape
    layers = w_qkv.shape[0]
    shard = jnp.concatenate(
        [w_qkv[:, 0], w_qkv[:, 1], w_qkv[:, 2], w_out, w_up, w_down], axis=2
    )
    shard = shard.reshape(layers, shard.shape[1], 3, -1).transpose(0, 2, 1, 3)
    shard = shard.reshape(layers * 3, shard.shape[2], -1)
    *saved, u, upstream, gain, pick_out, pick_in = forward(
        tokens, time_embed, cotangent, to_owner, from_owner, segment_ids, shard, biases,
        norm_gain, norm_bias, up_bias,
    )
    g_qkv, g_out, g_up, g_down, returned, sums = backward(
        upstream, u, pick_out, pick_in, saved, gain, segment_ids
    )
    returned = returned.reshape(2, micro, rows, width).astype(F32)
    return (
        returned[0],
        returned[1],
        g_qkv, g_out, g_up, g_down,
        jnp.concatenate([sums[:, 6:8], sums[:, 0:2]], axis=1),
        sums[:, 2:4],
        sums[:, 4:6],
        sums[:, 8:12].reshape(layers, -1),
    )


def solution(mesh):
    wide = P(None, GRP, "tp")
    vec = P(None, None, "tp")
    qkv = P(None, None, GRP, "tp")
    owner = P(None, GRP)
    return jax.shard_map(
        local,
        mesh=mesh,
        in_specs=(
            wide, wide, wide, P(None, "fsdp"), owner, owner, qkv, wide, wide, wide,
            vec, vec, vec, P(None, "tp"),
        ),
        out_specs=(wide, wide, qkv, wide, wide, wide, vec, vec, vec, P(None, "tp")),
        check_vma=False,
    )
```
